128 devices in a mesh: row: 16 (over x, y), col: 8 (over z, core).
Axes of the slice: x: 4, y: 4, z: 4, core: 2. Of those that a mesh axis runs over, the one named last changes fastest.
Arguments:
- subgrid_pixels: float32 [16384, 2, 2, 1024], P(('row', 'col')), may hold values from -6 to 6
- tile_offsets: int32 [16384, 2], P(('row', 'col')), may hold values from 0 to 255, as said below
- station_pairs: int32 [16384, 2], P(('row', 'col')), may hold values from 0 to 511
- time_blocks: int32 [16384], P(('row', 'col')), may hold values from 0 to 1
- channel_blocks: int32 [16384], P(('row', 'col')), may hold values from 0 to 7
- valid_counts: int32 [128], P(('row', 'col')), may hold values from 64 to 128, as said below
- aterms: bfloat16 [512, 2, 2, 2, 1024], replicated, may hold values from -4 to 4
- channel_weights: float32 [8], replicated, may hold values from 0.5 to 2
Outputs:
- image: float32 [2, 8192, 8192], P(None, ('row', 'col'))
The draws below stay inside these ranges and needn't reach their ends.
Inputs may be any that keep to these rules, and one draw needn't show every extreme that they name: `tile_offsets`: within the valid entries of one device's list, at most 2 subgrids lie in the grid block of any one device (rows 512 r to 512 (r + 1) - 1, columns 1024 c to 1024 (c + 1) - 1 of device index r * 8 + c), and some device's block receives exactly 2 valid subgrids from every device. `valid_counts`: entry d counts the valid subgrids of device d, which are the first slots of its list; some device's list is full.
All inputs are finite; a program needn't handle non-finite values.
Results may differ from the reference program's by a relative error of at most 0.0003.
Values sent between devices are 32-bit elements; how exact they have to be, the bound alone decides.
A program may use at most 192 MiB of HBM per device.

```python
import math
import jax
import jax.numpy as jnp
from jax import lax

G = 8192
SUB = 32
STATIONS = 512
TIME_BLOCKS = 2
CHAN_BLOCKS = 8
SG_DEV = 128
ROWS_DEV = 512
COLS_DEV = 1024
CAP = 2
SUBGRIDS = 16384
N_ROW = 16
N_COL = 8
DEVICES = 128


def draw_tile_offsets(key, part):
    key = jax.random.fold_in(key, 31)
    hot_key, device_keys, place_key = jax.random.split(key, 3)
    owners = jnp.arange(DEVICES, dtype=jnp.int32)
    owner_row = owners // N_COL
    owner_col = owners % N_COL
    row_offset = (2 * owner_row - (N_ROW - 1)) * (ROWS_DEV // SUB)
    column_offset = (2 * owner_col - (N_COL - 1)) * (COLS_DEV // SUB)
    distance = row_offset * row_offset + column_offset * column_offset
    hot_ranking = (distance * 16 + jax.random.randint(hot_key, (DEVICES,), 0, 16)) * DEVICES + owners
    hottest = jnp.argsort(hot_ranking)[0].astype(jnp.int32)

    def device_plan(device_key):
        first_key, second_key = jax.random.split(device_key)
        jitter = jax.random.randint(first_key, (DEVICES,), 0, jnp.max(distance) + 1)
        ranking = (distance + jitter) * DEVICES + owners
        ranking = jnp.where(owners == hottest, 2 ** 30, ranking)
        ordering = jnp.argsort(ranking).astype(jnp.int32)
        remainder = ordering[jnp.arange(SG_DEV - CAP, dtype=jnp.int32) // CAP]
        remainder = jax.random.permutation(second_key, remainder)
        return jnp.concatenate([jnp.full((CAP,), hottest, jnp.int32), remainder])
    owner_of = jax.vmap(device_plan)(jax.random.split(device_keys, DEVICES))
    row_key, column_key = jax.random.split(place_key)
    row_within = jax.random.randint(row_key, (DEVICES, SG_DEV), 0, ROWS_DEV // SUB)
    column_within = jax.random.randint(column_key, (DEVICES, SG_DEV), 0, COLS_DEV // SUB)
    tile_row = owner_of // N_COL * (ROWS_DEV // SUB) + row_within
    tile_column = owner_of % N_COL * (COLS_DEV // SUB) + column_within
    return jnp.stack([tile_row, tile_column], axis=-1).reshape(DEVICES * SG_DEV, 2).astype(jnp.int32)


def draw_valid_counts(key, part):
    key = jax.random.fold_in(key, 37)
    first_key, second_key = jax.random.split(key)
    counted = jax.random.randint(first_key, (DEVICES,), SG_DEV // 2, SG_DEV + 1)
    full_device = jax.random.randint(second_key, (), 0, DEVICES)
    return jnp.where(jnp.arange(DEVICES) == full_device, SG_DEV, counted).astype(jnp.int32)


def place_ends(entries, stream_key, smallest, top_value):
    longest = entries.shape.index(max(entries.shape))
    spots = []
    for shift in (0, 1):
        where = [jax.random.randint(jax.random.fold_in(stream_key, axis), (), 0, length) for axis, length in enumerate(entries.shape)]
        where[longest] = (where[longest] + shift) % entries.shape[longest]
        spots.append(tuple(where))
    return entries.at[spots[0]].set(smallest).at[spots[1]].set(top_value)


def shard_levels(own_key, shape, pieces, low, largest):
    level = 1.0
    for dim, shards_of in pieces:
        draws = jax.random.uniform(jax.random.fold_in(jax.random.fold_in(own_key, 6), dim), (shards_of,), jnp.float32, low / len(pieces), largest / len(pieces))
        level = level * jnp.repeat(jnp.exp(draws), shape[dim] // shards_of).reshape((-1,) + (1,) * (len(shape) - 1 - dim))
    return level


def centred(rng, shape, spread, bound, pieces=(), kind=jnp.bfloat16):
    entries = jax.random.normal(rng, shape, jnp.float32) * spread
    if len(pieces) > 0:
        entries = shard_levels(rng, shape, pieces, -0.22, 0.18) * entries
    return jnp.clip(entries, min=-bound, max=bound).astype(kind)


def setup_inputs(seed: int = 0) -> dict:
    keys = jax.random.split(jax.random.key(seed), 9)
    subgrid_pixels = centred(keys[0], (SUBGRIDS, 2, 2, SUB * SUB), 1.0, 6.0, ((0, 128),), jnp.float32)
    tile_offsets = draw_tile_offsets(jax.random.fold_in(keys[8], 71), 0)
    station_pairs = place_ends(jax.random.randint(keys[2], (SUBGRIDS, 2), 0, STATIONS), jax.random.fold_in(keys[2], 1), 0, STATIONS - 1).astype(jnp.int32)
    time_blocks = place_ends(jax.random.randint(keys[3], (SUBGRIDS,), 0, TIME_BLOCKS), jax.random.fold_in(keys[3], 1), 0, TIME_BLOCKS - 1).astype(jnp.int32)
    channel_blocks = place_ends(jax.random.randint(keys[4], (SUBGRIDS,), 0, CHAN_BLOCKS), jax.random.fold_in(keys[4], 1), 0, CHAN_BLOCKS - 1).astype(jnp.int32)
    valid_counts = draw_valid_counts(jax.random.fold_in(keys[8], 71), 0)
    aterms = centred(keys[6], (STATIONS, TIME_BLOCKS, 2, 2, SUB * SUB), 0.7, 4.0)
    channel_weights = jnp.clip(jnp.exp(jax.random.uniform(keys[7], (CHAN_BLOCKS,), jnp.float32, math.log(0.5), math.log(2.0))), 0.5, 2.0)
    return {"subgrid_pixels": subgrid_pixels, "tile_offsets": tile_offsets, "station_pairs": station_pairs, "time_blocks": time_blocks, "channel_blocks": channel_blocks, "valid_counts": valid_counts, "aterms": aterms, "channel_weights": channel_weights}


def reference(subgrid_pixels, tile_offsets, station_pairs, time_blocks, channel_blocks, valid_counts, aterms, channel_weights):
    subgrid_total = subgrid_pixels.shape[0]
    slot_index = jnp.arange(subgrid_total, dtype=jnp.int32)
    is_valid = slot_index % SG_DEV < valid_counts[slot_index // SG_DEV]
    beam_first = aterms[station_pairs[:, 0], time_blocks].astype(jnp.float32)
    beam_second = aterms[station_pairs[:, 1], time_blocks].astype(jnp.float32)
    gain_real = beam_first[:, 0] * beam_second[:, 0] + beam_first[:, 1] * beam_second[:, 1]
    gain_imag = beam_first[:, 1] * beam_second[:, 0] - beam_first[:, 0] * beam_second[:, 1]
    weight = (channel_weights[channel_blocks] * is_valid.astype(jnp.float32))[:, None, None]
    pixel_real = subgrid_pixels[:, 0]
    pixel_imag = subgrid_pixels[:, 1]
    fixed_real = (pixel_real * gain_real - pixel_imag * gain_imag) * weight
    fixed_imag = (pixel_real * gain_imag + pixel_imag * gain_real) * weight
    image_field = lax.complex(fixed_real, fixed_imag).reshape(subgrid_total, 2, SUB, SUB)
    spectrum = jnp.fft.fft2(image_field, axes=(2, 3)).reshape(subgrid_total, 2, SUB * SUB) / SUB
    tile_count = G // SUB
    tile_index = tile_offsets[:, 0] * tile_count + tile_offsets[:, 1]
    image_scale = 1.0 / (SUB * math.sqrt(SUBGRIDS))
    images = []
    for feed_index in range(2):
        planes = []
        for component in (jnp.real(spectrum[:, feed_index]), jnp.imag(spectrum[:, feed_index])):
            summed = jax.ops.segment_sum(component, tile_index, num_segments=tile_count * tile_count)
            planes.append(summed.reshape(tile_count, tile_count, SUB, SUB).transpose(0, 2, 1, 3).reshape(G, G))
        transformed = jnp.fft.fft2(lax.complex(planes[0], planes[1]))
        images.append(jnp.real(transformed).T * image_scale)
    return jnp.stack(images).astype(jnp.float32)
```

```python
import functools
import math

import jax
import jax.numpy as jnp
import ml_dtypes
import numpy as np
from jax import lax
from jax.experimental import pallas as pl
from jax.experimental.pallas import tpu as pltpu
from jax.sharding import PartitionSpec as P

BF = jnp.bfloat16
F32 = jnp.float32
I32 = jnp.int32

PAIR_J = (0, 8, 4, 12, 1, 9, 17, 25, 2, 10, 18, 26, 3, 11, 19, 27)
STEP_A = (0, 4, 1, 1, 2, 2, 3, 3)
STEP_B = (0, 4, 7, 7, 6, 6, 5, 5)
MSG = 72
VMEM = 56 * 1024 * 1024


def partner(j):
    return 16 if j == 0 else 32 - j


def unit(turns):
    return np.exp(-2j * np.pi * turns)


def split_np(x):
    hi = np.asarray(x, np.float32).astype(ml_dtypes.bfloat16)
    lo = (np.asarray(x, np.float64) - hi.astype(np.float64)).astype(ml_dtypes.bfloat16)
    return hi, lo


def split(x):
    hi = x.astype(BF)
    return hi, (x - hi.astype(F32)).astype(BF)


def dot(a, b):
    return lax.dot_general(a, b, (((1,), (0,)), ((), ())), preferred_element_type=F32)


def dot_nt(a, b):
    return lax.dot_general(a, b, (((1,), (1,)), ((), ())), preferred_element_type=F32)


@functools.lru_cache(None)
def tables():
    xi = np.arange(4)[:, None, None]
    y = np.arange(32)[None, :, None]
    v = np.arange(32)[None, None, :]
    b = np.zeros((8, 2, 2, 4, 32, 2, 2, 2, 32))
    for step in range(8):
        for pair in range(2):
            j = PAIR_J[2 * step + pair]
            for half, jj in enumerate((j, partner(j))):
                w = unit((xi * jj + y * v) % 32 / 32) / 32
                b[step, half, 0, :, :, pair, half, 0] = w.real
                b[step, half, 0, :, :, pair, half, 1] = w.imag
                b[step, half, 1, :, :, pair, half, 0] = -w.imag
                b[step, half, 1, :, :, pair, half, 1] = w.real
    b = b.reshape(8, 2, 256, 256)
    i = np.arange(256)
    w = unit(i[:, None] * i[None, :] % 256 / 256)
    wc = np.stack([w.real.reshape(4, 64, 256), w.imag.reshape(4, 64, 256)], 1).reshape(512, 256)
    tw = unit(i[:, None] * (np.arange(128) % 32)[None, :] / 8192)
    d = unit(np.arange(32)[:, None] * np.arange(32)[None, :] % 32 / 32)
    coef = np.stack([np.stack([d, 1j * d]), np.stack([1j * d, -d])])
    f = np.zeros((2, 3, 2, 2, 32, 2, 2, 2, 32))

    def put(kind, which, half, pm, conj):
        for pq in range(2):
            for reim in range(2):
                c = coef[pq, reim]
                f[kind, which, pm, 0, :, pq, half, reim, :] = c.real
                f[kind, which, pm, 1, :, pq, half, reim, :] = -c.imag if conj else c.imag

    put(0, 0, 0, 0, False)
    put(0, 0, 1, 1, True)
    put(0, 1, 1, 0, True)
    put(0, 1, 0, 1, False)
    put(1, 0, 0, 0, False)
    put(1, 0, 1, 1, False)
    put(1, 1, 1, 1, True)
    put(1, 2, 0, 0, True)
    f = f.reshape(2, 3, 128, 256)
    fh, fl = split_np(f)
    f = np.concatenate([fh, fl], axis=2)
    k = np.arange(256)
    q, rp, t, pm = k // 64, k // 32 % 2, k // 2 % 16, k % 2
    r = 16 * (2 * q + rp) + t
    rr = np.where(pm == 0, r, 255 - r)
    l0 = np.arange(256)
    w = unit(rr[:, None] * l0[None, :] % 256 / 256) / 4096
    wr = np.concatenate([w.real, w.imag], axis=1)
    w0 = np.where((pm == 0)[:, None], unit(r[:, None] * l0[None, :] % 256 / 256), 0) / 4096
    w16 = np.where((pm == 1)[:, None], unit((32 * r[:, None] + 16) * l0[None, :] % 8192 / 8192), 0) / 4096
    ws = np.stack([np.concatenate([w0.real, w16.real], 1), np.concatenate([-w0.imag, -w16.imag], 1)])
    kx = np.arange(32)
    qx, row = kx // 8, kx % 8
    rx = 16 * (15 - (2 * qx + row))
    wx = np.where((row < 2)[:, None], unit(-(rx[:, None] * l0[None, :] % 256) / 256), 0) / 4096
    zero = np.zeros_like(wx.real)
    wx = np.stack([np.concatenate([wx.real, zero], 1), np.concatenate([-wx.imag, zero], 1)])
    tj = unit(np.array(PAIR_J)[:, None] * l0[None, :] / 8192)
    tj = np.stack([tj.real, tj.imag], 1).astype(np.float32)
    return dict(
        b=split_np(b), wc=split_np(wc), tw=(tw.real.astype(np.float32), tw.imag.astype(np.float32)),
        f=f, wr=split_np(wr), ws=split_np(ws), wx=split_np(wx), tj=tj,
    )


def slot_kernel(pk, vc, table, target, count):
    def clear(i, _):
        count[i] = 0
        table[2 * i] = -1
        table[2 * i + 1] = -1
        return 0

    lax.fori_loop(0, 128, clear, 0)

    def place(s, _):
        row = pk[s]
        col = pk[128 + s]
        block_row = row // 16
        low = block_row < 8
        near = jnp.where(low, block_row, 15 - block_row)
        place_row = near // 2 * 4 + near % 2 + jnp.where(low, 0, 2)
        block = place_row * 8 + col // 32
        rank = count[block]
        valid = s < vc[0]
        slot = block * 2 + jnp.minimum(rank, 1)
        target[s] = jnp.where(valid, slot, -1)

        @pl.when(valid)
        def _():
            count[block] = rank + 1
            table[slot] = row % 16 * 32 + col % 32

        return 0

    lax.fori_loop(0, 128, place, 0)


def slots(packed, count):
    smem = pl.BlockSpec(memory_space=pltpu.SMEM)
    return pl.pallas_call(
        slot_kernel,
        out_shape=(jax.ShapeDtypeStruct((256,), I32), jax.ShapeDtypeStruct((128,), I32)),
        in_specs=[smem, smem],
        out_specs=(smem, smem),
        scratch_shapes=[pltpu.SMEM((128,), I32)],
        name="slots",
    )(packed, count)


def dft8(re, im):
    h = math.sqrt(0.5)

    def four(a, b):
        s0r, s0i = a[0] + a[2], b[0] + b[2]
        s1r, s1i = a[0] - a[2], b[0] - b[2]
        s2r, s2i = a[1] + a[3], b[1] + b[3]
        s3r, s3i = a[1] - a[3], b[1] - b[3]
        return (
            [s0r + s2r, s1r + s3i, s0r - s2r, s1r - s3i],
            [s0i + s2i, s1i - s3r, s0i - s2i, s1i + s3r],
        )

    er, ei = four(re[0::2], im[0::2])
    orr, oi = four(re[1::2], im[1::2])
    tr = [orr[0], (orr[1] + oi[1]) * h, oi[2], (oi[3] - orr[3]) * h]
    ti = [oi[0], (oi[1] - orr[1]) * h, -orr[2], -(oi[3] + orr[3]) * h]
    return (
        [er[k] + tr[k] for k in range(4)] + [er[k] - tr[k] for k in range(4)],
        [ei[k] + ti[k] for k in range(4)] + [ei[k] - ti[k] for k in range(4)],
    )


def source_kernel(
    pk, vc, cw, ja, jb, tgt, px, beams, bh, bl, out, got, corr, lhi, llo, perm, sems
):
    step = pl.program_id(0)

    @pl.when(step == 0)
    def _():
        for group in range(8):
            def fetch(i, _, group=group):
                s = group * 16 + i
                for e in range(2):
                    pltpu.make_async_copy(
                        beams.at[pk[256 + 128 * e + s]], got.at[s, e], sems.at[group]
                    ).start()
                return 0

            lax.fori_loop(0, 16, fetch, 0)
        slot = lax.broadcasted_iota(I32, (256, 128), 0)
        hit = jnp.where(slot == tgt[...], 1.0, 0.0).astype(BF)
        perm[:, :128] = hit
        perm[:, 128:] = hit
        for group in range(8):
            part = got.at[pl.ds(group * 16, 16)]
            pltpu.make_async_copy(part, part, sems.at[group]).wait()

            def correct(i, _, group=group):
                s = group * 16 + i
                weight = jnp.where(s < vc[0], cw[pk[512 + s]], 0.0)
                ar, ai = got[s, 0, 0].astype(F32), got[s, 0, 1].astype(F32)
                br, bi = got[s, 1, 0].astype(F32), got[s, 1, 1].astype(F32)
                gr = (ar * br + ai * bi) * weight
                gi = (ai * br - ar * bi) * weight
                pr, pi = px[s, 0], px[s, 1]
                at = pl.multiple_of(s * 32, 32)
                corr[pl.ds(at, 16), :] = pr * gr - pi * gi
                corr[pl.ds(at + 16, 16), :] = pr * gi + pi * gr
                return 0

            lax.fori_loop(0, 16, correct, 0, unroll=2)

            for f in range(2):
                base = group * 16 * 32 + f
                re = [corr[pl.ds(base + 2 * p, 16, stride=32), :] for p in range(8)]
                im = [corr[pl.ds(base + 16 + 2 * p, 16, stride=32), :] for p in range(8)]
                re, im = dft8(re, im)
                rows = slice(f * 128 + group * 16, f * 128 + group * 16 + 16)
                for k in range(8):
                    lhi[k, rows, :128], llo[k, rows, :128] = split(re[k])
                    lhi[k, rows, 128:], llo[k, rows, 128:] = split(im[k])

    acc = jnp.zeros((256, 256), F32)
    for half, pick in enumerate((ja, jb)):
        k = pick[step]
        acc = acc + dot(lhi[k], bh[0, half]) + dot(llo[k], bh[0, half]) + dot(lhi[k], bl[0, half])
    hi, lo = split(acc)
    for f in range(2):
        rows = slice(f * 128, f * 128 + 128)
        padded = dot(perm[...], jnp.concatenate([hi[rows], lo[rows]], axis=0))
        for pair in range(2):
            for q in range(4):
                out[(pair * 2 + f) * 4 + q] = padded[q * 64:(q + 1) * 64, pair * 128:(pair + 1) * 128]


def source(packed, count, weights, target, pixels, beams):
    t = tables()
    smem = pl.BlockSpec(memory_space=pltpu.SMEM)
    whole = pl.BlockSpec(memory_space=pltpu.VMEM)
    return pl.pallas_call(
        source_kernel,
        grid=(8,),
        out_shape=jax.ShapeDtypeStruct((128, 64, 128), F32),
        in_specs=[smem, smem, smem, smem, smem, whole, whole, pl.BlockSpec(memory_space=pl.ANY)]
        + [pl.BlockSpec((1, 2, 256, 256), lambda i: (i, 0, 0, 0))] * 2,
        out_specs=pl.BlockSpec((16, 64, 128), lambda i: (i, 0, 0)),
        scratch_shapes=[
            pltpu.VMEM((128, 2, 2, 16, 128), BF),
            pltpu.VMEM((128 * 32, 128), F32),
            pltpu.VMEM((8, 256, 256), BF),
            pltpu.VMEM((8, 256, 256), BF),
            pltpu.VMEM((256, 256), BF),
            pltpu.SemaphoreType.DMA((8,)),
        ],
        compiler_params=pltpu.CompilerParams(vmem_limit_bytes=VMEM),
        name="source",
    )(
        packed, count, weights, np.array(STEP_A, np.int32), np.array(STEP_B, np.int32), target,
        pixels, beams, t["b"][0], t["b"][1],
    )


def middle_kernel(
    dev, recv, tab, wh, wl, twr, twi, fmat, out, tabt, ghl, pqh, pql, zc
):
    kind = dev[0]
    quarter = dev[1]
    tabt[...] = tab[...].T
    for d in range(128):
        out[d * MSG + 64:d * MSG + 72, :] = jnp.zeros((8, 128), F32)
    lane = lax.broadcasted_iota(I32, (32, 128), 1)
    low = lane < 64

    def columns(pm, t):
        g = ghl[pm, pl.ds(pl.multiple_of(t * 256, 256), 256), :]
        for c in range(4):
            rows = slice(c * 128, c * 128 + 128)
            a = dot(wh[rows, :], g)
            b = dot(wl[rows, :], g[:, :128])
            u = a[:, :128] + a[:, 128:] + b
            ur, ui = u[:64], u[64:]
            m0 = slice(c * 64, c * 64 + 64)
            tr, ti = twr[m0, :], twi[m0, :]
            pqh[pm, m0, :128], pql[pm, m0, :128] = split(tr * ur - ti * ui)
            pqh[pm, m0, 128:], pql[pm, m0, 128:] = split(tr * ui + ti * ur)

    def mix(which, pm):
        both = fmat[kind, which]
        z = dot_nt(both, pqh[pm])
        return z[:128] + z[128:] + dot_nt(both[:128], pql[pm])

    def emit(z, row, pms):
        for pm in pms:
            for tile in range(2):
                lanes = slice(tile * 128, tile * 128 + 128)
                re, im = z[pm * 64:pm * 64 + 32, lanes], z[pm * 64 + 32:pm * 64 + 64, lanes]
                even = jnp.where(low, re, pltpu.roll(im, 64, 1))
                odd = jnp.where(low, pltpu.roll(re, 64, 1), im)
                out[pl.ds(2 * tile * MSG + row + pm, 32, stride=4 * MSG), :] = even
                out[pl.ds((2 * tile + 1) * MSG + row + pm, 32, stride=4 * MSG), :] = odd

    for rp in range(2):
        for pm in range(2):
            def block(c, _, pm=pm, rp=rp):
                first = (pm * 2 + rp) * 16 + 2 * c
                key = jnp.concatenate(
                    [tabt[pl.ds(quarter * 64 + first + k, 1), :] for k in range(2)], axis=1
                )
                parts = [split(recv[pl.ds(first + k, 128, stride=64), :]) for k in range(2)]
                rhs = jnp.concatenate(
                    [
                        jnp.concatenate([parts[0][0], parts[0][1]], axis=1),
                        jnp.concatenate([parts[1][0], parts[1][1]], axis=1),
                    ],
                    axis=0,
                )
                for chunk in range(4):
                    tile = lax.broadcasted_iota(I32, (128, 256), 0) + chunk * 128
                    hit = jnp.where(tile == key, 1.0, 0.0).astype(BF)
                    s = dot(hit, rhs)
                    hi, lo = split(s[:, :128] + s[:, 128:])
                    for i in range(4):
                        at = pl.multiple_of((chunk * 4 + i) * 256 + c * 32, 32)
                        ghl[pm, pl.ds(at, 32), :128] = hi[i * 32:i * 32 + 32]
                        ghl[pm, pl.ds(at, 32), 128:] = lo[i * 32:i * 32 + 32]
                return 0

            lax.fori_loop(0, 8, block, 0)
        zc[...] = jnp.zeros((128, 256), F32)

        def row(t, _, rp=rp):
            @pl.when((kind == 1) & (t > 0))
            def _():
                zc[...] = mix(2, 1)

            columns(0, t)
            columns(1, 15 - t)
            z = mix(0, 0) + mix(1, 1) + zc[...]
            emit(z, rp * 32 + 2 * t, (0, 1))
            return 0

        lax.fori_loop(0, 16, row, 0)

        @pl.when(kind == 1)
        def _(rp=rp):
            emit(mix(2, 1), 64 + rp, (0,))


def middle(dev, recv, table):
    t = tables()
    smem = pl.BlockSpec(memory_space=pltpu.SMEM)
    whole = pl.BlockSpec(memory_space=pltpu.VMEM)
    return pl.pallas_call(
        middle_kernel,
        out_shape=jax.ShapeDtypeStruct((128 * MSG, 128), F32),
        in_specs=[smem] + [whole] * 7,
        out_specs=whole,
        scratch_shapes=[
            pltpu.VMEM((256, 128), I32),
            pltpu.VMEM((2, 16 * 256, 256), BF),
            pltpu.VMEM((2, 256, 256), BF),
            pltpu.VMEM((2, 256, 256), BF),
            pltpu.VMEM((128, 256), F32),
        ],
        compiler_params=pltpu.CompilerParams(vmem_limit_bytes=VMEM),
        name="middle",
    )(dev, recv, table, t["wc"][0], t["wc"][1], t["tw"][0], t["tw"][1], t["f"])


def final_kernel(x, wh, wl, sh, sl, xh, xl, tj, out, val):
    pair = pl.program_id(1)

    def three(a, bh, bl):
        ah, al = split(a)
        return dot(ah, bh) + dot(al, bh) + dot(ah, bl)

    rows = jnp.concatenate([x[0, 0, q, :64, :] for q in range(4)], axis=0)
    a = rows.T

    @pl.when(pair > 0)
    def _():
        u = three(a, wh[...], wl[...])
        vr = u[:64, :256] - u[64:, 256:]
        vi = u[:64, 256:] + u[64:, :256]
        tr, ti = tj[0, 0:1, :], tj[0, 1:2, :]
        val[2 * pair] = vr * tr - vi * ti
        val[2 * pair + 1] = vr * ti + vi * tr

    @pl.when(pair == 0)
    def _():
        extra = jnp.concatenate([x[0, 0, q, 64:72, :] for q in range(4)], axis=0)
        extra = jnp.concatenate([extra, jnp.zeros((96, 128), F32)], axis=0).T[:, :32]
        v = three(a[:64], sh[0], sl[0]) + three(a[64:], sh[1], sl[1])
        v = v + three(extra[:64], xh[0], xl[0]) + three(extra[64:], xh[1], xl[1])
        val[0] = v[:, :256]
        val[1] = v[:, 256:]

    @pl.when(pair == 15)
    def _():
        index = {}
        for i, j in enumerate(PAIR_J):
            if i > 0:
                index[j if j < 16 else 32 - j] = (i, 1.0 if j < 16 else -1.0)

        def strip(i, _):
            at = pl.ds(pl.multiple_of(i * 8, 8), 8)
            for tile in range(2):
                lanes = slice(tile * 128, tile * 128 + 128)
                zero, mid = val[0, at, lanes], val[1, at, lanes]
                re = {j: val[2 * k, at, lanes] for j, (k, _) in index.items()}
                im = {j: val[2 * k + 1, at, lanes] for j, (k, _) in index.items()}

                def wave(fun, part, js, l1, signed):
                    total = None
                    for j in js:
                        turn = j * l1 % 32
                        c = fun(2 * math.pi * turn / 32)
                        if signed:
                            c = c * index[j][1]
                        if abs(c) < 1e-12:
                            continue
                        if abs(abs(c) - 1) < 1e-12:
                            term = part[j]
                            if total is None:
                                total = term if c > 0 else -term
                            else:
                                total = total + term if c > 0 else total - term
                        else:
                            term = part[j] * c
                            total = term if total is None else total + term
                    return total if total is not None else jnp.zeros((8, 128), F32)

                odd = range(1, 16, 2)
                ce, se = [None] * 9, [None] * 9
                for l1 in range(5):
                    sign = 1.0 if l1 % 2 == 0 else -1.0
                    ee = wave(math.cos, re, (4, 8, 12), l1, False)
                    ee = ee + (zero + mid if sign > 0 else zero - mid)
                    eo = wave(math.cos, re, (2, 6, 10, 14), l1, False)
                    oe = wave(math.sin, im, (4, 8, 12), l1, True)
                    oo = wave(math.sin, im, (2, 6, 10, 14), l1, True)
                    ce[l1], ce[8 - l1] = ee + eo, ee - eo
                    se[l1], se[8 - l1] = oe + oo, oo - oe
                for l1 in range(9):
                    co = wave(math.cos, re, odd, l1, False)
                    so = wave(math.sin, im, odd, l1, True)
                    p, m = ce[l1] + co, ce[l1] - co
                    s, d = se[l1] + so, se[l1] - so

                    def put(l, value):
                        out[0, at, l * 256 + tile * 128:l * 256 + tile * 128 + 128] = value

                    put(l1, p + s)
                    put(16 + l1, m + d)
                    if l1 > 0:
                        put(32 - l1, p - s)
                        if l1 < 8:
                            put(16 - l1, m - d)
            return 0

        lax.fori_loop(0, 8, strip, 0)


def final(recv):
    t = tables()
    whole = pl.BlockSpec(memory_space=pltpu.VMEM)
    return pl.pallas_call(
        final_kernel,
        grid=(2, 16),
        out_shape=jax.ShapeDtypeStruct((2, 64, 8192), F32),
        in_specs=[pl.BlockSpec((1, 1, 4, MSG, 128), lambda f, j: (j, f, 0, 0, 0))]
        + [whole] * 6
        + [pl.BlockSpec((1, 2, 256), lambda f, j: (j, 0, 0))],
        out_specs=pl.BlockSpec((1, 64, 8192), lambda f, j: (f, 0, 0)),
        scratch_shapes=[pltpu.VMEM((32, 64, 256), F32)],
        compiler_params=pltpu.CompilerParams(vmem_limit_bytes=VMEM),
        name="final",
    )(recv, *t["wr"], *t["ws"], *t["wx"], t["tj"])


def pixel_view(pixels):
    x = pixels.reshape(128, 2, 2, 8, 128).transpose(0, 1, 3, 2, 4)
    return x.reshape(128, 2, 16, 128)


def beam_view(aterms):
    x = aterms.reshape(512, 2, 2, 2, 8, 128).transpose(0, 1, 2, 4, 3, 5)
    return x.reshape(1024, 2, 16, 128)


def pack(tile_offsets, station_pairs, time_blocks, channel_blocks):
    return jnp.concatenate(
        [
            tile_offsets[:, 0], tile_offsets[:, 1],
            station_pairs[:, 0] * 2 + time_blocks, station_pairs[:, 1] * 2 + time_blocks,
            channel_blocks,
        ]
    )


def local(
    subgrid_pixels, tile_offsets, station_pairs, time_blocks, channel_blocks, valid_counts,
    aterms, channel_weights,
):
    axes = ("row", "col")
    me = lax.axis_index(axes)
    packed = pack(tile_offsets, station_pairs, time_blocks, channel_blocks)
    table, target = slots(packed, valid_counts)
    everyone = lax.all_gather(table, axes, axis=0, tiled=False)
    send = source(
        packed, valid_counts, channel_weights, target.reshape(1, 128),
        pixel_view(subgrid_pixels), beam_view(aterms),
    )
    recv = lax.all_to_all(send, axes, split_axis=0, concat_axis=0, tiled=True)
    dev = jnp.stack([(me < 8).astype(I32), me % 4]).astype(I32)
    half = middle(dev, recv.reshape(128 * 64, 128), everyone)
    half = lax.all_to_all(
        half.reshape(128, MSG, 128), axes, split_axis=0, concat_axis=0, tiled=True
    )
    return final(half.reshape(16, 2, 4, MSG, 128))


def solution(mesh):
    in_specs = (
        P(("row", "col"), None, None, None),
        P(("row", "col"), None),
        P(("row", "col"), None),
        P(("row", "col")),
        P(("row", "col")),
        P(("row", "col")),
        P(),
        P(),
    )
    out_specs = P(None, ("row", "col"), None)
    return jax.shard_map(local, mesh=mesh, in_specs=in_specs, out_specs=out_specs, check_vma=False)
```

```python
import functools
import math

import jax
import jax.numpy as jnp
import ml_dtypes
import numpy as np
from jax import lax
from jax.experimental import pallas as pl
from jax.experimental.pallas import tpu as pltpu
from jax.sharding import PartitionSpec as P

BF = jnp.bfloat16
F32 = jnp.float32
I32 = jnp.int32

PAIR_J = (0, 8, 4, 12, 1, 9, 17, 25, 2, 10, 18, 26, 3, 11, 19, 27)
STEP_A = (0, 4, 1, 1, 2, 2, 3, 3)
STEP_B = (0, 4, 7, 7, 6, 6, 5, 5)
VMEM = 56 * 1024 * 1024


def partner(j):
    return 16 if j == 0 else 32 - j


def unit(turns):
    return np.exp(-2j * np.pi * turns)


def split_np(x):
    hi = np.asarray(x, np.float32).astype(ml_dtypes.bfloat16)
    lo = (np.asarray(x, np.float64) - hi.astype(np.float64)).astype(ml_dtypes.bfloat16)
    return hi, lo


def split(x):
    hi = x.astype(BF)
    return hi, (x - hi.astype(F32)).astype(BF)


def dot(a, b):
    return lax.dot_general(a, b, (((1,), (0,)), ((), ())), preferred_element_type=F32)


def dot_nt(a, b):
    return lax.dot_general(a, b, (((1,), (1,)), ((), ())), preferred_element_type=F32)


@functools.lru_cache(None)
def tables():
    xi = np.arange(4)[:, None, None]
    y = np.arange(32)[None, :, None]
    v = np.arange(32)[None, None, :]
    b = np.zeros((8, 2, 2, 4, 32, 2, 2, 2, 32))
    for step in range(8):
        for pair in range(2):
            j = PAIR_J[2 * step + pair]
            for half, jj in enumerate((j, partner(j))):
                w = unit((xi * jj + y * v) % 32 / 32) / 32
                b[step, half, 0, :, :, pair, half, 0] = w.real
                b[step, half, 0, :, :, pair, half, 1] = w.imag
                b[step, half, 1, :, :, pair, half, 0] = -w.imag
                b[step, half, 1, :, :, pair, half, 1] = w.real
    b = b.reshape(8, 2, 256, 256)
    i = np.arange(256)
    w = unit(i[:, None] * i[None, :] % 256 / 256)
    wc = np.stack([w.real.reshape(4, 64, 256), w.imag.reshape(4, 64, 256)], 1).reshape(512, 256)
    tw = unit(i[:, None] * (np.arange(128) % 32)[None, :] / 8192)
    d = unit(np.arange(32)[:, None] * np.arange(32)[None, :] % 32 / 32)
    coef = np.stack([np.stack([d, 1j * d]), np.stack([1j * d, -d])])
    f = np.zeros((2, 3, 2, 2, 32, 2, 2, 2, 32))

    def put(kind, which, half, pm, conj):
        for pq in range(2):
            for reim in range(2):
                c = coef[pq, reim]
                f[kind, which, pm, 0, :, pq, half, reim, :] = c.real
                f[kind, which, pm, 1, :, pq, half, reim, :] = -c.imag if conj else c.imag

    put(0, 0, 0, 0, False)
    put(0, 0, 1, 1, True)
    put(0, 1, 1, 0, True)
    put(0, 1, 0, 1, False)
    put(1, 0, 0, 0, False)
    put(1, 0, 1, 1, False)
    put(1, 1, 1, 1, True)
    put(1, 2, 0, 0, True)
    f = f.reshape(2, 3, 128, 256)
    fh, fl = split_np(f)
    f = np.concatenate([fh, fl], axis=2)
    k = np.arange(256)
    q, rp, t, pm = k // 64, k // 32 % 2, k // 2 % 16, k % 2
    r = 16 * (2 * q + rp) + t
    rr = np.where(pm == 0, r, 255 - r)
    l0 = np.arange(256)
    w = unit(rr[:, None] * l0[None, :] % 256 / 256) / 4096
    wr = np.concatenate([w.real, w.imag], axis=1)
    w0 = np.where((pm == 0)[:, None], unit(r[:, None] * l0[None, :] % 256 / 256), 0) / 4096
    w16 = np.where((pm == 1)[:, None], unit((32 * r[:, None] + 16) * l0[None, :] % 8192 / 8192), 0) / 4096
    ws = np.stack([np.concatenate([w0.real, w16.real], 1), np.concatenate([-w0.imag, -w16.imag], 1)])
    kx = np.arange(32)
    qx, row = kx // 8, kx % 8
    rx = 16 * (15 - (2 * qx + row))
    wx = np.where((row < 2)[:, None], unit(-(rx[:, None] * l0[None, :] % 256) / 256), 0) / 4096
    zero = np.zeros_like(wx.real)
    wx = np.stack([np.concatenate([wx.real, zero], 1), np.concatenate([-wx.imag, zero], 1)])
    tj = unit(np.array(PAIR_J)[:, None] * l0[None, :] / 8192)
    tj = np.stack([tj.real, tj.imag], 1).astype(np.float32)
    return dict(
        b=split_np(b), wc=split_np(wc), tw=(tw.real.astype(np.float32), tw.imag.astype(np.float32)),
        f=f, wr=split_np(wr), ws=split_np(ws), wx=split_np(wx), tj=tj,
    )


def slot_kernel(pk, vc, table, target, count):
    def clear(i, _):
        count[i] = 0
        for k in range(4):
            table[4 * i + k] = -1
        return 0

    lax.fori_loop(0, 128, clear, 0)

    def place(s, _):
        row = pk[s]
        col = pk[128 + s]
        block_row = row // 16
        low = block_row < 8
        near = jnp.where(low, block_row, 15 - block_row)
        place_row = near // 2 * 4 + near % 2 * 2 + jnp.where(low, 0, 1)
        block = place_row * 8 + col // 32
        rank = count[block]
        valid = s < vc[0]
        slot = block * 2 + jnp.minimum(rank, 1)
        target[s] = jnp.where(valid, slot, -1)

        @pl.when(valid)
        def _():
            count[block] = rank + 1
            table[slot // 64 * 128 + slot % 64] = row % 16 * 32 + col % 32

        return 0

    lax.fori_loop(0, 128, place, 0)


def slots(packed, count):
    smem = pl.BlockSpec(memory_space=pltpu.SMEM)
    return pl.pallas_call(
        slot_kernel,
        out_shape=(jax.ShapeDtypeStruct((512,), I32), jax.ShapeDtypeStruct((128,), I32)),
        in_specs=[smem, smem],
        out_specs=(smem, smem),
        scratch_shapes=[pltpu.SMEM((128,), I32)],
        name="slots",
    )(packed, count)


def dft8(re, im):
    h = math.sqrt(0.5)

    def four(a, b):
        s0r, s0i = a[0] + a[2], b[0] + b[2]
        s1r, s1i = a[0] - a[2], b[0] - b[2]
        s2r, s2i = a[1] + a[3], b[1] + b[3]
        s3r, s3i = a[1] - a[3], b[1] - b[3]
        return (
            [s0r + s2r, s1r + s3i, s0r - s2r, s1r - s3i],
            [s0i + s2i, s1i - s3r, s0i - s2i, s1i + s3r],
        )

    er, ei = four(re[0::2], im[0::2])
    orr, oi = four(re[1::2], im[1::2])
    tr = [orr[0], (orr[1] + oi[1]) * h, oi[2], (oi[3] - orr[3]) * h]
    ti = [oi[0], (oi[1] - orr[1]) * h, -orr[2], -(oi[3] + orr[3]) * h]
    return (
        [er[k] + tr[k] for k in range(4)] + [er[k] - tr[k] for k in range(4)],
        [ei[k] + ti[k] for k in range(4)] + [ei[k] - ti[k] for k in range(4)],
    )


def source_kernel(
    pk, vc, cw, ja, jb, tgt, px, beams, bh, bl, out, got, corr, lhi, llo, perm, sems
):
    step = pl.program_id(0)

    @pl.when(step == 0)
    def _():
        for group in range(8):
            def fetch(i, _, group=group):
                s = group * 16 + i
                for e in range(2):
                    pltpu.make_async_copy(
                        beams.at[pk[256 + 128 * e + s]], got.at[s, e], sems.at[group]
                    ).start()
                return 0

            lax.fori_loop(0, 16, fetch, 0)
        slot = lax.broadcasted_iota(I32, (256, 128), 0)
        hit = jnp.where(slot == tgt[...], 1.0, 0.0).astype(BF)
        perm[:, :128] = hit
        perm[:, 128:] = hit
        for group in range(8):
            part = got.at[pl.ds(group * 16, 16)]
            pltpu.make_async_copy(part, part, sems.at[group]).wait()

            def correct(i, _, group=group):
                s = group * 16 + i
                weight = jnp.where(s < vc[0], cw[pk[512 + s]], 0.0)
                ar, ai = got[s, 0, 0].astype(F32), got[s, 0, 1].astype(F32)
                br, bi = got[s, 1, 0].astype(F32), got[s, 1, 1].astype(F32)
                gr = (ar * br + ai * bi) * weight
                gi = (ai * br - ar * bi) * weight
                pr, pi = px[s, 0], px[s, 1]
                at = pl.multiple_of(s * 32, 32)
                corr[pl.ds(at, 16), :] = pr * gr - pi * gi
                corr[pl.ds(at + 16, 16), :] = pr * gi + pi * gr
                return 0

            lax.fori_loop(0, 16, correct, 0, unroll=2)

            for f in range(2):
                base = group * 16 * 32 + f
                re = [corr[pl.ds(base + 2 * p, 16, stride=32), :] for p in range(8)]
                im = [corr[pl.ds(base + 16 + 2 * p, 16, stride=32), :] for p in range(8)]
                re, im = dft8(re, im)
                rows = slice(f * 128 + group * 16, f * 128 + group * 16 + 16)
                for k in range(8):
                    lhi[k, rows, :128], llo[k, rows, :128] = split(re[k])
                    lhi[k, rows, 128:], llo[k, rows, 128:] = split(im[k])

    acc = jnp.zeros((256, 256), F32)
    for half, pick in enumerate((ja, jb)):
        k = pick[step]
        acc = acc + dot(lhi[k], bh[0, half]) + dot(llo[k], bh[0, half]) + dot(lhi[k], bl[0, half])
    hi, lo = split(acc)
    for f in range(2):
        rows = slice(f * 128, f * 128 + 128)
        padded = dot(perm[...], jnp.concatenate([hi[rows], lo[rows]], axis=0))
        for pair in range(2):
            for q in range(4):
                out[(pair * 2 + f) * 4 + q] = padded[q * 64:(q + 1) * 64, pair * 128:(pair + 1) * 128]


def source(packed, count, weights, target, pixels, beams):
    t = tables()
    smem = pl.BlockSpec(memory_space=pltpu.SMEM)
    whole = pl.BlockSpec(memory_space=pltpu.VMEM)
    return pl.pallas_call(
        source_kernel,
        grid=(8,),
        out_shape=jax.ShapeDtypeStruct((128, 64, 128), F32),
        in_specs=[smem, smem, smem, smem, smem, whole, whole, pl.BlockSpec(memory_space=pl.ANY)]
        + [pl.BlockSpec((1, 2, 256, 256), lambda i: (i, 0, 0, 0))] * 2,
        out_specs=pl.BlockSpec((16, 64, 128), lambda i: (i, 0, 0)),
        scratch_shapes=[
            pltpu.VMEM((128, 2, 2, 16, 128), BF),
            pltpu.VMEM((128 * 32, 128), F32),
            pltpu.VMEM((8, 256, 256), BF),
            pltpu.VMEM((8, 256, 256), BF),
            pltpu.VMEM((256, 256), BF),
            pltpu.SemaphoreType.DMA((8,)),
        ],
        compiler_params=pltpu.CompilerParams(vmem_limit_bytes=VMEM),
        name="source",
    )(
        packed, count, weights, np.array(STEP_A, np.int32), np.array(STEP_B, np.int32), target,
        pixels, beams, t["b"][0], t["b"][1],
    )


def spread(i):
    o = lax.rem(i * 37, 128)
    row, col = lax.axis_index("row"), lax.axis_index("col")
    x = lax.rem(lax.div(row, 4) + lax.div(o, 32), 4)
    y = lax.rem(lax.rem(row, 4) + lax.rem(lax.div(o, 8), 4), 4)
    z = lax.rem(lax.div(col, 2) + lax.rem(lax.div(o, 2), 4), 4)
    c = lax.rem(col + o, 2)
    return x * 4 + y, z * 2 + c


def exchange_kernel(
    send, tabs, wh, wl, twr, twi, fmat, out, outx,
    recv, tabr, tabt, ghl, pqh, pql, zc, stage, extra, ssem, rsem, lsem
):
    me = lax.axis_index("row") * 8 + lax.axis_index("col")
    first = me < 8
    kind = jnp.where(first, 1, 0)
    barrier = pltpu.get_barrier_semaphore()

    def each(fun):
        def step(i, _):
            row, col = spread(i)
            fun(row * 8 + col, (row, col))
            return 0

        lax.fori_loop(1, 128, step, 0)

    def push(src, dst, k, dev):
        pltpu.make_async_remote_copy(
            src_ref=src, dst_ref=dst, send_sem=ssem.at[k], recv_sem=rsem.at[k],
            device_id=dev, device_id_type=pl.DeviceIdType.MESH,
        ).start()

    def wait(part, sem):
        pltpu.make_async_copy(part, part, sem).wait()

    def keep(src, dst):
        copy = pltpu.make_async_copy(src, dst, lsem)
        copy.start()
        copy.wait()

    each(lambda d, dev: pl.semaphore_signal(
        barrier, inc=1, device_id=dev, device_id_type=pl.DeviceIdType.MESH))
    pl.semaphore_wait(barrier, 127)
    each(lambda d, dev: push(tabs.at[lax.rem(d, 4)], tabr.at[me], 0, dev))
    for rp in range(2):
        rows = pl.ds(rp * 32, 32)
        each(lambda d, dev: push(send.at[d, rows], recv.at[me, rows], 1 + rp, dev))
    keep(tabs.at[lax.rem(me, 4)], tabr.at[me])
    keep(send.at[me], recv.at[me])
    flat = recv.reshape(128 * 64, 128)

    extra[...] = jnp.zeros((1024, 128), F32)
    wait(tabr.at[pl.ds(0, 127)], rsem.at[0])
    tabt[...] = tabr[...].reshape(128, 128).T
    lane = lax.broadcasted_iota(I32, (32, 128), 1)
    low = lane < 64

    def columns(pm, t):
        g = ghl[pm, pl.ds(pl.multiple_of(t * 256, 256), 256), :]
        for c in range(4):
            rows = slice(c * 128, c * 128 + 128)
            a = dot(wh[rows, :], g)
            b = dot(wl[rows, :], g[:, :128])
            u = a[:, :128] + a[:, 128:] + b
            ur, ui = u[:64], u[64:]
            m0 = slice(c * 64, c * 64 + 64)
            tr, ti = twr[m0, :], twi[m0, :]
            pqh[pm, m0, :128], pql[pm, m0, :128] = split(tr * ur - ti * ui)
            pqh[pm, m0, 128:], pql[pm, m0, 128:] = split(tr * ui + ti * ur)

    def mix(which, pm):
        both = fmat[kind, which]
        z = dot_nt(both, pqh[pm])
        return z[:128] + z[128:] + dot_nt(both[:128], pql[pm])

    def emit(dst, size, z, row, pms):
        for pm in pms:
            for tile in range(2):
                lanes = slice(tile * 128, tile * 128 + 128)
                re, im = z[pm * 64:pm * 64 + 32, lanes], z[pm * 64 + 32:pm * 64 + 64, lanes]
                even = jnp.where(low, re, pltpu.roll(im, 64, 1))
                odd = jnp.where(low, pltpu.roll(re, 64, 1), im)
                dst[pl.ds(2 * tile * size + row + pm, 32, stride=4 * size), :] = even
                dst[pl.ds((2 * tile + 1) * size + row + pm, 32, stride=4 * size), :] = odd

    def phase(rp, _):
        rows = pl.ds(pl.multiple_of(rp * 32, 32), 32)
        wait(recv.at[pl.ds(0, 127), rows], rsem.at[1 + rp])
        for pm in range(2):
            def block(c, _, pm=pm):
                at = rp * 32 + pm * 16 + 2 * c
                key = jnp.concatenate([tabt[pl.ds(at + k, 1), :] for k in range(2)], axis=1)
                parts = [split(flat[pl.ds(at + k, 128, stride=64), :]) for k in range(2)]
                rhs = jnp.concatenate([jnp.concatenate(p, axis=1) for p in parts], axis=0)
                for chunk in range(4):
                    tile = lax.broadcasted_iota(I32, (128, 256), 0) + chunk * 128
                    hit = jnp.where(tile == key, 1.0, 0.0).astype(BF)
                    s = dot(hit, rhs)
                    hi, lo = split(s[:, :128] + s[:, 128:])
                    for i in range(4):
                        to = pl.multiple_of((chunk * 4 + i) * 256 + c * 32, 32)
                        ghl[pm, pl.ds(to, 32), :128] = hi[i * 32:i * 32 + 32]
                        ghl[pm, pl.ds(to, 32), 128:] = lo[i * 32:i * 32 + 32]
                return 0

            lax.fori_loop(0, 8, block, 0)
        zc[...] = jnp.zeros((128, 256), F32)

        def row(t, _):
            @pl.when(first & (t > 0))
            def _():
                zc[...] = mix(2, 1)

            columns(0, t)
            columns(1, 15 - t)
            emit(stage, 64, mix(0, 0) + mix(1, 1) + zc[...], rp * 32 + 2 * t, (0, 1))
            return 0

        lax.fori_loop(0, 16, row, 0)

        @pl.when(first)
        def _():
            emit(extra, 8, mix(2, 1), rp, (0,))

        def piece(d):
            return stage.at[pl.ds(pl.multiple_of(d * 64 + rp * 32, 32), 32), :]

        each(lambda d, dev: push(piece(d), out.at[me, rows], 3 + rp, dev))
        keep(piece(me), out.at[me, rows])
        return 0

    lax.fori_loop(0, 2, phase, 0)

    def piece(d):
        return extra.at[pl.ds(pl.multiple_of(d * 8, 8), 8), :]

    @pl.when(first)
    def _():
        each(lambda d, dev: push(piece(d), outx.at[me], 5, dev))
        keep(piece(me), outx.at[me])
        wait(outx.at[pl.ds(0, 7)], rsem.at[5])
        wait(extra.at[pl.ds(0, 127 * 8), :], ssem.at[5])

    @pl.when(me >= 8)
    def _():
        wait(outx, rsem.at[5])

    wait(tabr.at[pl.ds(0, 127)], ssem.at[0])
    for rp in range(2):
        part = recv.at[pl.ds(0, 127), pl.ds(rp * 32, 32)]
        wait(part, ssem.at[1 + rp])
        wait(part, ssem.at[3 + rp])
        wait(out.at[pl.ds(0, 127), pl.ds(rp * 32, 32)], rsem.at[3 + rp])


def exchange(send, tabs):
    t = tables()
    whole = pl.BlockSpec(memory_space=pltpu.VMEM)
    away = pl.BlockSpec(memory_space=pl.ANY)
    return pl.pallas_call(
        exchange_kernel,
        out_shape=(
            jax.ShapeDtypeStruct((128, 64, 128), F32), jax.ShapeDtypeStruct((8, 8, 128), F32)
        ),
        in_specs=[away, whole] + [whole] * 5,
        out_specs=(away, away),
        scratch_shapes=[
            pltpu.VMEM((128, 64, 128), F32),
            pltpu.VMEM((128, 1, 128), I32),
            pltpu.VMEM((128, 128), I32),
            pltpu.VMEM((2, 16 * 256, 256), BF),
            pltpu.VMEM((2, 256, 256), BF),
            pltpu.VMEM((2, 256, 256), BF),
            pltpu.VMEM((128, 256), F32),
            pltpu.VMEM((128 * 64, 128), F32),
            pltpu.VMEM((128 * 8, 128), F32),
            pltpu.SemaphoreType.DMA((6,)),
            pltpu.SemaphoreType.DMA((6,)),
            pltpu.SemaphoreType.DMA,
        ],
        compiler_params=pltpu.CompilerParams(
            vmem_limit_bytes=VMEM, collective_id=0, has_side_effects=True
        ),
        name="exchange",
    )(send, tabs, t["wc"][0], t["wc"][1], t["tw"][0], t["tw"][1], t["f"])


def final_kernel(x, ex, wh, wl, sh, sl, xh, xl, tj, out, val):
    pair = pl.program_id(1)

    def three(a, bh, bl):
        ah, al = split(a)
        return dot(ah, bh) + dot(al, bh) + dot(ah, bl)

    rows = jnp.concatenate([x[0, 0, q] for q in range(4)], axis=0)
    a = rows.T

    @pl.when(pair > 0)
    def _():
        u = three(a, wh[...], wl[...])
        vr = u[:64, :256] - u[64:, 256:]
        vi = u[:64, 256:] + u[64:, :256]
        tr, ti = tj[0, 0:1, :], tj[0, 1:2, :]
        val[2 * pair] = vr * tr - vi * ti
        val[2 * pair + 1] = vr * ti + vi * tr

    @pl.when(pair == 0)
    def _():
        extra = jnp.concatenate([ex[0, q] for q in range(4)], axis=0)
        extra = jnp.concatenate([extra, jnp.zeros((96, 128), F32)], axis=0).T[:, :32]
        v = three(a[:64], sh[0], sl[0]) + three(a[64:], sh[1], sl[1])
        v = v + three(extra[:64], xh[0], xl[0]) + three(extra[64:], xh[1], xl[1])
        val[0] = v[:, :256]
        val[1] = v[:, 256:]

    @pl.when(pair == 15)
    def _():
        index = {}
        for i, j in enumerate(PAIR_J):
            if i > 0:
                index[j if j < 16 else 32 - j] = (i, 1.0 if j < 16 else -1.0)

        def strip(i, _):
            at = pl.ds(pl.multiple_of(i * 8, 8), 8)
            for tile in range(2):
                lanes = slice(tile * 128, tile * 128 + 128)
                zero, mid = val[0, at, lanes], val[1, at, lanes]
                re = {j: val[2 * k, at, lanes] for j, (k, _) in index.items()}
                im = {j: val[2 * k + 1, at, lanes] for j, (k, _) in index.items()}

                def wave(fun, part, js, l1, signed):
                    total = None
                    for j in js:
                        turn = j * l1 % 32
                        c = fun(2 * math.pi * turn / 32)
                        if signed:
                            c = c * index[j][1]
                        if abs(c) < 1e-12:
                            continue
                        if abs(abs(c) - 1) < 1e-12:
                            term = part[j]
                            if total is None:
                                total = term if c > 0 else -term
                            else:
                                total = total + term if c > 0 else total - term
                        else:
                            term = part[j] * c
                            total = term if total is None else total + term
                    return total if total is not None else jnp.zeros((8, 128), F32)

                odd = range(1, 16, 2)
                ce, se = [None] * 9, [None] * 9
                for l1 in range(5):
                    sign = 1.0 if l1 % 2 == 0 else -1.0
                    ee = wave(math.cos, re, (4, 8, 12), l1, False)
                    ee = ee + (zero + mid if sign > 0 else zero - mid)
                    eo = wave(math.cos, re, (2, 6, 10, 14), l1, False)
                    oe = wave(math.sin, im, (4, 8, 12), l1, True)
                    oo = wave(math.sin, im, (2, 6, 10, 14), l1, True)
                    ce[l1], ce[8 - l1] = ee + eo, ee - eo
                    se[l1], se[8 - l1] = oe + oo, oo - oe
                for l1 in range(9):
                    co = wave(math.cos, re, odd, l1, False)
                    so = wave(math.sin, im, odd, l1, True)
                    p, m = ce[l1] + co, ce[l1] - co
                    s, d = se[l1] + so, se[l1] - so

                    def put(l, value):
                        out[0, at, l * 256 + tile * 128:l * 256 + tile * 128 + 128] = value

                    put(l1, p + s)
                    put(16 + l1, m + d)
                    if l1 > 0:
                        put(32 - l1, p - s)
                        if l1 < 8:
                            put(16 - l1, m - d)
            return 0

        lax.fori_loop(0, 8, strip, 0)


def final(recv, extra):
    t = tables()
    whole = pl.BlockSpec(memory_space=pltpu.VMEM)
    return pl.pallas_call(
        final_kernel,
        grid=(2, 16),
        out_shape=jax.ShapeDtypeStruct((2, 64, 8192), F32),
        in_specs=[
            pl.BlockSpec((1, 1, 4, 64, 128), lambda f, j: (j, f, 0, 0, 0)),
            pl.BlockSpec((1, 4, 8, 128), lambda f, j: (f, 0, 0, 0)),
        ]
        + [whole] * 6
        + [pl.BlockSpec((1, 2, 256), lambda f, j: (j, 0, 0))],
        out_specs=pl.BlockSpec((1, 64, 8192), lambda f, j: (f, 0, 0)),
        scratch_shapes=[pltpu.VMEM((32, 64, 256), F32)],
        compiler_params=pltpu.CompilerParams(vmem_limit_bytes=VMEM),
        name="final",
    )(recv, extra, *t["wr"], *t["ws"], *t["wx"], t["tj"])


def pixel_view(pixels):
    x = pixels.reshape(128, 2, 2, 8, 128).transpose(0, 1, 3, 2, 4)
    return x.reshape(128, 2, 16, 128)


def beam_view(aterms):
    x = aterms.reshape(512, 2, 2, 2, 8, 128).transpose(0, 1, 2, 4, 3, 5)
    return x.reshape(1024, 2, 16, 128)


def pack(tile_offsets, station_pairs, time_blocks, channel_blocks):
    return jnp.concatenate(
        [
            tile_offsets[:, 0], tile_offsets[:, 1],
            station_pairs[:, 0] * 2 + time_blocks, station_pairs[:, 1] * 2 + time_blocks,
            channel_blocks,
        ]
    )


def local(
    subgrid_pixels, tile_offsets, station_pairs, time_blocks, channel_blocks, valid_counts,
    aterms, channel_weights,
):
    packed = pack(tile_offsets, station_pairs, time_blocks, channel_blocks)
    table, target = slots(packed, valid_counts)
    send = source(
        packed, valid_counts, channel_weights, target.reshape(1, 128),
        pixel_view(subgrid_pixels), beam_view(aterms),
    )
    half, extra = exchange(send, table.reshape(4, 1, 128))
    return final(half.reshape(16, 2, 4, 64, 128), extra.reshape(2, 4, 8, 128))


def solution(mesh):
    in_specs = (
        P(("row", "col"), None, None, None),
        P(("row", "col"), None),
        P(("row", "col"), None),
        P(("row", "col")),
        P(("row", "col")),
        P(("row", "col")),
        P(),
        P(),
    )
    out_specs = P(None, ("row", "col"), None)
    return jax.shard_map(local, mesh=mesh, in_specs=in_specs, out_specs=out_specs, check_vma=False)
```

```python
import functools
import math

import jax
import jax.numpy as jnp
import ml_dtypes
import numpy as np
from jax import lax
from jax.experimental import pallas as pl
from jax.experimental.pallas import tpu as pltpu
from jax.sharding import PartitionSpec as P

BF = jnp.bfloat16
F32 = jnp.float32
I32 = jnp.int32

PAIR_J = (0, 8, 4, 12, 1, 9, 17, 25, 2, 10, 18, 26, 3, 11, 19, 27)
STEP_A = (0, 4, 1, 1, 2, 2, 3, 3)
STEP_B = (0, 4, 7, 7, 6, 6, 5, 5)
VMEM = 56 * 1024 * 1024


def partner(j):
    return 16 if j == 0 else 32 - j


def unit(turns):
    return np.exp(-2j * np.pi * turns)


def split_np(x):
    hi = np.asarray(x, np.float32).astype(ml_dtypes.bfloat16)
    lo = (np.asarray(x, np.float64) - hi.astype(np.float64)).astype(ml_dtypes.bfloat16)
    return hi, lo


def split(x):
    hi = x.astype(BF)
    return hi, (x - hi.astype(F32)).astype(BF)


def dot(a, b):
    return lax.dot_general(a, b, (((1,), (0,)), ((), ())), preferred_element_type=F32)


def dot_nt(a, b):
    return lax.dot_general(a, b, (((1,), (1,)), ((), ())), preferred_element_type=F32)


@functools.lru_cache(None)
def tables():
    xi = np.arange(4)[:, None, None]
    y = np.arange(32)[None, :, None]
    v = np.arange(32)[None, None, :]
    b = np.zeros((8, 2, 2, 4, 32, 2, 2, 2, 32))
    for step in range(8):
        for pair in range(2):
            j = PAIR_J[2 * step + pair]
            for half, jj in enumerate((j, partner(j))):
                w = unit((xi * jj + y * v) % 32 / 32) / 32
                b[step, half, 0, :, :, pair, half, 0] = w.real
                b[step, half, 0, :, :, pair, half, 1] = w.imag
                b[step, half, 1, :, :, pair, half, 0] = -w.imag
                b[step, half, 1, :, :, pair, half, 1] = w.real
    b = b.reshape(8, 2, 256, 256)
    i = np.arange(256)
    w = unit(i[:, None] * i[None, :] % 256 / 256)
    wc = np.stack([w.real.reshape(4, 64, 256), w.imag.reshape(4, 64, 256)], 1).reshape(512, 256)
    tw = unit(i[:, None] * (np.arange(128) % 32)[None, :] / 8192)
    d = unit(np.arange(32)[:, None] * np.arange(32)[None, :] % 32 / 32)
    coef = np.stack([np.stack([d, 1j * d]), np.stack([1j * d, -d])])
    f = np.zeros((2, 3, 2, 2, 32, 2, 2, 2, 32))

    def put(kind, which, half, pm, conj):
        for pq in range(2):
            for reim in range(2):
                c = coef[pq, reim]
                f[kind, which, pm, 0, :, pq, half, reim, :] = c.real
                f[kind, which, pm, 1, :, pq, half, reim, :] = -c.imag if conj else c.imag

    put(0, 0, 0, 0, False)
    put(0, 0, 1, 1, True)
    put(0, 1, 1, 0, True)
    put(0, 1, 0, 1, False)
    put(1, 0, 0, 0, False)
    put(1, 0, 1, 1, False)
    put(1, 1, 1, 1, True)
    put(1, 2, 0, 0, True)
    f = f.reshape(2, 3, 128, 256)
    fh, fl = split_np(f)
    f = np.concatenate([fh, fl], axis=2)
    k = np.arange(256)
    q, rp, t, pm = k // 64, k // 32 % 2, k // 2 % 16, k % 2
    r = 16 * (2 * q + rp) + t
    rr = np.where(pm == 0, r, 255 - r)
    l0 = np.arange(256)
    w = unit(rr[:, None] * l0[None, :] % 256 / 256) / 4096
    wr = np.concatenate([w.real, w.imag], axis=1)
    w0 = np.where((pm == 0)[:, None], unit(r[:, None] * l0[None, :] % 256 / 256), 0) / 4096
    w16 = np.where((pm == 1)[:, None], unit((32 * r[:, None] + 16) * l0[None, :] % 8192 / 8192), 0) / 4096
    ws = np.stack([np.concatenate([w0.real, w16.real], 1), np.concatenate([-w0.imag, -w16.imag], 1)])
    kx = np.arange(32)
    qx, row = kx // 8, kx % 8
    rx = 16 * (15 - (2 * qx + row))
    wx = np.where((row < 2)[:, None], unit(-(rx[:, None] * l0[None, :] % 256) / 256), 0) / 4096
    zero = np.zeros_like(wx.real)
    wx = np.stack([np.concatenate([wx.real, zero], 1), np.concatenate([-wx.imag, zero], 1)])
    tj = unit(np.array(PAIR_J)[:, None] * l0[None, :] / 8192)
    tj = np.stack([tj.real, tj.imag], 1).astype(np.float32)
    return dict(
        b=split_np(b), wc=split_np(wc), tw=(tw.real.astype(np.float32), tw.imag.astype(np.float32)),
        f=f, wr=split_np(wr), ws=split_np(ws), wx=split_np(wx), tj=tj,
    )


def place(tiles, vc, table, count, perm):
    def clear(i, _):
        count[i] = 0
        for k in range(4):
            table[4 * i + k] = -1
        return 0

    lax.fori_loop(0, 128, clear, 0, unroll=8)
    perm[...] = jnp.zeros((256, 128), F32)
    lane = lax.broadcasted_iota(I32, (1, 128), 1)

    def one(s, _):
        row, col = tiles[0, s], tiles[1, s]
        block_row = row >> 4
        low = block_row < 8
        near = jnp.where(low, block_row, 15 - block_row)
        block = ((near << 1) + jnp.where(low, 0, 1)) * 8 + (col >> 5)
        rank = count[block]
        slot = block * 2 + jnp.minimum(rank, 1)
        count[block] = rank + 1
        table[((slot >> 6) << 7) + (slot & 63)] = ((row & 15) << 5) + (col & 31)
        perm[pl.ds(slot, 1), :] = jnp.where(lane == s, 1.0, 0.0)
        return 0

    lax.fori_loop(0, vc[0], one, 0)


def dft8(re, im):
    h = math.sqrt(0.5)

    def four(a, b):
        s0r, s0i = a[0] + a[2], b[0] + b[2]
        s1r, s1i = a[0] - a[2], b[0] - b[2]
        s2r, s2i = a[1] + a[3], b[1] + b[3]
        s3r, s3i = a[1] - a[3], b[1] - b[3]
        return (
            [s0r + s2r, s1r + s3i, s0r - s2r, s1r - s3i],
            [s0i + s2i, s1i - s3r, s0i - s2i, s1i + s3r],
        )

    er, ei = four(re[0::2], im[0::2])
    orr, oi = four(re[1::2], im[1::2])
    tr = [orr[0], (orr[1] + oi[1]) * h, oi[2], (oi[3] - orr[3]) * h]
    ti = [oi[0], (oi[1] - orr[1]) * h, -orr[2], -(oi[3] + orr[3]) * h]
    return (
        [er[k] + tr[k] for k in range(4)] + [er[k] - tr[k] for k in range(4)],
        [ei[k] + ti[k] for k in range(4)] + [ei[k] - ti[k] for k in range(4)],
    )


def source_kernel(
    tiles, pair, time, chan, vc, cw, ja, jb, px, beams, bh, bl, out, table,
    got, corr, lhi, llo, perm, count, sems
):
    step = pl.program_id(0)

    @pl.when(step == 0)
    def _():
        for group in range(8):
            def fetch(i, _, group=group):
                s = group * 16 + i
                for e in range(2):
                    pltpu.make_async_copy(
                        beams.at[pair[e, s] * 2 + time[s]], got.at[s, e], sems.at[group]
                    ).start()
                return 0

            lax.fori_loop(0, 16, fetch, 0, unroll=4)
        place(tiles, vc, table, count, perm)
        for group in range(8):
            part = got.at[pl.ds(group * 16, 16)]
            pltpu.make_async_copy(part, part, sems.at[group]).wait()

            def correct(i, _, group=group):
                s = group * 16 + i
                weight = jnp.where(s < vc[0], cw[chan[s]], 0.0)
                ar, ai = got[s, 0, 0].astype(F32), got[s, 0, 1].astype(F32)
                br, bi = got[s, 1, 0].astype(F32), got[s, 1, 1].astype(F32)
                gr = (ar * br + ai * bi) * weight
                gi = (ai * br - ar * bi) * weight
                pr, pi = px[s, 0], px[s, 1]
                at = pl.multiple_of(s * 32, 32)
                corr[pl.ds(at, 16), :] = pr * gr - pi * gi
                corr[pl.ds(at + 16, 16), :] = pr * gi + pi * gr
                return 0

            lax.fori_loop(0, 16, correct, 0, unroll=2)

            for f in range(2):
                base = group * 16 * 32 + f
                re = [corr[pl.ds(base + 2 * p, 16, stride=32), :] for p in range(8)]
                im = [corr[pl.ds(base + 16 + 2 * p, 16, stride=32), :] for p in range(8)]
                re, im = dft8(re, im)
                rows = slice(f * 128 + group * 16, f * 128 + group * 16 + 16)
                for k in range(8):
                    lhi[k, rows, :128], llo[k, rows, :128] = split(re[k])
                    lhi[k, rows, 128:], llo[k, rows, 128:] = split(im[k])

    acc = jnp.zeros((256, 256), F32)
    for half, pick in enumerate((ja, jb)):
        k = pick[step]
        acc = acc + dot(lhi[k], bh[0, half]) + dot(llo[k], bh[0, half]) + dot(lhi[k], bl[0, half])
    hi, lo = split(acc)
    both = perm[...].astype(BF)
    both = jnp.concatenate([both, both], axis=1)
    for f in range(2):
        rows = slice(f * 128, f * 128 + 128)
        padded = dot(both, jnp.concatenate([hi[rows], lo[rows]], axis=0))
        for pair in range(2):
            for q in range(4):
                out[(pair * 2 + f) * 4 + q] = padded[q * 64:(q + 1) * 64, pair * 128:(pair + 1) * 128]


def source(tiles, pair, time, chan, count, weights, pixels, beams):
    t = tables()
    smem = pl.BlockSpec(memory_space=pltpu.SMEM)
    whole = pl.BlockSpec(memory_space=pltpu.VMEM)
    return pl.pallas_call(
        source_kernel,
        grid=(8,),
        out_shape=(jax.ShapeDtypeStruct((128, 64, 128), F32), jax.ShapeDtypeStruct((512,), I32)),
        in_specs=[smem] * 8 + [whole, pl.BlockSpec(memory_space=pl.ANY)]
        + [pl.BlockSpec((1, 2, 256, 256), lambda i: (i, 0, 0, 0))] * 2,
        out_specs=(pl.BlockSpec((16, 64, 128), lambda i: (i, 0, 0)), smem),
        scratch_shapes=[
            pltpu.VMEM((128, 2, 2, 16, 128), BF),
            pltpu.VMEM((128 * 32, 128), F32),
            pltpu.VMEM((8, 256, 256), BF),
            pltpu.VMEM((8, 256, 256), BF),
            pltpu.VMEM((256, 128), F32),
            pltpu.SMEM((128,), I32),
            pltpu.SemaphoreType.DMA((8,)),
        ],
        compiler_params=pltpu.CompilerParams(vmem_limit_bytes=VMEM),
        name="source",
    )(
        tiles, pair, time, chan, count, weights,
        np.array(STEP_A, np.int32), np.array(STEP_B, np.int32),
        pixels, beams, t["b"][0], t["b"][1],
    )


def spread(i):
    o = lax.rem(i * 37, 128)
    row, col = lax.axis_index("row"), lax.axis_index("col")
    x = lax.rem(lax.div(row, 4) + lax.div(o, 32), 4)
    y = lax.rem(lax.rem(row, 4) + lax.rem(lax.div(o, 8), 4), 4)
    z = lax.rem(lax.div(col, 2) + lax.rem(lax.div(o, 2), 4), 4)
    c = lax.rem(col + o, 2)
    return x * 4 + y, z * 2 + c


def exchange_kernel(
    send, tabs, wh, wl, twr, twi, fmat, out, outx,
    recv, tabr, tabt, ghl, pqh, pql, zc, stage, extra, ssem, rsem, lsem
):
    me = lax.axis_index("row") * 8 + lax.axis_index("col")
    first = me < 8
    kind = jnp.where(first, 1, 0)
    barrier = pltpu.get_barrier_semaphore()

    def each(fun):
        def step(i, _):
            row, col = spread(i)
            fun(row * 8 + col, (row, col))
            return 0

        lax.fori_loop(1, 128, step, 0)

    def push(src, dst, k, dev):
        pltpu.make_async_remote_copy(
            src_ref=src, dst_ref=dst, send_sem=ssem.at[k], recv_sem=rsem.at[k],
            device_id=dev, device_id_type=pl.DeviceIdType.MESH,
        ).start()

    def wait(part, sem):
        pltpu.make_async_copy(part, part, sem).wait()

    def keep(src, dst):
        copy = pltpu.make_async_copy(src, dst, lsem)
        copy.start()
        copy.wait()

    each(lambda d, dev: pl.semaphore_signal(
        barrier, inc=1, device_id=dev, device_id_type=pl.DeviceIdType.MESH))
    pl.semaphore_wait(barrier, 127)
    each(lambda d, dev: push(tabs.at[lax.rem(d, 4)], tabr.at[me], 0, dev))
    for rp in range(2):
        rows = pl.ds(rp * 32, 32)
        each(lambda d, dev: push(send.at[d, rows], recv.at[me, rows], 1 + rp, dev))
    keep(tabs.at[lax.rem(me, 4)], tabr.at[me])
    keep(send.at[me], recv.at[me])
    flat = recv.reshape(128 * 64, 128)

    extra[...] = jnp.zeros((1024, 128), F32)
    wait(tabr.at[pl.ds(0, 127)], rsem.at[0])
    tabt[...] = tabr[...].reshape(128, 128).T
    lane = lax.broadcasted_iota(I32, (32, 128), 1)
    low = lane < 64

    def columns(pm, t):
        g = ghl[pm, pl.ds(pl.multiple_of(t * 256, 256), 256), :]
        for c in range(4):
            rows = slice(c * 128, c * 128 + 128)
            a = dot(wh[rows, :], g)
            b = dot(wl[rows, :], g[:, :128])
            u = a[:, :128] + a[:, 128:] + b
            ur, ui = u[:64], u[64:]
            m0 = slice(c * 64, c * 64 + 64)
            tr, ti = twr[m0, :], twi[m0, :]
            pqh[pm, m0, :128], pql[pm, m0, :128] = split(tr * ur - ti * ui)
            pqh[pm, m0, 128:], pql[pm, m0, 128:] = split(tr * ui + ti * ur)

    def mix(which, pm):
        both = fmat[kind, which]
        z = dot_nt(both, pqh[pm])
        return z[:128] + z[128:] + dot_nt(both[:128], pql[pm])

    def emit(dst, size, z, row, pms):
        for pm in pms:
            for tile in range(2):
                lanes = slice(tile * 128, tile * 128 + 128)
                re, im = z[pm * 64:pm * 64 + 32, lanes], z[pm * 64 + 32:pm * 64 + 64, lanes]
                even = jnp.where(low, re, pltpu.roll(im, 64, 1))
                odd = jnp.where(low, pltpu.roll(re, 64, 1), im)
                dst[pl.ds(2 * tile * size + row + pm, 32, stride=4 * size), :] = even
                dst[pl.ds((2 * tile + 1) * size + row + pm, 32, stride=4 * size), :] = odd

    def phase(rp, _):
        rows = pl.ds(pl.multiple_of(rp * 32, 32), 32)
        wait(recv.at[pl.ds(0, 127), rows], rsem.at[1 + rp])
        for pm in range(2):
            def block(c, _, pm=pm):
                at = rp * 32 + pm * 16 + 2 * c
                key = jnp.concatenate([tabt[pl.ds(at + k, 1), :] for k in range(2)], axis=1)
                parts = [split(flat[pl.ds(at + k, 128, stride=64), :]) for k in range(2)]
                rhs = jnp.concatenate([jnp.concatenate(p, axis=1) for p in parts], axis=0)
                for chunk in range(4):
                    tile = lax.broadcasted_iota(I32, (128, 256), 0) + chunk * 128
                    hit = jnp.where(tile == key, 1.0, 0.0).astype(BF)
                    s = dot(hit, rhs)
                    hi, lo = split(s[:, :128] + s[:, 128:])
                    for i in range(4):
                        to = pl.multiple_of((chunk * 4 + i) * 256 + c * 32, 32)
                        ghl[pm, pl.ds(to, 32), :128] = hi[i * 32:i * 32 + 32]
                        ghl[pm, pl.ds(to, 32), 128:] = lo[i * 32:i * 32 + 32]
                return 0

            lax.fori_loop(0, 8, block, 0)
        zc[...] = jnp.zeros((128, 256), F32)

        def row(t, _):
            @pl.when(first & (t > 0))
            def _():
                zc[...] = mix(2, 1)

            columns(0, t)
            columns(1, 15 - t)
            emit(stage, 64, mix(0, 0) + mix(1, 1) + zc[...], rp * 32 + 2 * t, (0, 1))
            return 0

        lax.fori_loop(0, 16, row, 0)

        @pl.when(first)
        def _():
            emit(extra, 8, mix(2, 1), rp, (0,))

        def piece(d):
            return stage.at[pl.ds(pl.multiple_of(d * 64 + rp * 32, 32), 32), :]

        each(lambda d, dev: push(piece(d), out.at[me, rows], 3 + rp, dev))
        keep(piece(me), out.at[me, rows])
        return 0

    lax.fori_loop(0, 2, phase, 0)

    def piece(d):
        return extra.at[pl.ds(pl.multiple_of(d * 8, 8), 8), :]

    @pl.when(first)
    def _():
        each(lambda d, dev: push(piece(d), outx.at[me], 5, dev))
        keep(piece(me), outx.at[me])
        wait(outx.at[pl.ds(0, 7)], rsem.at[5])
        wait(extra.at[pl.ds(0, 127 * 8), :], ssem.at[5])

    @pl.when(me >= 8)
    def _():
        wait(outx, rsem.at[5])

    wait(tabr.at[pl.ds(0, 127)], ssem.at[0])
    for rp in range(2):
        part = recv.at[pl.ds(0, 127), pl.ds(rp * 32, 32)]
        wait(part, ssem.at[1 + rp])
        wait(part, ssem.at[3 + rp])
        wait(out.at[pl.ds(0, 127), pl.ds(rp * 32, 32)], rsem.at[3 + rp])


def exchange(send, tabs):
    t = tables()
    whole = pl.BlockSpec(memory_space=pltpu.VMEM)
    away = pl.BlockSpec(memory_space=pl.ANY)
    return pl.pallas_call(
        exchange_kernel,
        out_shape=(
            jax.ShapeDtypeStruct((128, 64, 128), F32), jax.ShapeDtypeStruct((8, 8, 128), F32)
        ),
        in_specs=[away, whole] + [whole] * 5,
        out_specs=(away, away),
        scratch_shapes=[
            pltpu.VMEM((128, 64, 128), F32),
            pltpu.VMEM((128, 1, 128), I32),
            pltpu.VMEM((128, 128), I32),
            pltpu.VMEM((2, 16 * 256, 256), BF),
            pltpu.VMEM((2, 256, 256), BF),
            pltpu.VMEM((2, 256, 256), BF),
            pltpu.VMEM((128, 256), F32),
            pltpu.VMEM((128 * 64, 128), F32),
            pltpu.VMEM((128 * 8, 128), F32),
            pltpu.SemaphoreType.DMA((6,)),
            pltpu.SemaphoreType.DMA((6,)),
            pltpu.SemaphoreType.DMA,
        ],
        compiler_params=pltpu.CompilerParams(
            vmem_limit_bytes=VMEM, collective_id=0, has_side_effects=True
        ),
        name="exchange",
    )(send, tabs, t["wc"][0], t["wc"][1], t["tw"][0], t["tw"][1], t["f"])


def final_kernel(x, ex, wh, wl, sh, sl, xh, xl, tj, out, val):
    group = pl.program_id(1)

    def three(a, bh, bl):
        ah, al = split(a)
        return dot(ah, bh) + dot(al, bh) + dot(ah, bl)

    a = jnp.concatenate(
        [jnp.concatenate([x[k, 0, q] for q in range(4)], axis=0).T for k in range(4)], axis=0
    )
    u = three(a, wh[...], wl[...])
    for k in range(4):
        v = u[k * 128:k * 128 + 128]
        vr = v[:64, :256] - v[64:, 256:]
        vi = v[:64, 256:] + v[64:, :256]
        tr, ti = tj[k, 0:1, :], tj[k, 1:2, :]
        at = 8 * group + 2 * k
        val[at] = vr * tr - vi * ti
        val[at + 1] = vr * ti + vi * tr

    @pl.when(group == 0)
    def _():
        extra = jnp.concatenate([ex[0, q] for q in range(4)], axis=0)
        extra = jnp.concatenate([extra, jnp.zeros((96, 128), F32)], axis=0).T[:, :32]
        v = three(a[:64], sh[0], sl[0]) + three(a[64:128], sh[1], sl[1])
        v = v + three(extra[:64], xh[0], xl[0]) + three(extra[64:], xh[1], xl[1])
        val[0] = v[:, :256]
        val[1] = v[:, 256:]

    @pl.when(group == 3)
    def _():
        index = {}
        for i, j in enumerate(PAIR_J):
            if i > 0:
                index[j if j < 16 else 32 - j] = (i, 1.0 if j < 16 else -1.0)

        def strip(i, _):
            at = pl.ds(pl.multiple_of(i * 8, 8), 8)
            for tile in range(2):
                lanes = slice(tile * 128, tile * 128 + 128)
                zero, mid = val[0, at, lanes], val[1, at, lanes]
                re = {j: val[2 * k, at, lanes] for j, (k, _) in index.items()}
                im = {j: val[2 * k + 1, at, lanes] for j, (k, _) in index.items()}

                def wave(fun, part, js, l1, signed):
                    total = None
                    for j in js:
                        turn = j * l1 % 32
                        c = fun(2 * math.pi * turn / 32)
                        if signed:
                            c = c * index[j][1]
                        if abs(c) < 1e-12:
                            continue
                        if abs(abs(c) - 1) < 1e-12:
                            term = part[j]
                            if total is None:
                                total = term if c > 0 else -term
                            else:
                                total = total + term if c > 0 else total - term
                        else:
                            term = part[j] * c
                            total = term if total is None else total + term
                    return total if total is not None else jnp.zeros((8, 128), F32)

                odd = range(1, 16, 2)
                ce, se = [None] * 9, [None] * 9
                for l1 in range(5):
                    sign = 1.0 if l1 % 2 == 0 else -1.0
                    ee = wave(math.cos, re, (4, 8, 12), l1, False)
                    ee = ee + (zero + mid if sign > 0 else zero - mid)
                    eo = wave(math.cos, re, (2, 6, 10, 14), l1, False)
                    oe = wave(math.sin, im, (4, 8, 12), l1, True)
                    oo = wave(math.sin, im, (2, 6, 10, 14), l1, True)
                    ce[l1], ce[8 - l1] = ee + eo, ee - eo
                    se[l1], se[8 - l1] = oe + oo, oo - oe
                for l1 in range(9):
                    co = wave(math.cos, re, odd, l1, False)
                    so = wave(math.sin, im, odd, l1, True)
                    p, m = ce[l1] + co, ce[l1] - co
                    s, d = se[l1] + so, se[l1] - so

                    def put(l, value):
                        out[0, at, l * 256 + tile * 128:l * 256 + tile * 128 + 128] = value

                    put(l1, p + s)
                    put(16 + l1, m + d)
                    if l1 > 0:
                        put(32 - l1, p - s)
                        if l1 < 8:
                            put(16 - l1, m - d)
            return 0

        lax.fori_loop(0, 8, strip, 0)


def final(recv, extra):
    t = tables()
    whole = pl.BlockSpec(memory_space=pltpu.VMEM)
    return pl.pallas_call(
        final_kernel,
        grid=(2, 4),
        out_shape=jax.ShapeDtypeStruct((2, 64, 8192), F32),
        in_specs=[
            pl.BlockSpec((4, 1, 4, 64, 128), lambda f, j: (j, f, 0, 0, 0)),
            pl.BlockSpec((1, 4, 8, 128), lambda f, j: (f, 0, 0, 0)),
        ]
        + [whole] * 6
        + [pl.BlockSpec((4, 2, 256), lambda f, j: (j, 0, 0))],
        out_specs=pl.BlockSpec((1, 64, 8192), lambda f, j: (f, 0, 0)),
        scratch_shapes=[pltpu.VMEM((32, 64, 256), F32)],
        compiler_params=pltpu.CompilerParams(vmem_limit_bytes=VMEM),
        name="final",
    )(recv, extra, *t["wr"], *t["ws"], *t["wx"], t["tj"])


def pixel_view(pixels):
    x = pixels.reshape(128, 2, 2, 8, 128).transpose(0, 1, 3, 2, 4)
    return x.reshape(128, 2, 16, 128)


def beam_view(aterms):
    x = aterms.reshape(512, 2, 2, 2, 8, 128).transpose(0, 1, 2, 4, 3, 5)
    return x.reshape(1024, 2, 16, 128)


def local(
    subgrid_pixels, tile_offsets, station_pairs, time_blocks, channel_blocks, valid_counts,
    aterms, channel_weights,
):
    send, table = source(
        tile_offsets.T, station_pairs.T, time_blocks, channel_blocks, valid_counts, channel_weights,
        pixel_view(subgrid_pixels), beam_view(aterms),
    )
    half, extra = exchange(send, table.reshape(4, 1, 128))
    return final(half.reshape(16, 2, 4, 64, 128), extra.reshape(2, 4, 8, 128))


def solution(mesh):
    in_specs = (
        P(("row", "col"), None, None, None),
        P(("row", "col"), None),
        P(("row", "col"), None),
        P(("row", "col")),
        P(("row", "col")),
        P(("row", "col")),
        P(),
        P(),
    )
    out_specs = P(None, ("row", "col"), None)
    return jax.shard_map(local, mesh=mesh, in_specs=in_specs, out_specs=out_specs, check_vma=False)
```

```python
import functools
import math

import jax
import jax.numpy as jnp
import ml_dtypes
import numpy as np
from jax import lax
from jax.experimental import pallas as pl
from jax.experimental.pallas import tpu as pltpu
from jax.sharding import PartitionSpec as P

BF = jnp.bfloat16
F32 = jnp.float32
I32 = jnp.int32

PAIR_J = (0, 8, 4, 12, 1, 9, 17, 25, 2, 10, 18, 26, 3, 11, 19, 27)
VMEM = 56 * 1024 * 1024


def partner(j):
    return 16 if j == 0 else 32 - j


def unit(turns):
    return np.exp(-2j * np.pi * turns)


def split_np(x):
    hi = np.asarray(x, np.float32).astype(ml_dtypes.bfloat16)
    lo = (np.asarray(x, np.float64) - hi.astype(np.float64)).astype(ml_dtypes.bfloat16)
    return hi, lo


def split(x):
    hi = x.astype(BF)
    return hi, (x - hi.astype(F32)).astype(BF)


def dot(a, b):
    return lax.dot_general(a, b, (((1,), (0,)), ((), ())), preferred_element_type=F32)


def dot_nt(a, b):
    return lax.dot_general(a, b, (((1,), (1,)), ((), ())), preferred_element_type=F32)


@functools.lru_cache(None)
def tables():
    xi = np.arange(4)[:, None, None]
    y = np.arange(32)[None, :, None]
    v = np.arange(32)[None, None, :]
    b = np.zeros((8, 2, 2, 4, 32, 2, 2, 2, 32))
    for step in range(8):
        for pair in range(2):
            j = PAIR_J[2 * step + pair]
            for half, jj in enumerate((j, partner(j))):
                w = unit((xi * jj + y * v) % 32 / 32) / 32
                b[step, half, 0, :, :, pair, half, 0] = w.real
                b[step, half, 0, :, :, pair, half, 1] = w.imag
                b[step, half, 1, :, :, pair, half, 0] = -w.imag
                b[step, half, 1, :, :, pair, half, 1] = w.real
    b = b.reshape(8, 2, 256, 256)
    i = np.arange(256)
    w = unit(i[:, None] * i[None, :] % 256 / 256)
    wc = np.stack([w.real.reshape(4, 64, 256), w.imag.reshape(4, 64, 256)], 1).reshape(512, 256)
    tw = unit(i[:, None] * (np.arange(128) % 32)[None, :] / 8192)
    d = unit(np.arange(32)[:, None] * np.arange(32)[None, :] % 32 / 32)
    coef = np.stack([np.stack([d, 1j * d]), np.stack([1j * d, -d])])
    f = np.zeros((2, 3, 2, 2, 32, 2, 2, 2, 32))

    def put(kind, which, half, pm, conj):
        for pq in range(2):
            for reim in range(2):
                c = coef[pq, reim]
                f[kind, which, pm, 0, :, pq, half, reim, :] = c.real
                f[kind, which, pm, 1, :, pq, half, reim, :] = -c.imag if conj else c.imag

    put(0, 0, 0, 0, False)
    put(0, 0, 1, 1, True)
    put(0, 1, 1, 0, True)
    put(0, 1, 0, 1, False)
    put(1, 0, 0, 0, False)
    put(1, 0, 1, 1, False)
    put(1, 1, 1, 1, True)
    put(1, 2, 0, 0, True)
    f = f.reshape(2, 3, 128, 256)
    fh, fl = split_np(f)
    f = np.concatenate([fh, fl], axis=2)
    k = np.arange(256)
    q, rp, t, pm = k // 64, k // 32 % 2, k // 2 % 16, k % 2
    r = 16 * (2 * q + rp) + t
    rr = np.where(pm == 0, r, 255 - r)
    l0 = np.arange(256)
    w = unit(rr[:, None] * l0[None, :] % 256 / 256) / 4096
    wr = np.concatenate([w.real, w.imag], axis=1)
    w0 = np.where((pm == 0)[:, None], unit(r[:, None] * l0[None, :] % 256 / 256), 0) / 4096
    w16 = np.where((pm == 1)[:, None], unit((32 * r[:, None] + 16) * l0[None, :] % 8192 / 8192), 0) / 4096
    ws = np.stack([np.concatenate([w0.real, w16.real], 1), np.concatenate([-w0.imag, -w16.imag], 1)])
    kx = np.arange(32)
    qx, row = kx // 8, kx % 8
    rx = 16 * (15 - (2 * qx + row))
    wx = np.where((row < 2)[:, None], unit(-(rx[:, None] * l0[None, :] % 256) / 256), 0) / 4096
    zero = np.zeros_like(wx.real)
    wx = np.stack([np.concatenate([wx.real, zero], 1), np.concatenate([-wx.imag, zero], 1)])
    tj = unit(np.array(PAIR_J)[:, None] * l0[None, :] / 8192)
    tj = np.stack([tj.real, tj.imag], 1).astype(np.float32)
    return dict(
        b=split_np(b), wc=split_np(wc), tw=(tw.real.astype(np.float32), tw.imag.astype(np.float32)),
        f=f, wr=split_np(wr), ws=split_np(ws), wx=split_np(wx), tj=tj,
    )


def dft8(re, im):
    h = math.sqrt(0.5)

    def four(a, b):
        s0r, s0i = a[0] + a[2], b[0] + b[2]
        s1r, s1i = a[0] - a[2], b[0] - b[2]
        s2r, s2i = a[1] + a[3], b[1] + b[3]
        s3r, s3i = a[1] - a[3], b[1] - b[3]
        return (
            [s0r + s2r, s1r + s3i, s0r - s2r, s1r - s3i],
            [s0i + s2i, s1i - s3r, s0i - s2i, s1i + s3r],
        )

    er, ei = four(re[0::2], im[0::2])
    orr, oi = four(re[1::2], im[1::2])
    tr = [orr[0], (orr[1] + oi[1]) * h, oi[2], (oi[3] - orr[3]) * h]
    ti = [oi[0], (oi[1] - orr[1]) * h, -orr[2], -(oi[3] + orr[3]) * h]
    return (
        [er[k] + tr[k] for k in range(4)] + [er[k] - tr[k] for k in range(4)],
        [ei[k] + ti[k] for k in range(4)] + [ei[k] - ti[k] for k in range(4)],
    )


def place(tiles, count, tabs):
    row, col = tiles[0:1, :], tiles[1:2, :]
    block_row = lax.shift_right_logical(row, 4)
    low = block_row < 8
    near = jnp.where(low, block_row, 15 - block_row)
    block = (near * 2 + jnp.where(low, 0, 1)) * 8 + lax.shift_right_logical(col, 5)
    tile = (row & 15) * 32 + (col & 31)
    down = lax.broadcasted_iota(I32, (128, 128), 0)
    along = lax.broadcasted_iota(I32, (128, 128), 1)

    def column(x):
        return jnp.broadcast_to(x, (128, 128)).T

    earlier = (column(block) == block) & (down < along)
    rank = jnp.sum(jnp.where(earlier, 1.0, 0.0), axis=0, keepdims=True)
    slot = block * 2 + jnp.where(rank > 0.5, 1, 0)
    slot = jnp.where(along[0:1] < count, slot, -1)
    slots, tile = column(slot), column(tile).astype(F32)
    for q in range(4):
        tabs[q] = jnp.sum(jnp.where(slots == along + 64 * q, tile, 0.0), axis=0, keepdims=True).astype(I32)
    hit = jnp.where(lax.broadcasted_iota(I32, (256, 128), 0) == slot, 1.0, 0.0).astype(BF)
    return jnp.concatenate([hit, hit], axis=1)


def spread(i):
    o = lax.rem(i * 37, 128)
    row, col = lax.axis_index("row"), lax.axis_index("col")
    x = lax.rem(lax.div(row, 4) + lax.div(o, 32), 4)
    y = lax.rem(lax.rem(row, 4) + lax.rem(lax.div(o, 8), 4), 4)
    z = lax.rem(lax.div(col, 2) + lax.rem(lax.div(o, 2), 4), 4)
    c = lax.rem(col + o, 2)
    return x * 4 + y, z * 2 + c


def exchange_kernel(
    tiles, pair, time, chan, vc, cw, pixels_hbm, beams_hbm, bh_hbm, bl_hbm,
    wh_hbm, wl_hbm, twr_hbm, twi_hbm, fmat_hbm, out, outx,
    px, beams, bh, bl, wh, wl, twr, twi, fmat,
    corr, lhi, llo, perm, send, tabs,
    recv, tabr, tabt, ghl, pqh, pql, zc, stage, extra, ssem, rsem, lsem, csem
):
    me = lax.axis_index("row") * 8 + lax.axis_index("col")
    first = me < 8
    kind = jnp.where(first, 1, 0)
    barrier = pltpu.get_barrier_semaphore()
    loads = [
        pltpu.make_async_copy(src, dst, csem.at[i])
        for i, (src, dst) in enumerate((
            (beams_hbm, beams), (pixels_hbm, px), (bh_hbm, bh), (bl_hbm, bl), (wh_hbm, wh),
            (wl_hbm, wl), (twr_hbm, twr), (twi_hbm, twi), (fmat_hbm, fmat),
        ))
    ]
    for load in loads:
        load.start()

    def each(fun):
        def step(i, _):
            row, col = spread(i)
            fun(row * 8 + col, (row, col))
            return 0

        lax.fori_loop(1, 128, step, 0)

    def push(src, dst, k, dev):
        pltpu.make_async_remote_copy(
            src_ref=src, dst_ref=dst, send_sem=ssem.at[k], recv_sem=rsem.at[k],
            device_id=dev, device_id_type=pl.DeviceIdType.MESH,
        ).start()

    def wait(part, sem):
        pltpu.make_async_copy(part, part, sem).wait()

    def keep(src, dst):
        copy = pltpu.make_async_copy(src, dst, lsem)
        copy.start()
        copy.wait()

    each(lambda d, dev: pl.semaphore_signal(
        barrier, inc=1, device_id=dev, device_id_type=pl.DeviceIdType.MESH))
    perm[...] = place(tiles, vc[0], tabs)
    loads[0].wait()
    loads[1].wait()

    def correct(s, _):
        weight = jnp.where(s < vc[0], cw[chan[s]], 0.0)
        one = beams[pair[0, s] * 2 + time[s]].astype(F32)
        two = beams[pair[1, s] * 2 + time[s]].astype(F32)
        gr = (one[0] * two[0] + one[1] * two[1]) * weight
        gi = (one[1] * two[0] - one[0] * two[1]) * weight
        pr, pi = px[s, 0], px[s, 1]
        at = pl.multiple_of(s * 32, 32)
        corr[pl.ds(at, 16), :] = pr * gr - pi * gi
        corr[pl.ds(at + 16, 16), :] = pr * gi + pi * gr
        return 0

    lax.fori_loop(0, 128, correct, 0, unroll=4)

    def coarse(group, _):
        for f in range(2):
            base = group * 16 * 32 + f
            re = [corr[pl.ds(base + 2 * p, 16, stride=32), :] for p in range(8)]
            im = [corr[pl.ds(base + 16 + 2 * p, 16, stride=32), :] for p in range(8)]
            re, im = dft8(re, im)
            rows = pl.ds(pl.multiple_of(f * 128 + group * 16, 16), 16)
            for k in range(8):
                lhi[k, rows, :128], llo[k, rows, :128] = split(re[k])
                lhi[k, rows, 128:], llo[k, rows, 128:] = split(im[k])
        return 0

    lax.fori_loop(0, 8, coarse, 0)
    loads[2].wait()
    loads[3].wait()

    def fine(k, _):
        a = jnp.where(k == 0, 0, jnp.where(k == 1, 4, lax.div(k, 2)))
        b = jnp.where(k < 2, a, 8 - a)
        acc = None
        for half, at in enumerate((a, b)):
            h = bh[k, half]
            term = dot(lhi[at], h) + dot(llo[at], h) + dot(lhi[at], bl[k, half])
            acc = term if acc is None else acc + term
        hi, lo = split(acc)
        for f in range(2):
            rows = slice(f * 128, f * 128 + 128)
            padded = dot(perm[...], jnp.concatenate([hi[rows], lo[rows]], axis=0))
            for p in range(2):
                for q in range(4):
                    send[(k * 4 + p * 2 + f) * 4 + q] = (
                        padded[q * 64:(q + 1) * 64, p * 128:(p + 1) * 128]
                    )
        return 0

    lax.fori_loop(0, 8, fine, 0)
    pl.semaphore_wait(barrier, 127)
    each(lambda d, dev: push(tabs.at[lax.rem(d, 4)], tabr.at[me], 0, dev))
    for rp in range(2):
        rows = pl.ds(rp * 32, 32)
        each(lambda d, dev: push(send.at[d, rows], recv.at[me, rows], 1 + rp, dev))
    keep(tabs.at[lax.rem(me, 4)], tabr.at[me])
    keep(send.at[me], recv.at[me])
    flat = recv.reshape(128 * 64, 128)

    extra[...] = jnp.zeros((1024, 128), F32)
    for load in loads[4:]:
        load.wait()
    wait(tabr.at[pl.ds(0, 127)], rsem.at[0])
    tabt[...] = tabr[...].reshape(128, 128).T
    lane = lax.broadcasted_iota(I32, (32, 128), 1)
    low = lane < 64

    def columns(pm, t):
        g = ghl[pm, pl.ds(pl.multiple_of(t * 256, 256), 256), :]
        for c in range(4):
            rows = slice(c * 128, c * 128 + 128)
            a = dot(wh[rows, :], g)
            b = dot(wl[rows, :], g[:, :128])
            u = a[:, :128] + a[:, 128:] + b
            ur, ui = u[:64], u[64:]
            m0 = slice(c * 64, c * 64 + 64)
            tr, ti = twr[m0, :], twi[m0, :]
            pqh[pm, m0, :128], pql[pm, m0, :128] = split(tr * ur - ti * ui)
            pqh[pm, m0, 128:], pql[pm, m0, 128:] = split(tr * ui + ti * ur)

    def mix(which, pm):
        both = fmat[kind, which]
        z = dot_nt(both, pqh[pm])
        return z[:128] + z[128:] + dot_nt(both[:128], pql[pm])

    def emit(dst, size, z, row, pms):
        for pm in pms:
            for tile in range(2):
                lanes = slice(tile * 128, tile * 128 + 128)
                re, im = z[pm * 64:pm * 64 + 32, lanes], z[pm * 64 + 32:pm * 64 + 64, lanes]
                even = jnp.where(low, re, pltpu.roll(im, 64, 1))
                odd = jnp.where(low, pltpu.roll(re, 64, 1), im)
                dst[pl.ds(2 * tile * size + row + pm, 32, stride=4 * size), :] = even
                dst[pl.ds((2 * tile + 1) * size + row + pm, 32, stride=4 * size), :] = odd

    def gather(rp):
        rows = pl.ds(pl.multiple_of(rp * 32, 32), 32)
        wait(recv.at[pl.ds(0, 127), rows], rsem.at[1 + rp])
        for pm in range(2):
            def block(c, _, pm=pm):
                at = rp * 32 + pm * 16 + 2 * c
                key = jnp.concatenate([tabt[pl.ds(at + k, 1), :] for k in range(2)], axis=1)
                parts = [split(flat[pl.ds(at + k, 128, stride=64), :]) for k in range(2)]
                rhs = jnp.concatenate([jnp.concatenate(p, axis=1) for p in parts], axis=0)
                for chunk in range(4):
                    tile = lax.broadcasted_iota(I32, (128, 256), 0) + chunk * 128
                    hit = jnp.where(tile == key, 1.0, 0.0).astype(BF)
                    s = dot(hit, rhs)
                    hi, lo = split(s[:, :128] + s[:, 128:])
                    for i in range(4):
                        to = pl.multiple_of((chunk * 4 + i) * 256 + c * 32, 32)
                        ghl[pm, pl.ds(to, 32), :128] = hi[i * 32:i * 32 + 32]
                        ghl[pm, pl.ds(to, 32), 128:] = lo[i * 32:i * 32 + 32]
                return 0

            lax.fori_loop(0, 8, block, 0)
        zc[...] = jnp.zeros((128, 256), F32)

    def phase(p, _):
        rp, half = lax.div(p, 2), lax.rem(p, 2)

        @pl.when(half == 0)
        def _():
            gather(rp)

        def row(i, _):
            t = half * 8 + i

            @pl.when(first & (t > 0))
            def _():
                zc[...] = mix(2, 1)

            columns(0, t)
            columns(1, 15 - t)
            emit(stage, 64, mix(0, 0) + mix(1, 1) + zc[...], rp * 32 + 2 * t, (0, 1))
            return 0

        lax.fori_loop(0, 8, row, 0)

        @pl.when(first & (half == 1))
        def _():
            emit(extra, 8, mix(2, 1), rp, (0,))

        rows = pl.ds(pl.multiple_of(p * 16, 16), 16)

        def piece(d):
            return stage.at[pl.ds(pl.multiple_of(d * 64 + p * 16, 16), 16), :]

        each(lambda d, dev: push(piece(d), out.at[me, rows], 4 + p, dev))
        keep(piece(me), out.at[me, rows])
        return 0

    lax.fori_loop(0, 4, phase, 0)

    def piece(d):
        return extra.at[pl.ds(pl.multiple_of(d * 8, 8), 8), :]

    @pl.when(first)
    def _():
        each(lambda d, dev: push(piece(d), outx.at[me], 3, dev))
        keep(piece(me), outx.at[me])
        wait(outx.at[pl.ds(0, 7)], rsem.at[3])
        wait(extra.at[pl.ds(0, 127 * 8), :], ssem.at[3])

    @pl.when(me >= 8)
    def _():
        wait(outx, rsem.at[3])

    wait(tabr.at[pl.ds(0, 127)], ssem.at[0])
    for rp in range(2):
        wait(send.at[pl.ds(0, 127), pl.ds(rp * 32, 32)], ssem.at[1 + rp])
    for p in range(4):
        wait(recv.at[pl.ds(0, 127), pl.ds(p * 16, 16)], ssem.at[4 + p])
        wait(out.at[pl.ds(0, 127), pl.ds(p * 16, 16)], rsem.at[4 + p])


def exchange(tiles, pair, time, chan, count, weights, pixels, beams):
    t = tables()
    smem = pl.BlockSpec(memory_space=pltpu.SMEM)
    away = pl.BlockSpec(memory_space=pl.ANY)
    constants = (*t["b"], *t["wc"], *t["tw"], t["f"])
    return pl.pallas_call(
        exchange_kernel,
        out_shape=(
            jax.ShapeDtypeStruct((128, 64, 128), F32), jax.ShapeDtypeStruct((8, 8, 128), F32)
        ),
        in_specs=[pl.BlockSpec(memory_space=pltpu.VMEM)] + [smem] * 5 + [away] * 9,
        out_specs=(away, away),
        scratch_shapes=[
            pltpu.VMEM((128, 2, 16, 128), F32),
            pltpu.VMEM((1024, 2, 16, 128), BF),
            pltpu.VMEM((8, 2, 256, 256), BF),
            pltpu.VMEM((8, 2, 256, 256), BF),
            pltpu.VMEM((512, 256), BF),
            pltpu.VMEM((512, 256), BF),
            pltpu.VMEM((256, 128), F32),
            pltpu.VMEM((256, 128), F32),
            pltpu.VMEM((2, 3, 256, 256), BF),
            pltpu.VMEM((128 * 32, 128), F32),
            pltpu.VMEM((8, 256, 256), BF),
            pltpu.VMEM((8, 256, 256), BF),
            pltpu.VMEM((256, 256), BF),
            pltpu.VMEM((128, 64, 128), F32),
            pltpu.VMEM((4, 1, 128), I32),
            pltpu.VMEM((128, 64, 128), F32),
            pltpu.VMEM((128, 1, 128), I32),
            pltpu.VMEM((128, 128), I32),
            pltpu.VMEM((2, 16 * 256, 256), BF),
            pltpu.VMEM((2, 256, 256), BF),
            pltpu.VMEM((2, 256, 256), BF),
            pltpu.VMEM((128, 256), F32),
            pltpu.VMEM((128 * 64, 128), F32),
            pltpu.VMEM((128 * 8, 128), F32),
            pltpu.SemaphoreType.DMA((8,)),
            pltpu.SemaphoreType.DMA((8,)),
            pltpu.SemaphoreType.DMA,
            pltpu.SemaphoreType.DMA((9,)),
        ],
        compiler_params=pltpu.CompilerParams(
            vmem_limit_bytes=VMEM, collective_id=0, has_side_effects=True
        ),
        name="exchange",
    )(tiles, pair, time, chan, count, weights, pixels, beams, *constants)


def final_kernel(x, ex, wh, wl, sh, sl, xh, xl, tj, out, val):
    group = pl.program_id(1)

    def three(a, bh, bl):
        ah, al = split(a)
        return dot(ah, bh) + dot(al, bh) + dot(ah, bl)

    a = jnp.concatenate(
        [jnp.concatenate([x[k, 0, q] for q in range(4)], axis=0).T for k in range(4)], axis=0
    )
    u = three(a, wh[...], wl[...])
    for k in range(4):
        v = u[k * 128:k * 128 + 128]
        vr = v[:64, :256] - v[64:, 256:]
        vi = v[:64, 256:] + v[64:, :256]
        tr, ti = tj[k, 0:1, :], tj[k, 1:2, :]
        at = 8 * group + 2 * k
        val[at] = vr * tr - vi * ti
        val[at + 1] = vr * ti + vi * tr

    @pl.when(group == 0)
    def _():
        extra = jnp.concatenate([ex[0, q] for q in range(4)], axis=0)
        extra = jnp.concatenate([extra, jnp.zeros((96, 128), F32)], axis=0).T[:, :32]
        v = three(a[:64], sh[0], sl[0]) + three(a[64:128], sh[1], sl[1])
        v = v + three(extra[:64], xh[0], xl[0]) + three(extra[64:], xh[1], xl[1])
        val[0] = v[:, :256]
        val[1] = v[:, 256:]

    @pl.when(group == 3)
    def _():
        index = {}
        for i, j in enumerate(PAIR_J):
            if i > 0:
                index[j if j < 16 else 32 - j] = (i, 1.0 if j < 16 else -1.0)

        def strip(i, _):
            at = pl.ds(pl.multiple_of(i * 8, 8), 8)
            for tile in range(2):
                lanes = slice(tile * 128, tile * 128 + 128)
                zero, mid = val[0, at, lanes], val[1, at, lanes]
                re = {j: val[2 * k, at, lanes] for j, (k, _) in index.items()}
                im = {j: val[2 * k + 1, at, lanes] for j, (k, _) in index.items()}

                def wave(fun, part, js, l1, signed):
                    total = None
                    for j in js:
                        turn = j * l1 % 32
                        c = fun(2 * math.pi * turn / 32)
                        if signed:
                            c = c * index[j][1]
                        if abs(c) < 1e-12:
                            continue
                        if abs(abs(c) - 1) < 1e-12:
                            term = part[j]
                            if total is None:
                                total = term if c > 0 else -term
                            else:
                                total = total + term if c > 0 else total - term
                        else:
                            term = part[j] * c
                            total = term if total is None else total + term
                    return total if total is not None else jnp.zeros((8, 128), F32)

                odd = range(1, 16, 2)
                ce, se = [None] * 9, [None] * 9
                for l1 in range(5):
                    sign = 1.0 if l1 % 2 == 0 else -1.0
                    ee = wave(math.cos, re, (4, 8, 12), l1, False)
                    ee = ee + (zero + mid if sign > 0 else zero - mid)
                    eo = wave(math.cos, re, (2, 6, 10, 14), l1, False)
                    oe = wave(math.sin, im, (4, 8, 12), l1, True)
                    oo = wave(math.sin, im, (2, 6, 10, 14), l1, True)
                    ce[l1], ce[8 - l1] = ee + eo, ee - eo
                    se[l1], se[8 - l1] = oe + oo, oo - oe
                for l1 in range(9):
                    co = wave(math.cos, re, odd, l1, False)
                    so = wave(math.sin, im, odd, l1, True)
                    p, m = ce[l1] + co, ce[l1] - co
                    s, d = se[l1] + so, se[l1] - so

                    def put(l, value):
                        out[0, at, l * 256 + tile * 128:l * 256 + tile * 128 + 128] = value

                    put(l1, p + s)
                    put(16 + l1, m + d)
                    if l1 > 0:
                        put(32 - l1, p - s)
                        if l1 < 8:
                            put(16 - l1, m - d)
            return 0

        lax.fori_loop(0, 8, strip, 0)


def final(recv, extra):
    t = tables()
    whole = pl.BlockSpec(memory_space=pltpu.VMEM)
    return pl.pallas_call(
        final_kernel,
        grid=(2, 4),
        out_shape=jax.ShapeDtypeStruct((2, 64, 8192), F32),
        in_specs=[
            pl.BlockSpec((4, 1, 4, 64, 128), lambda f, j: (j, f, 0, 0, 0)),
            pl.BlockSpec((1, 4, 8, 128), lambda f, j: (f, 0, 0, 0)),
        ]
        + [whole] * 6
        + [pl.BlockSpec((4, 2, 256), lambda f, j: (j, 0, 0))],
        out_specs=pl.BlockSpec((1, 64, 8192), lambda f, j: (f, 0, 0)),
        scratch_shapes=[pltpu.VMEM((32, 64, 256), F32)],
        compiler_params=pltpu.CompilerParams(vmem_limit_bytes=VMEM),
        name="final",
    )(recv, extra, *t["wr"], *t["ws"], *t["wx"], t["tj"])


def pixel_view(pixels):
    x = pixels.reshape(128, 2, 2, 8, 128).transpose(0, 1, 3, 2, 4)
    return x.reshape(128, 2, 16, 128)


def beam_view(aterms):
    x = aterms.reshape(512, 2, 2, 2, 8, 128).transpose(0, 1, 2, 4, 3, 5)
    return x.reshape(1024, 2, 16, 128)


def local(
    subgrid_pixels, tile_offsets, station_pairs, time_blocks, channel_blocks, valid_counts,
    aterms, channel_weights,
):
    half, extra = exchange(
        tile_offsets.T, station_pairs.T, time_blocks, channel_blocks, valid_counts, channel_weights,
        pixel_view(subgrid_pixels), beam_view(aterms),
    )
    return final(half.reshape(16, 2, 4, 64, 128), extra.reshape(2, 4, 8, 128))


def solution(mesh):
    in_specs = (
        P(("row", "col"), None, None, None),
        P(("row", "col"), None),
        P(("row", "col"), None),
        P(("row", "col")),
        P(("row", "col")),
        P(("row", "col")),
        P(),
        P(),
    )
    out_specs = P(None, ("row", "col"), None)
    return jax.shard_map(local, mesh=mesh, in_specs=in_specs, out_specs=out_specs, check_vma=False)
```

```python
import functools
import math

import jax
import jax.numpy as jnp
import ml_dtypes
import numpy as np
from jax import lax
from jax.experimental import pallas as pl
from jax.experimental.pallas import tpu as pltpu
from jax.sharding import PartitionSpec as P

BF = jnp.bfloat16
F32 = jnp.float32
I32 = jnp.int32

PAIR_J = (0, 8, 4, 12, 1, 9, 17, 25, 2, 10, 18, 26, 3, 11, 19, 27)
VMEM = 56 * 1024 * 1024


def partner(j):
    return 16 if j == 0 else 32 - j


def unit(turns):
    return np.exp(-2j * np.pi * turns)


def split_np(x):
    hi = np.asarray(x, np.float32).astype(ml_dtypes.bfloat16)
    lo = (np.asarray(x, np.float64) - hi.astype(np.float64)).astype(ml_dtypes.bfloat16)
    return hi, lo


def split(x):
    hi = x.astype(BF)
    return hi, (x - hi.astype(F32)).astype(BF)


def dot(a, b):
    return lax.dot_general(a, b, (((1,), (0,)), ((), ())), preferred_element_type=F32)


def dot_nt(a, b):
    return lax.dot_general(a, b, (((1,), (1,)), ((), ())), preferred_element_type=F32)


@functools.lru_cache(None)
def tables():
    xi = np.arange(4)[:, None, None]
    y = np.arange(32)[None, :, None]
    v = np.arange(32)[None, None, :]
    b = np.zeros((8, 2, 2, 4, 32, 2, 2, 2, 32))
    for step in range(8):
        for pair in range(2):
            j = PAIR_J[2 * step + pair]
            for half, jj in enumerate((j, partner(j))):
                w = unit((xi * jj + y * v) % 32 / 32) / 32
                b[step, half, 0, :, :, pair, half, 0] = w.real
                b[step, half, 0, :, :, pair, half, 1] = w.imag
                b[step, half, 1, :, :, pair, half, 0] = -w.imag
                b[step, half, 1, :, :, pair, half, 1] = w.real
    b = b.reshape(8, 2, 256, 256)
    i = np.arange(256)
    w = unit(i[:, None] * i[None, :] % 256 / 256)
    wc = np.stack([w.real.reshape(4, 64, 256), w.imag.reshape(4, 64, 256)], 1).reshape(512, 256)
    tw = unit(i[:, None] * (np.arange(128) % 32)[None, :] / 8192)
    d = unit(np.arange(32)[:, None] * np.arange(32)[None, :] % 32 / 32)
    coef = np.stack([np.stack([d, 1j * d]), np.stack([1j * d, -d])])
    f = np.zeros((2, 3, 2, 2, 32, 2, 2, 2, 32))

    def put(kind, which, half, pm, conj):
        for pq in range(2):
            for reim in range(2):
                c = coef[pq, reim]
                f[kind, which, pm, 0, :, pq, half, reim, :] = c.real
                f[kind, which, pm, 1, :, pq, half, reim, :] = -c.imag if conj else c.imag

    put(0, 0, 0, 0, False)
    put(0, 0, 1, 1, True)
    put(0, 1, 1, 0, True)
    put(0, 1, 0, 1, False)
    put(1, 0, 0, 0, False)
    put(1, 0, 1, 1, False)
    put(1, 1, 1, 1, True)
    put(1, 2, 0, 0, True)
    f = f.reshape(2, 3, 128, 256)
    fh, fl = split_np(f)
    f = np.concatenate([fh, fl], axis=2)
    k = np.arange(256)
    q, rp, t, pm = k // 64, k // 32 % 2, k // 2 % 16, k % 2
    r = 16 * (2 * q + rp) + t
    rr = np.where(pm == 0, r, 255 - r)
    l0 = np.arange(256)
    w = unit(rr[:, None] * l0[None, :] % 256 / 256) / 4096
    wr = np.concatenate([w.real, w.imag], axis=1)
    w0 = np.where((pm == 0)[:, None], unit(r[:, None] * l0[None, :] % 256 / 256), 0) / 4096
    w16 = np.where((pm == 1)[:, None], unit((32 * r[:, None] + 16) * l0[None, :] % 8192 / 8192), 0) / 4096
    ws = np.stack([np.concatenate([w0.real, w16.real], 1), np.concatenate([-w0.imag, -w16.imag], 1)])
    kx = np.arange(32)
    qx, row = kx // 8, kx % 8
    rx = 16 * (15 - (2 * qx + row))
    wx = np.where((row < 2)[:, None], unit(-(rx[:, None] * l0[None, :] % 256) / 256), 0) / 4096
    zero = np.zeros_like(wx.real)
    wx = np.stack([np.concatenate([wx.real, zero], 1), np.concatenate([-wx.imag, zero], 1)])
    tj = unit(np.array(PAIR_J)[:, None] * l0[None, :] / 8192)
    tj = np.stack([tj.real, tj.imag], 1).astype(np.float32)
    wr, ws = wr.reshape(4, 2, 32, 512), ws.reshape(2, 4, 2, 32, 512)
    wr = [split_np(wr[:, i].reshape(128, 512)) for i in range(2)]
    ws = [split_np(ws[:, :, i].reshape(2, 128, 512)) for i in range(2)]
    return dict(
        b=split_np(b), wc=split_np(wc), tw=(tw.real.astype(np.float32), tw.imag.astype(np.float32)),
        f=f, wr=wr, ws=ws, wx=split_np(wx), tj=tj,
    )


def dft8(re, im):
    h = math.sqrt(0.5)

    def four(a, b):
        s0r, s0i = a[0] + a[2], b[0] + b[2]
        s1r, s1i = a[0] - a[2], b[0] - b[2]
        s2r, s2i = a[1] + a[3], b[1] + b[3]
        s3r, s3i = a[1] - a[3], b[1] - b[3]
        return (
            [s0r + s2r, s1r + s3i, s0r - s2r, s1r - s3i],
            [s0i + s2i, s1i - s3r, s0i - s2i, s1i + s3r],
        )

    er, ei = four(re[0::2], im[0::2])
    orr, oi = four(re[1::2], im[1::2])
    tr = [orr[0], (orr[1] + oi[1]) * h, oi[2], (oi[3] - orr[3]) * h]
    ti = [oi[0], (oi[1] - orr[1]) * h, -orr[2], -(oi[3] + orr[3]) * h]
    return (
        [er[k] + tr[k] for k in range(4)] + [er[k] - tr[k] for k in range(4)],
        [ei[k] + ti[k] for k in range(4)] + [ei[k] - ti[k] for k in range(4)],
    )


def place(tiles, count, tabs):
    row, col = tiles[0:1, :], tiles[1:2, :]
    block_row = lax.shift_right_logical(row, 4)
    low = block_row < 8
    near = jnp.where(low, block_row, 15 - block_row)
    block = (near * 2 + jnp.where(low, 0, 1)) * 8 + lax.shift_right_logical(col, 5)
    tile = (row & 15) * 32 + (col & 31)
    down = lax.broadcasted_iota(I32, (128, 128), 0)
    along = lax.broadcasted_iota(I32, (128, 128), 1)

    def column(x):
        return jnp.broadcast_to(x, (128, 128)).T

    earlier = (column(block) == block) & (down < along)
    rank = jnp.sum(jnp.where(earlier, 1.0, 0.0), axis=0, keepdims=True)
    slot = block * 2 + jnp.where(rank > 0.5, 1, 0)
    slot = jnp.where(along[0:1] < count, slot, -1)
    slots, tile = column(slot), column(tile).astype(F32)
    for q in range(4):
        tabs[q] = jnp.sum(jnp.where(slots == along + 64 * q, tile, 0.0), axis=0, keepdims=True).astype(I32)
    hit = jnp.where(lax.broadcasted_iota(I32, (256, 128), 0) == slot, 1.0, 0.0).astype(BF)
    return jnp.concatenate([hit, hit], axis=1)


def three(a, b):
    ah, al = split(a)
    return dot(ah, b[0]) + dot(al, b[0]) + dot(ah, b[1])


def halves(re, im):
    return [re[:, :128], re[:, 128:], im[:, :128], im[:, 128:]]


def row_dft(blocks, w, tj, group):
    a = jnp.concatenate([jnp.concatenate(b, axis=0).T for b in blocks], axis=0)
    u = three(a, (w[0][...], w[1][...]))
    outs = []
    for k in range(4):
        v = u[k * 128:k * 128 + 128]
        vr = v[:64, :256] - v[64:, 256:]
        vi = v[:64, 256:] + v[64:, :256]
        tr, ti = tj[4 * group + k, 0:1, :], tj[4 * group + k, 1:2, :]
        outs += halves(vr * tr - vi * ti, vr * ti + vi * tr)
    return outs


def row_dft_zero(block, w):
    a = jnp.concatenate(block, axis=0).T
    v = three(a[:64], (w[0][0], w[1][0])) + three(a[64:], (w[0][1], w[1][1]))
    return halves(v[:, :256], v[:, 256:])


def exchange_kernel(
    tiles, pair, time, chan, vc, cw, pixels_hbm, beams_hbm, bh_hbm, bl_hbm,
    wh_hbm, wl_hbm, twr_hbm, twi_hbm, fmat_hbm,
    wrh_hbm, wrl_hbm, wsh_hbm, wsl_hbm, tj_hbm, out, outx, part,
    px, beams, bh, bl, wh, wl, twr, twi, fmat, wrh, wrl, wsh, wsl, tj,
    corr, lhi, llo, perm, send, tabs,
    recv, tabr, tabt, ghl, pqh, pql, zc, stage, extra, half0, ssem, rsem, lsem, csem
):
    me = lax.axis_index("row") * 8 + lax.axis_index("col")
    first = me < 8
    kind = jnp.where(first, 1, 0)
    barrier = pltpu.get_barrier_semaphore()
    loads = [
        pltpu.make_async_copy(src, dst, csem.at[i])
        for i, (src, dst) in enumerate((
            (beams_hbm, beams), (pixels_hbm, px), (bh_hbm, bh), (bl_hbm, bl), (wh_hbm, wh),
            (wl_hbm, wl), (twr_hbm, twr), (twi_hbm, twi), (fmat_hbm, fmat),
            (wrh_hbm, wrh), (wrl_hbm, wrl), (wsh_hbm, wsh), (wsl_hbm, wsl), (tj_hbm, tj),
        ))
    ]
    for load in loads:
        load.start()
    wr, ws = (wrh, wrl), (wsh, wsl)

    x, y = lax.div(lax.axis_index("row"), 4), lax.rem(lax.axis_index("row"), 4)
    z, core = lax.div(lax.axis_index("col"), 2), lax.rem(lax.axis_index("col"), 2)
    cols = [lax.rem(z + b // 2, 4) * 2 + lax.rem(core + b, 2) for b in range(8)]

    def each(fun):
        def step(a, _):
            def one(b):
                o = lax.rem(a + 5 * b, 16)
                row = lax.rem(x + lax.div(o, 4), 4) * 4 + lax.rem(y + o, 4)
                fun(row * 8 + cols[b], (row, cols[b]))

            for b in (3, 6, 1, 4, 7, 2, 5):
                one(b)

            @pl.when(a > 0)
            def _():
                one(0)

            return 0

        lax.fori_loop(0, 16, step, 0)

    def push(src, dst, k, dev):
        pltpu.make_async_remote_copy(
            src_ref=src, dst_ref=dst, send_sem=ssem.at[k], recv_sem=rsem.at[k],
            device_id=dev, device_id_type=pl.DeviceIdType.MESH,
        ).start()

    def wait(part, sem):
        pltpu.make_async_copy(part, part, sem).wait()

    def keep(src, dst):
        copy = pltpu.make_async_copy(src, dst, lsem)
        copy.start()
        copy.wait()

    each(lambda d, dev: pl.semaphore_signal(
        barrier, inc=1, device_id=dev, device_id_type=pl.DeviceIdType.MESH))
    perm[...] = place(tiles, vc[0], tabs)
    loads[0].wait()
    loads[1].wait()

    def correct(s, _):
        weight = jnp.where(s < vc[0], cw[chan[s]], 0.0)
        one = beams[pair[0, s] * 2 + time[s]].astype(F32)
        two = beams[pair[1, s] * 2 + time[s]].astype(F32)
        gr = (one[0] * two[0] + one[1] * two[1]) * weight
        gi = (one[1] * two[0] - one[0] * two[1]) * weight
        pr, pi = px[s, 0], px[s, 1]
        at = pl.multiple_of(s * 32, 32)
        corr[pl.ds(at, 16), :] = pr * gr - pi * gi
        corr[pl.ds(at + 16, 16), :] = pr * gi + pi * gr
        return 0

    lax.fori_loop(0, 128, correct, 0, unroll=4)

    def coarse(group, _):
        for f in range(2):
            base = group * 16 * 32 + f
            re = [corr[pl.ds(base + 2 * p, 16, stride=32), :] for p in range(8)]
            im = [corr[pl.ds(base + 16 + 2 * p, 16, stride=32), :] for p in range(8)]
            re, im = dft8(re, im)
            rows = pl.ds(pl.multiple_of(f * 128 + group * 16, 16), 16)
            for k in range(8):
                lhi[k, rows, :128], llo[k, rows, :128] = split(re[k])
                lhi[k, rows, 128:], llo[k, rows, 128:] = split(im[k])
        return 0

    lax.fori_loop(0, 8, coarse, 0)
    loads[2].wait()
    loads[3].wait()

    pl.semaphore_wait(barrier, 127)
    early, late = pl.ds(0, 32), pl.ds(32, 32)

    def fine(i, _):
        k = lax.rem(i + lax.div(me, 16), 8)
        a = jnp.where(k == 0, 0, jnp.where(k == 1, 4, lax.div(k, 2)))
        b = jnp.where(k < 2, a, 8 - a)
        acc = None
        for half, at in enumerate((a, b)):
            h = bh[k, half]
            term = dot(lhi[at], h) + dot(llo[at], h) + dot(lhi[at], bl[k, half])
            acc = term if acc is None else acc + term
        hi, lo = split(acc)
        for f in range(2):
            rows = slice(f * 128, f * 128 + 128)
            padded = dot(perm[...], jnp.concatenate([hi[rows], lo[rows]], axis=0))
            for p in range(2):
                for q in range(4):
                    send[(k * 4 + p * 2 + f) * 4 + q] = (
                        padded[q * 64:(q + 1) * 64, p * 128:(p + 1) * 128]
                    )
        for n in range(16):
            row, col = 2 * k + n % 2, n * 3 // 2 % 8
            d = row * 8 + col

            @pl.when(d != me)
            def _(d=d, dev=(row, jnp.int32(col))):
                push(send.at[d, early], recv.at[me, early], 1, dev)

        return 0

    lax.fori_loop(0, 8, fine, 0)
    each(lambda d, dev: push(tabs.at[lax.rem(d, 4)], tabr.at[me], 0, dev))
    each(lambda d, dev: push(send.at[d, late], recv.at[me, late], 2, dev))
    keep(tabs.at[lax.rem(me, 4)], tabr.at[me])
    keep(send.at[me], recv.at[me])
    flat = recv.reshape(128 * 64, 128)

    extra[...] = jnp.zeros((1024, 128), F32)
    for load in loads[4:9]:
        load.wait()
    wait(tabr.at[pl.ds(0, 127)], rsem.at[0])
    tabt[...] = tabr[...].reshape(128, 128).T
    lane = lax.broadcasted_iota(I32, (32, 128), 1)
    low = lane < 64

    def columns(pm, t):
        g = ghl[pm, pl.ds(pl.multiple_of(t * 256, 256), 256), :]
        for c in range(4):
            rows = slice(c * 128, c * 128 + 128)
            a = dot(wh[rows, :], g)
            b = dot(wl[rows, :], g[:, :128])
            u = a[:, :128] + a[:, 128:] + b
            ur, ui = u[:64], u[64:]
            m0 = slice(c * 64, c * 64 + 64)
            tr, ti = twr[m0, :], twi[m0, :]
            pqh[pm, m0, :128], pql[pm, m0, :128] = split(tr * ur - ti * ui)
            pqh[pm, m0, 128:], pql[pm, m0, 128:] = split(tr * ui + ti * ur)

    def mix(which, pm):
        both = fmat[kind, which]
        z = dot_nt(both, pqh[pm])
        return z[:128] + z[128:] + dot_nt(both[:128], pql[pm])

    def emit(dst, size, z, row, pms):
        for pm in pms:
            for tile in range(2):
                lanes = slice(tile * 128, tile * 128 + 128)
                re, im = z[pm * 64:pm * 64 + 32, lanes], z[pm * 64 + 32:pm * 64 + 64, lanes]
                even = jnp.where(low, re, pltpu.roll(im, 64, 1))
                odd = jnp.where(low, pltpu.roll(re, 64, 1), im)
                dst[pl.ds(2 * tile * size + row + pm, 32, stride=4 * size), :] = even
                dst[pl.ds((2 * tile + 1) * size + row + pm, 32, stride=4 * size), :] = odd

    def gather(rp):
        for pm in range(2):
            def block(c, _, pm=pm):
                at = rp * 32 + pm * 16 + 2 * c
                key = jnp.concatenate([tabt[pl.ds(at + k, 1), :] for k in range(2)], axis=1)
                parts = [split(flat[pl.ds(at + k, 128, stride=64), :]) for k in range(2)]
                rhs = jnp.concatenate([jnp.concatenate(p, axis=1) for p in parts], axis=0)
                for chunk in range(4):
                    tile = lax.broadcasted_iota(I32, (128, 256), 0) + chunk * 128
                    hit = jnp.where(tile == key, 1.0, 0.0).astype(BF)
                    s = dot(hit, rhs)
                    hi, lo = split(s[:, :128] + s[:, 128:])
                    for i in range(4):
                        to = pl.multiple_of((chunk * 4 + i) * 256 + c * 32, 32)
                        ghl[pm, pl.ds(to, 32), :128] = hi[i * 32:i * 32 + 32]
                        ghl[pm, pl.ds(to, 32), 128:] = lo[i * 32:i * 32 + 32]
                return 0

            lax.fori_loop(0, 8, block, 0)
        zc[...] = jnp.zeros((128, 256), F32)

    def phase(p, _):
        rp, half = lax.div(p, 2), lax.rem(p, 2)

        @pl.when(half == 0)
        def _():
            gather(rp)

        def row(i, _):
            t = half * 8 + i

            @pl.when(first & (t > 0))
            def _():
                zc[...] = mix(2, 1)

            columns(0, t)
            columns(1, 15 - t)
            emit(stage, 64, mix(0, 0) + mix(1, 1) + zc[...], rp * 32 + 2 * t, (0, 1))
            return 0

        lax.fori_loop(0, 8, row, 0)

        @pl.when(first & (half == 1))
        def _():
            emit(extra, 8, mix(2, 1), rp, (0,))

        @pl.when(p == 1)
        def _():
            def piece(d):
                return stage.at[pl.ds(pl.multiple_of(d * 64, 64), 32), :]

            wait(recv.at[pl.ds(0, 127), late], rsem.at[2])
            each(lambda d, dev: push(piece(d), half0.at[me], 4, dev))
            keep(piece(me), half0.at[me])

        @pl.when(p > 1)
        def _():
            rows = pl.ds(pl.multiple_of(half * 16, 16), 16)

            def piece(d):
                return stage.at[pl.ds(pl.multiple_of(d * 64 + p * 16, 16), 16), :]

            each(lambda d, dev: push(piece(d), out.at[me, rows], 3 + p, dev))
            keep(piece(me), out.at[me, rows])

        return 0

    wait(recv.at[pl.ds(0, 127), early], rsem.at[1])
    lax.fori_loop(0, 4, phase, 0)

    def piece(d):
        return extra.at[pl.ds(pl.multiple_of(d * 8, 8), 8), :]

    @pl.when(first)
    def _():
        each(lambda d, dev: push(piece(d), outx.at[me], 3, dev))
        keep(piece(me), outx.at[me])
        wait(outx.at[pl.ds(0, 7)], rsem.at[3])
        wait(extra.at[pl.ds(0, 127 * 8), :], ssem.at[3])

    @pl.when(me >= 8)
    def _():
        wait(outx, rsem.at[3])

    wait(send.at[pl.ds(0, 127), early], ssem.at[1])
    wait(send.at[pl.ds(0, 127), late], ssem.at[2])
    for load in loads[9:]:
        load.wait()
    wait(half0.at[pl.ds(0, 127)], rsem.at[4])

    def transform(n, _):
        f, group = lax.div(n, 4), lax.rem(n, 4)
        turned = row_dft(
            [[half0[((4 * group + k) * 2 + f) * 4 + q] for q in range(4)] for k in range(4)],
            wr, tj, group,
        )
        for k in range(16):
            send[n * 16 + k] = turned[k]

        @pl.when(group == 0)
        def _():
            for k, v in enumerate(row_dft_zero([half0[f * 4 + q] for q in range(4)], ws)):
                send[n * 16 + k] = v

        pltpu.make_async_copy(
            send.at[pl.ds(n * 16, 16)], part.at[pl.ds(n * 16, 16)], lsem
        ).start()
        return 0

    lax.fori_loop(0, 8, transform, 0)
    wait(part, lsem)
    wait(tabr.at[pl.ds(0, 127)], ssem.at[0])
    wait(half0.at[pl.ds(0, 127)], ssem.at[4])
    for p in range(2):
        wait(out.at[pl.ds(0, 127), pl.ds(p * 16, 16)], rsem.at[5 + p])
        wait(recv.at[pl.ds(0, 127), pl.ds(p * 16, 16)], ssem.at[5 + p])


def exchange(tiles, pair, time, chan, count, weights, pixels, beams):
    t = tables()
    smem = pl.BlockSpec(memory_space=pltpu.SMEM)
    away = pl.BlockSpec(memory_space=pl.ANY)
    constants = (*t["b"], *t["wc"], *t["tw"], t["f"], *t["wr"][0], *t["ws"][0], t["tj"])
    return pl.pallas_call(
        exchange_kernel,
        out_shape=(
            jax.ShapeDtypeStruct((128, 32, 128), F32), jax.ShapeDtypeStruct((8, 8, 128), F32),
            jax.ShapeDtypeStruct((128, 64, 128), F32),
        ),
        in_specs=[pl.BlockSpec(memory_space=pltpu.VMEM)] + [smem] * 5 + [away] * 14,
        out_specs=(away, away, away),
        scratch_shapes=[
            pltpu.VMEM((128, 2, 16, 128), F32),
            pltpu.VMEM((1024, 2, 16, 128), BF),
            pltpu.VMEM((8, 2, 256, 256), BF),
            pltpu.VMEM((8, 2, 256, 256), BF),
            pltpu.VMEM((512, 256), BF),
            pltpu.VMEM((512, 256), BF),
            pltpu.VMEM((256, 128), F32),
            pltpu.VMEM((256, 128), F32),
            pltpu.VMEM((2, 3, 256, 256), BF),
            pltpu.VMEM((128, 512), BF),
            pltpu.VMEM((128, 512), BF),
            pltpu.VMEM((2, 128, 512), BF),
            pltpu.VMEM((2, 128, 512), BF),
            pltpu.VMEM((16, 2, 256), F32),
            pltpu.VMEM((128 * 32, 128), F32),
            pltpu.VMEM((8, 256, 256), BF),
            pltpu.VMEM((8, 256, 256), BF),
            pltpu.VMEM((256, 256), BF),
            pltpu.VMEM((128, 64, 128), F32),
            pltpu.VMEM((4, 1, 128), I32),
            pltpu.VMEM((128, 64, 128), F32),
            pltpu.VMEM((128, 1, 128), I32),
            pltpu.VMEM((128, 128), I32),
            pltpu.VMEM((2, 16 * 256, 256), BF),
            pltpu.VMEM((2, 256, 256), BF),
            pltpu.VMEM((2, 256, 256), BF),
            pltpu.VMEM((128, 256), F32),
            pltpu.VMEM((128 * 64, 128), F32),
            pltpu.VMEM((128 * 8, 128), F32),
            pltpu.VMEM((128, 32, 128), F32),
            pltpu.SemaphoreType.DMA((8,)),
            pltpu.SemaphoreType.DMA((8,)),
            pltpu.SemaphoreType.DMA,
            pltpu.SemaphoreType.DMA((14,)),
        ],
        compiler_params=pltpu.CompilerParams(
            vmem_limit_bytes=VMEM, collective_id=0, has_side_effects=True
        ),
        name="exchange",
    )(tiles, pair, time, chan, count, weights, pixels, beams, *constants)


def final_kernel(x, ex, part, wh, wl, sh, sl, xh, xl, tj, out, val):
    group = pl.program_id(1)
    turned = row_dft([[x[k, 0, q] for q in range(4)] for k in range(4)], (wh, wl), tj, group)
    for k in range(16):
        val[16 * group + k] = turned[k] + part[k]

    @pl.when(group == 0)
    def _():
        extra = jnp.concatenate([ex[0, q] for q in range(4)], axis=0)
        extra = jnp.concatenate([extra, jnp.zeros((96, 128), F32)], axis=0).T[:, :32]
        v = three(extra[:64], (xh[0], xl[0])) + three(extra[64:], (xh[1], xl[1]))
        more = halves(v[:, :256], v[:, 256:])
        for k, v in enumerate(row_dft_zero([x[0, 0, q] for q in range(4)], (sh, sl))):
            val[k] = v + part[k] + more[k]

    @pl.when(group == 3)
    def _():
        index = {}
        for i, j in enumerate(PAIR_J):
            if i > 0:
                index[j if j < 16 else 32 - j] = (i, 1.0 if j < 16 else -1.0)

        def strip(i, _):
            at = pl.ds(pl.multiple_of(i * 8, 8), 8)
            for tile in range(2):
                zero, mid = val[tile, at, :], val[2 + tile, at, :]
                re = {j: val[4 * k + tile, at, :] for j, (k, _) in index.items()}
                im = {j: val[4 * k + 2 + tile, at, :] for j, (k, _) in index.items()}

                def wave(fun, part, js, l1, signed):
                    total = None
                    for j in js:
                        turn = j * l1 % 32
                        c = fun(2 * math.pi * turn / 32)
                        if signed:
                            c = c * index[j][1]
                        if abs(c) < 1e-12:
                            continue
                        if abs(abs(c) - 1) < 1e-12:
                            term = part[j]
                            if total is None:
                                total = term if c > 0 else -term
                            else:
                                total = total + term if c > 0 else total - term
                        else:
                            term = part[j] * c
                            total = term if total is None else total + term
                    return total if total is not None else jnp.zeros((8, 128), F32)

                odd = range(1, 16, 2)
                ce, se = [None] * 9, [None] * 9
                for l1 in range(5):
                    sign = 1.0 if l1 % 2 == 0 else -1.0
                    ee = wave(math.cos, re, (4, 8, 12), l1, False)
                    ee = ee + (zero + mid if sign > 0 else zero - mid)
                    eo = wave(math.cos, re, (2, 6, 10, 14), l1, False)
                    oe = wave(math.sin, im, (4, 8, 12), l1, True)
                    oo = wave(math.sin, im, (2, 6, 10, 14), l1, True)
                    ce[l1], ce[8 - l1] = ee + eo, ee - eo
                    se[l1], se[8 - l1] = oe + oo, oo - oe
                for l1 in range(9):
                    co = wave(math.cos, re, odd, l1, False)
                    so = wave(math.sin, im, odd, l1, True)
                    p, m = ce[l1] + co, ce[l1] - co
                    s, d = se[l1] + so, se[l1] - so

                    def put(l, value):
                        out[0, at, l * 256 + tile * 128:l * 256 + tile * 128 + 128] = value

                    put(l1, p + s)
                    put(16 + l1, m + d)
                    if l1 > 0:
                        put(32 - l1, p - s)
                        if l1 < 8:
                            put(16 - l1, m - d)
            return 0

        lax.fori_loop(0, 8, strip, 0)


def final(recv, extra, part):
    t = tables()
    whole = pl.BlockSpec(memory_space=pltpu.VMEM)
    return pl.pallas_call(
        final_kernel,
        grid=(2, 4),
        out_shape=jax.ShapeDtypeStruct((2, 64, 8192), F32),
        in_specs=[
            pl.BlockSpec((4, 1, 4, 32, 128), lambda f, j: (j, f, 0, 0, 0)),
            pl.BlockSpec((1, 4, 8, 128), lambda f, j: (f, 0, 0, 0)),
            pl.BlockSpec((16, 64, 128), lambda f, j: (f * 4 + j, 0, 0)),
        ]
        + [whole] * 7,
        out_specs=pl.BlockSpec((1, 64, 8192), lambda f, j: (f, 0, 0)),
        scratch_shapes=[pltpu.VMEM((64, 64, 128), F32)],
        compiler_params=pltpu.CompilerParams(vmem_limit_bytes=VMEM),
        name="final",
    )(recv, extra, part, *t["wr"][1], *t["ws"][1], *t["wx"], t["tj"])


def pixel_view(pixels):
    x = pixels.reshape(128, 2, 2, 8, 128).transpose(0, 1, 3, 2, 4)
    return x.reshape(128, 2, 16, 128)


def beam_view(aterms):
    x = aterms.reshape(512, 2, 2, 2, 8, 128).transpose(0, 1, 2, 4, 3, 5)
    return x.reshape(1024, 2, 16, 128)


def local(
    subgrid_pixels, tile_offsets, station_pairs, time_blocks, channel_blocks, valid_counts,
    aterms, channel_weights,
):
    half, extra, part = exchange(
        tile_offsets.T, station_pairs.T, time_blocks, channel_blocks, valid_counts, channel_weights,
        pixel_view(subgrid_pixels), beam_view(aterms),
    )
    return final(half.reshape(16, 2, 4, 32, 128), extra.reshape(2, 4, 8, 128), part)


def solution(mesh):
    in_specs = (
        P(("row", "col"), None, None, None),
        P(("row", "col"), None),
        P(("row", "col"), None),
        P(("row", "col")),
        P(("row", "col")),
        P(("row", "col")),
        P(),
        P(),
    )
    out_specs = P(None, ("row", "col"), None)
    return jax.shard_map(local, mesh=mesh, in_specs=in_specs, out_specs=out_specs, check_vma=False)
```

```python
import functools
import math

import jax
import jax.numpy as jnp
import ml_dtypes
import numpy as np
from jax import lax
from jax.experimental import pallas as pl
from jax.experimental.pallas import tpu as pltpu
from jax.sharding import PartitionSpec as P

BF = jnp.bfloat16
F32 = jnp.float32
I32 = jnp.int32

PAIR_J = (0, 8, 4, 12, 1, 9, 17, 25, 2, 10, 18, 26, 3, 11, 19, 27)
VMEM = 56 * 1024 * 1024


def partner(j):
    return 16 if j == 0 else 32 - j


def unit(turns):
    return np.exp(-2j * np.pi * turns)


def split_np(x):
    hi = np.asarray(x, np.float32).astype(ml_dtypes.bfloat16)
    lo = (np.asarray(x, np.float64) - hi.astype(np.float64)).astype(ml_dtypes.bfloat16)
    return hi, lo


def split(x):
    hi = x.astype(BF)
    return hi, (x - hi.astype(F32)).astype(BF)


def dot(a, b):
    return lax.dot_general(a, b, (((1,), (0,)), ((), ())), preferred_element_type=F32)


def dot_nt(a, b):
    return lax.dot_general(a, b, (((1,), (1,)), ((), ())), preferred_element_type=F32)


@functools.lru_cache(None)
def tables():
    xi = np.arange(4)[:, None, None]
    y = np.arange(32)[None, :, None]
    v = np.arange(32)[None, None, :]
    b = np.zeros((8, 2, 2, 4, 32, 2, 2, 2, 32))
    for step in range(8):
        for pair in range(2):
            j = PAIR_J[2 * step + pair]
            for half, jj in enumerate((j, partner(j))):
                w = unit((xi * jj + y * v) % 32 / 32) / 32
                b[step, half, 0, :, :, pair, half, 0] = w.real
                b[step, half, 0, :, :, pair, half, 1] = w.imag
                b[step, half, 1, :, :, pair, half, 0] = -w.imag
                b[step, half, 1, :, :, pair, half, 1] = w.real
    b = b.reshape(8, 2, 256, 256)
    i = np.arange(256)
    w = unit(i[:, None] * i[None, :] % 256 / 256)
    wc = np.stack([w.real.reshape(4, 64, 256), w.imag.reshape(4, 64, 256)], 1).reshape(512, 256)
    tw = unit(i[:, None] * (np.arange(128) % 32)[None, :] / 8192)
    d = unit(np.arange(32)[:, None] * np.arange(32)[None, :] % 32 / 32)
    coef = np.stack([np.stack([d, 1j * d]), np.stack([1j * d, -d])])
    f = np.zeros((2, 3, 2, 2, 32, 2, 2, 2, 32))

    def put(kind, which, half, pm, conj):
        for pq in range(2):
            for reim in range(2):
                c = coef[pq, reim]
                f[kind, which, pm, 0, :, pq, half, reim, :] = c.real
                f[kind, which, pm, 1, :, pq, half, reim, :] = -c.imag if conj else c.imag

    put(0, 0, 0, 0, False)
    put(0, 0, 1, 1, True)
    put(0, 1, 1, 0, True)
    put(0, 1, 0, 1, False)
    put(1, 0, 0, 0, False)
    put(1, 0, 1, 1, False)
    put(1, 1, 1, 1, True)
    put(1, 2, 0, 0, True)
    f = f.reshape(2, 3, 128, 256)
    fh, fl = split_np(f)
    f = np.concatenate([fh, fl], axis=2)
    k = np.arange(256)
    q, rp, t, pm = k // 64, k // 32 % 2, k // 2 % 16, k % 2
    r = 16 * (2 * q + rp) + t
    rr = np.where(pm == 0, r, 255 - r)
    l0 = np.arange(256)
    w = unit(rr[:, None] * l0[None, :] % 256 / 256) / 4096
    wr = np.concatenate([w.real, w.imag], axis=1)
    w0 = np.where((pm == 0)[:, None], unit(r[:, None] * l0[None, :] % 256 / 256), 0) / 4096
    w16 = np.where((pm == 1)[:, None], unit((32 * r[:, None] + 16) * l0[None, :] % 8192 / 8192), 0) / 4096
    ws = np.stack([np.concatenate([w0.real, w16.real], 1), np.concatenate([-w0.imag, -w16.imag], 1)])
    kx = np.arange(32)
    qx, row = kx // 8, kx % 8
    rx = 16 * (15 - (2 * qx + row))
    wx = np.where((row < 2)[:, None], unit(-(rx[:, None] * l0[None, :] % 256) / 256), 0) / 4096
    zero = np.zeros_like(wx.real)
    wx = np.stack([np.concatenate([wx.real, zero], 1), np.concatenate([-wx.imag, zero], 1)])
    tj = unit(np.array(PAIR_J)[:, None] * l0[None, :] / 8192)
    tj = np.stack([tj.real, tj.imag], 1).astype(np.float32)
    wr, ws = wr.reshape(4, 2, 32, 512), ws.reshape(2, 4, 2, 32, 512)
    wr = split_np(wr.transpose(1, 0, 2, 3).reshape(2, 128, 512))
    ws = split_np(ws.transpose(2, 0, 1, 3, 4).reshape(2, 2, 128, 512))
    return dict(
        b=split_np(b), wc=split_np(wc), tw=(tw.real.astype(np.float32), tw.imag.astype(np.float32)),
        f=f, wr=wr, ws=ws, wx=split_np(wx), tj=tj,
    )


def dft8(re, im):
    h = math.sqrt(0.5)

    def four(a, b):
        s0r, s0i = a[0] + a[2], b[0] + b[2]
        s1r, s1i = a[0] - a[2], b[0] - b[2]
        s2r, s2i = a[1] + a[3], b[1] + b[3]
        s3r, s3i = a[1] - a[3], b[1] - b[3]
        return (
            [s0r + s2r, s1r + s3i, s0r - s2r, s1r - s3i],
            [s0i + s2i, s1i - s3r, s0i - s2i, s1i + s3r],
        )

    er, ei = four(re[0::2], im[0::2])
    orr, oi = four(re[1::2], im[1::2])
    tr = [orr[0], (orr[1] + oi[1]) * h, oi[2], (oi[3] - orr[3]) * h]
    ti = [oi[0], (oi[1] - orr[1]) * h, -orr[2], -(oi[3] + orr[3]) * h]
    return (
        [er[k] + tr[k] for k in range(4)] + [er[k] - tr[k] for k in range(4)],
        [ei[k] + ti[k] for k in range(4)] + [ei[k] - ti[k] for k in range(4)],
    )


def place(tiles, count, tabs):
    row, col = tiles[0:1, :], tiles[1:2, :]
    block_row = lax.shift_right_logical(row, 4)
    low = block_row < 8
    near = jnp.where(low, block_row, 15 - block_row)
    block = (near * 2 + jnp.where(low, 0, 1)) * 8 + lax.shift_right_logical(col, 5)
    tile = (row & 15) * 32 + (col & 31)
    down = lax.broadcasted_iota(I32, (128, 128), 0)
    along = lax.broadcasted_iota(I32, (128, 128), 1)

    def column(x):
        return jnp.broadcast_to(x, (128, 128)).T

    earlier = (column(block) == block) & (down < along)
    rank = jnp.sum(jnp.where(earlier, 1.0, 0.0), axis=0, keepdims=True)
    slot = block * 2 + jnp.where(rank > 0.5, 1, 0)
    slot = jnp.where(along[0:1] < count, slot, -1)
    slots, tile = column(slot), column(tile).astype(F32)
    for q in range(4):
        tabs[q] = jnp.sum(jnp.where(slots == along + 64 * q, tile, 0.0), axis=0, keepdims=True).astype(I32)
    hit = jnp.where(lax.broadcasted_iota(I32, (256, 128), 0) == slot, 1.0, 0.0).astype(BF)
    return jnp.concatenate([hit, hit], axis=1)


def three(a, b):
    ah, al = split(a)
    return dot(ah, b[0]) + dot(al, b[0]) + dot(ah, b[1])


def halves(re, im):
    return [re[:, :128], re[:, 128:], im[:, :128], im[:, 128:]]


def row_dft(blocks, w, tj, group):
    a = jnp.concatenate([jnp.concatenate(b, axis=0).T for b in blocks], axis=0)
    u = three(a, (w[0][...], w[1][...]))
    outs = []
    for k in range(4):
        v = u[k * 128:k * 128 + 128]
        vr = v[:64, :256] - v[64:, 256:]
        vi = v[:64, 256:] + v[64:, :256]
        tr, ti = tj[4 * group + k, 0:1, :], tj[4 * group + k, 1:2, :]
        outs += halves(vr * tr - vi * ti, vr * ti + vi * tr)
    return outs


def row_dft_zero(block, w):
    a = jnp.concatenate(block, axis=0).T
    v = three(a[:64], (w[0][0], w[1][0])) + three(a[64:], (w[0][1], w[1][1]))
    return halves(v[:, :256], v[:, 256:])


def mix_pairs(load):
    index = {}
    for i, j in enumerate(PAIR_J):
        if i > 0:
            index[j if j < 16 else 32 - j] = (i, 1.0 if j < 16 else -1.0)
    zero, mid = load(0, 0), load(0, 1)
    re = {j: load(k, 0) for j, (k, _) in index.items()}
    im = {j: load(k, 1) for j, (k, _) in index.items()}

    def wave(fun, part, js, l1, signed):
        total = jnp.zeros((8, 128), F32)
        started = False
        for j in js:
            c = fun(2 * math.pi * (j * l1 % 32) / 32) * (index[j][1] if signed else 1.0)
            if abs(c) < 1e-12:
                continue
            term = part[j] if abs(abs(c) - 1) < 1e-12 else part[j] * abs(c)
            if started:
                total = total + term if c > 0 else total - term
            else:
                total = term if c > 0 else -term
            started = True
        return total

    odd, even, four = range(1, 16, 2), (2, 6, 10, 14), (4, 8, 12)
    ce, se = [None] * 9, [None] * 9
    for l1 in range(5):
        ee = wave(math.cos, re, four, l1, False) + (zero + mid if l1 % 2 == 0 else zero - mid)
        eo = wave(math.cos, re, even, l1, False)
        oe = wave(math.sin, im, four, l1, True)
        oo = wave(math.sin, im, even, l1, True)
        ce[l1], ce[8 - l1] = ee + eo, ee - eo
        se[l1], se[8 - l1] = oe + oo, oo - oe
    outs = []
    for l1 in range(9):
        co = wave(math.cos, re, odd, l1, False)
        so = wave(math.sin, im, odd, l1, True)
        p, m = ce[l1] + co, ce[l1] - co
        s, d = se[l1] + so, se[l1] - so
        outs += [(l1, p + s), (16 + l1, m + d)]
        if l1 > 0:
            outs.append((32 - l1, p - s))
            if l1 < 8:
                outs.append((16 - l1, m - d))
    return outs


def exchange_kernel(
    tiles, pair, time, chan, vc, cw, pixels_hbm, beams_hbm, bh_hbm, bl_hbm,
    wh_hbm, wl_hbm, twr_hbm, twi_hbm, fmat_hbm,
    wrh_hbm, wrl_hbm, wsh_hbm, wsl_hbm, xh_hbm, xl_hbm, tj_hbm, out,
    px, beams, bh, bl, wh, wl, twr, twi, fmat, wrh, wrl, wsh, wsl, xh, xl, tj,
    corr, lhi, llo, perm, send, tabs,
    recv, tabr, tabt, ghl, pqh, pql, zc, stage, extra, got, gotx, image, ssem, rsem, lsem, csem
):
    me = lax.axis_index("row") * 8 + lax.axis_index("col")
    first = me < 8
    kind = jnp.where(first, 1, 0)
    barrier = pltpu.get_barrier_semaphore()
    loads = [
        pltpu.make_async_copy(src, dst, csem.at[i])
        for i, (src, dst) in enumerate((
            (beams_hbm, beams), (pixels_hbm, px), (bh_hbm, bh), (bl_hbm, bl), (wh_hbm, wh),
            (wl_hbm, wl), (twr_hbm, twr), (twi_hbm, twi), (fmat_hbm, fmat),
            (wrh_hbm, wrh), (wrl_hbm, wrl), (wsh_hbm, wsh), (wsl_hbm, wsl),
            (xh_hbm, xh), (xl_hbm, xl), (tj_hbm, tj),
        ))
    ]
    for load in loads:
        load.start()

    x, y = lax.div(lax.axis_index("row"), 4), lax.rem(lax.axis_index("row"), 4)
    z, core = lax.div(lax.axis_index("col"), 2), lax.rem(lax.axis_index("col"), 2)
    cols = [lax.rem(z + b // 2, 4) * 2 + lax.rem(core + b, 2) for b in range(8)]

    def each(fun):
        def step(a, _):
            def one(b):
                o = lax.rem(a + 5 * b, 16)
                row = lax.rem(x + lax.div(o, 4), 4) * 4 + lax.rem(y + o, 4)
                fun(row * 8 + cols[b], (row, cols[b]))

            for b in (3, 6, 1, 4, 7, 2, 5):
                one(b)

            @pl.when(a > 0)
            def _():
                one(0)

            return 0

        lax.fori_loop(0, 16, step, 0)

    def push(src, dst, k, dev):
        pltpu.make_async_remote_copy(
            src_ref=src, dst_ref=dst, send_sem=ssem.at[k], recv_sem=rsem.at[k],
            device_id=dev, device_id_type=pl.DeviceIdType.MESH,
        ).start()

    def wait(part, sem):
        pltpu.make_async_copy(part, part, sem).wait()

    def keep(src, dst):
        copy = pltpu.make_async_copy(src, dst, lsem)
        copy.start()
        copy.wait()

    each(lambda d, dev: pl.semaphore_signal(
        barrier, inc=1, device_id=dev, device_id_type=pl.DeviceIdType.MESH))
    perm[...] = place(tiles, vc[0], tabs)
    loads[0].wait()
    loads[1].wait()

    def correct(s, _):
        weight = jnp.where(s < vc[0], cw[chan[s]], 0.0)
        one = beams[pair[0, s] * 2 + time[s]].astype(F32)
        two = beams[pair[1, s] * 2 + time[s]].astype(F32)
        gr = (one[0] * two[0] + one[1] * two[1]) * weight
        gi = (one[1] * two[0] - one[0] * two[1]) * weight
        pr, pi = px[s, 0], px[s, 1]
        at = pl.multiple_of(s * 32, 32)
        corr[pl.ds(at, 16), :] = pr * gr - pi * gi
        corr[pl.ds(at + 16, 16), :] = pr * gi + pi * gr
        return 0

    lax.fori_loop(0, 128, correct, 0, unroll=4)

    def coarse(group, _):
        for f in range(2):
            base = group * 16 * 32 + f
            re = [corr[pl.ds(base + 2 * p, 16, stride=32), :] for p in range(8)]
            im = [corr[pl.ds(base + 16 + 2 * p, 16, stride=32), :] for p in range(8)]
            re, im = dft8(re, im)
            rows = pl.ds(pl.multiple_of(f * 128 + group * 16, 16), 16)
            for k in range(8):
                lhi[k, rows, :128], llo[k, rows, :128] = split(re[k])
                lhi[k, rows, 128:], llo[k, rows, 128:] = split(im[k])
        return 0

    lax.fori_loop(0, 8, coarse, 0)
    loads[2].wait()
    loads[3].wait()

    early, late = pl.ds(0, 32), pl.ds(32, 32)

    def fine(k, _):
        a = jnp.where(k == 0, 0, jnp.where(k == 1, 4, lax.div(k, 2)))
        b = jnp.where(k < 2, a, 8 - a)
        acc = None
        for half, at in enumerate((a, b)):
            h = bh[k, half]
            term = dot(lhi[at], h) + dot(llo[at], h) + dot(lhi[at], bl[k, half])
            acc = term if acc is None else acc + term
        hi, lo = split(acc)
        for f in range(2):
            rows = slice(f * 128, f * 128 + 128)
            padded = dot(perm[...], jnp.concatenate([hi[rows], lo[rows]], axis=0))
            for p in range(2):
                for q in range(4):
                    send[(k * 4 + p * 2 + f) * 4 + q] = (
                        padded[q * 64:(q + 1) * 64, p * 128:(p + 1) * 128]
                    )
        return 0

    lax.fori_loop(0, 8, fine, 0)
    pl.semaphore_wait(barrier, 127)
    each(lambda d, dev: push(send.at[d, early], recv.at[me, early], 1, dev))
    each(lambda d, dev: push(tabs.at[lax.rem(d, 4)], tabr.at[me], 0, dev))
    each(lambda d, dev: push(send.at[d, late], recv.at[me, late], 2, dev))
    keep(tabs.at[lax.rem(me, 4)], tabr.at[me])
    keep(send.at[me], recv.at[me])
    flat = recv.reshape(128 * 64, 128)

    extra[...] = jnp.zeros((1024, 128), F32)
    for load in loads[4:9]:
        load.wait()
    wait(tabr.at[pl.ds(0, 127)], rsem.at[0])
    tabt[...] = tabr[...].reshape(128, 128).T
    lane = lax.broadcasted_iota(I32, (32, 128), 1)
    low = lane < 64

    def columns(pm, t):
        g = ghl[pm, pl.ds(pl.multiple_of(t * 256, 256), 256), :]
        for c in range(4):
            rows = slice(c * 128, c * 128 + 128)
            a = dot(wh[rows, :], g)
            b = dot(wl[rows, :], g[:, :128])
            u = a[:, :128] + a[:, 128:] + b
            ur, ui = u[:64], u[64:]
            m0 = slice(c * 64, c * 64 + 64)
            tr, ti = twr[m0, :], twi[m0, :]
            pqh[pm, m0, :128], pql[pm, m0, :128] = split(tr * ur - ti * ui)
            pqh[pm, m0, 128:], pql[pm, m0, 128:] = split(tr * ui + ti * ur)

    def mix(which, pm):
        both = fmat[kind, which]
        z = dot_nt(both, pqh[pm])
        return z[:128] + z[128:] + dot_nt(both[:128], pql[pm])

    def emit(dst, size, z, row, pms):
        for pm in pms:
            for tile in range(2):
                lanes = slice(tile * 128, tile * 128 + 128)
                re, im = z[pm * 64:pm * 64 + 32, lanes], z[pm * 64 + 32:pm * 64 + 64, lanes]
                even = jnp.where(low, re, pltpu.roll(im, 64, 1))
                odd = jnp.where(low, pltpu.roll(re, 64, 1), im)
                dst[pl.ds(2 * tile * size + row + pm, 32, stride=4 * size), :] = even
                dst[pl.ds((2 * tile + 1) * size + row + pm, 32, stride=4 * size), :] = odd

    def gather(rp):
        for pm in range(2):
            def block(c, _, pm=pm):
                at = rp * 32 + pm * 16 + 2 * c
                key = jnp.concatenate([tabt[pl.ds(at + k, 1), :] for k in range(2)], axis=1)
                parts = [split(flat[pl.ds(at + k, 128, stride=64), :]) for k in range(2)]
                rhs = jnp.concatenate([jnp.concatenate(p, axis=1) for p in parts], axis=0)
                for chunk in range(4):
                    tile = lax.broadcasted_iota(I32, (128, 256), 0) + chunk * 128
                    hit = jnp.where(tile == key, 1.0, 0.0).astype(BF)
                    s = dot(hit, rhs)
                    hi, lo = split(s[:, :128] + s[:, 128:])
                    for i in range(4):
                        to = pl.multiple_of((chunk * 4 + i) * 256 + c * 32, 32)
                        ghl[pm, pl.ds(to, 32), :128] = hi[i * 32:i * 32 + 32]
                        ghl[pm, pl.ds(to, 32), 128:] = lo[i * 32:i * 32 + 32]
                return 0

            lax.fori_loop(0, 8, block, 0)
        zc[...] = jnp.zeros((128, 256), F32)

    def phase(p, _):
        rp, half = lax.div(p, 2), lax.rem(p, 2)

        @pl.when(half == 0)
        def _():
            gather(rp)

        def row(i, _):
            t = half * 8 + i

            @pl.when(first & (t > 0))
            def _():
                zc[...] = mix(2, 1)

            columns(0, t)
            columns(1, 15 - t)
            emit(stage, 64, mix(0, 0) + mix(1, 1) + zc[...], rp * 32 + 2 * t, (0, 1))
            return 0

        lax.fori_loop(0, 8, row, 0)

        @pl.when(first & (half == 1))
        def _():
            emit(extra, 8, mix(2, 1), rp, (0,))

        @pl.when(p == 1)
        def _():
            def piece(d):
                return stage.at[pl.ds(pl.multiple_of(d * 64, 64), 32), :]

            wait(recv.at[pl.ds(0, 127), late], rsem.at[2])
            each(lambda d, dev: push(piece(d), got.at[me, early], 4, dev))
            keep(piece(me), got.at[me, early])

        @pl.when(p > 1)
        def _():
            rows = pl.ds(pl.multiple_of(p * 16, 16), 16)

            def piece(d):
                return stage.at[pl.ds(pl.multiple_of(d * 64 + p * 16, 16), 16), :]

            each(lambda d, dev: push(piece(d), got.at[me, rows], 3 + p, dev))
            keep(piece(me), got.at[me, rows])

        return 0

    wait(recv.at[pl.ds(0, 127), early], rsem.at[1])
    lax.fori_loop(0, 4, phase, 0)

    def piece(d):
        return extra.at[pl.ds(pl.multiple_of(d * 8, 8), 8), :]

    @pl.when(first)
    def _():
        each(lambda d, dev: push(piece(d), gotx.at[me], 3, dev))
        keep(piece(me), gotx.at[me])
        wait(extra.at[pl.ds(0, 127 * 8), :], ssem.at[3])

    wait(send.at[pl.ds(0, 127), early], ssem.at[1])
    wait(send.at[pl.ds(0, 127), late], ssem.at[2])
    for load in loads[9:]:
        load.wait()
    wait(got.at[pl.ds(0, 127), early], rsem.at[4])

    def transform(n, _, rp):
        f, group = lax.div(n, 4), lax.rem(n, 4)
        rows = slice(rp * 32, rp * 32 + 32)
        turned = row_dft(
            [[got[((4 * group + k) * 2 + f) * 4 + q, rows, :] for q in range(4)] for k in range(4)],
            (wrh.at[rp], wrl.at[rp]), tj, group,
        )

        def add(k, v):
            at = n * 16 + k
            send[at] = v if rp == 0 else send[at] + v

        for k in range(4, 16):
            add(k, turned[k])

        @pl.when(group > 0)
        def _():
            for k in range(4):
                add(k, turned[k])

        @pl.when(group == 0)
        def _():
            zero = row_dft_zero(
                [got[f * 4 + q, rows, :] for q in range(4)], (wsh.at[rp], wsl.at[rp])
            )
            if rp == 1:
                edge = jnp.concatenate([gotx[f * 4 + q] for q in range(4)], axis=0)
                edge = jnp.concatenate([edge, jnp.zeros((96, 128), F32)], axis=0).T[:, :32]
                v = three(edge[:64], (xh[0], xl[0])) + three(edge[64:], (xh[1], xl[1]))
                zero = [a + b for a, b in zip(zero, halves(v[:, :256], v[:, 256:]))]
            for k in range(4):
                add(k, zero[k])

        return 0

    lax.fori_loop(0, 8, functools.partial(transform, rp=0), 0)

    @pl.when(first)
    def _():
        wait(gotx.at[pl.ds(0, 7)], rsem.at[3])

    @pl.when(me >= 8)
    def _():
        wait(gotx, rsem.at[3])

    for p in range(2):
        wait(got.at[pl.ds(0, 127), pl.ds(p * 16, 16)], rsem.at[5 + p])

    def picture(f, _):
        lax.fori_loop(4 * f, 4 * f + 4, functools.partial(transform, rp=1), 0)

        def strip(i, _):
            at = pl.ds(pl.multiple_of(i * 8, 8), 8)
            for tile in range(2):
                mixed = mix_pairs(lambda k, part: send[f * 64 + 4 * k + 2 * part + tile, at, :])
                for l, value in mixed:
                    image[f, at, l * 256 + tile * 128:l * 256 + tile * 128 + 128] = value
            pltpu.make_async_copy(image.at[f, at, :], out.at[f, at, :], lsem).start()
            return 0

        lax.fori_loop(0, 8, strip, 0)
        return 0

    lax.fori_loop(0, 2, picture, 0)
    wait(out, lsem)
    wait(tabr.at[pl.ds(0, 127)], ssem.at[0])
    wait(got.at[pl.ds(0, 127), early], ssem.at[4])
    for p in range(2):
        wait(got.at[pl.ds(0, 127), pl.ds(p * 16, 16)], ssem.at[5 + p])


def exchange(tiles, pair, time, chan, count, weights, pixels, beams):
    t = tables()
    smem = pl.BlockSpec(memory_space=pltpu.SMEM)
    away = pl.BlockSpec(memory_space=pl.ANY)
    constants = (*t["b"], *t["wc"], *t["tw"], t["f"], *t["wr"], *t["ws"], *t["wx"], t["tj"])
    return pl.pallas_call(
        exchange_kernel,
        out_shape=jax.ShapeDtypeStruct((2, 64, 8192), F32),
        in_specs=[pl.BlockSpec(memory_space=pltpu.VMEM)] + [smem] * 5 + [away] * 16,
        out_specs=away,
        scratch_shapes=[
            pltpu.VMEM((128, 2, 16, 128), F32),
            pltpu.VMEM((1024, 2, 16, 128), BF),
            pltpu.VMEM((8, 2, 256, 256), BF),
            pltpu.VMEM((8, 2, 256, 256), BF),
            pltpu.VMEM((512, 256), BF),
            pltpu.VMEM((512, 256), BF),
            pltpu.VMEM((256, 128), F32),
            pltpu.VMEM((256, 128), F32),
            pltpu.VMEM((2, 3, 256, 256), BF),
            pltpu.VMEM((2, 128, 512), BF),
            pltpu.VMEM((2, 128, 512), BF),
            pltpu.VMEM((2, 2, 128, 512), BF),
            pltpu.VMEM((2, 2, 128, 512), BF),
            pltpu.VMEM((2, 32, 512), BF),
            pltpu.VMEM((2, 32, 512), BF),
            pltpu.VMEM((16, 2, 256), F32),
            pltpu.VMEM((128 * 32, 128), F32),
            pltpu.VMEM((8, 256, 256), BF),
            pltpu.VMEM((8, 256, 256), BF),
            pltpu.VMEM((256, 256), BF),
            pltpu.VMEM((128, 64, 128), F32),
            pltpu.VMEM((4, 1, 128), I32),
            pltpu.VMEM((128, 64, 128), F32),
            pltpu.VMEM((128, 1, 128), I32),
            pltpu.VMEM((128, 128), I32),
            pltpu.VMEM((2, 16 * 256, 256), BF),
            pltpu.VMEM((2, 256, 256), BF),
            pltpu.VMEM((2, 256, 256), BF),
            pltpu.VMEM((128, 256), F32),
            pltpu.VMEM((128 * 64, 128), F32),
            pltpu.VMEM((128 * 8, 128), F32),
            pltpu.VMEM((128, 64, 128), F32),
            pltpu.VMEM((8, 8, 128), F32),
            pltpu.VMEM((2, 64, 8192), F32),
            pltpu.SemaphoreType.DMA((8,)),
            pltpu.SemaphoreType.DMA((8,)),
            pltpu.SemaphoreType.DMA,
            pltpu.SemaphoreType.DMA((16,)),
        ],
        compiler_params=pltpu.CompilerParams(
            vmem_limit_bytes=VMEM, collective_id=0, has_side_effects=True
        ),
        name="exchange",
    )(tiles, pair, time, chan, count, weights, pixels, beams, *constants)


def pixel_view(pixels):
    x = pixels.reshape(128, 2, 2, 8, 128).transpose(0, 1, 3, 2, 4)
    return x.reshape(128, 2, 16, 128)


def beam_view(aterms):
    x = aterms.reshape(512, 2, 2, 2, 8, 128).transpose(0, 1, 2, 4, 3, 5)
    return x.reshape(1024, 2, 16, 128)


def local(
    subgrid_pixels, tile_offsets, station_pairs, time_blocks, channel_blocks, valid_counts,
    aterms, channel_weights,
):
    return exchange(
        tile_offsets.T, station_pairs.T, time_blocks, channel_blocks, valid_counts, channel_weights,
        pixel_view(subgrid_pixels), beam_view(aterms),
    )


def solution(mesh):
    in_specs = (
        P(("row", "col"), None, None, None),
        P(("row", "col"), None),
        P(("row", "col"), None),
        P(("row", "col")),
        P(("row", "col")),
        P(("row", "col")),
        P(),
        P(),
    )
    out_specs = P(None, ("row", "col"), None)
    return jax.shard_map(local, mesh=mesh, in_specs=in_specs, out_specs=out_specs, check_vma=False)
```

```python
import functools
import math

import jax
import jax.numpy as jnp
import ml_dtypes
import numpy as np
from jax import lax
from jax.experimental import pallas as pl
from jax.experimental.pallas import tpu as pltpu
from jax.sharding import PartitionSpec as P

BF = jnp.bfloat16
F32 = jnp.float32
I32 = jnp.int32

PAIR_J = (0, 8, 4, 12, 1, 9, 17, 25, 2, 10, 18, 26, 3, 11, 19, 27)
VMEM = 56 * 1024 * 1024


def partner(j):
    return 16 if j == 0 else 32 - j


def unit(turns):
    return np.exp(-2j * np.pi * turns)


def split_np(x):
    hi = np.asarray(x, np.float32).astype(ml_dtypes.bfloat16)
    lo = (np.asarray(x, np.float64) - hi.astype(np.float64)).astype(ml_dtypes.bfloat16)
    return hi, lo


def split(x):
    hi = x.astype(BF)
    return hi, (x - hi.astype(F32)).astype(BF)


def dot(a, b):
    return lax.dot_general(a, b, (((1,), (0,)), ((), ())), preferred_element_type=F32)


def dot_nt(a, b):
    return lax.dot_general(a, b, (((1,), (1,)), ((), ())), preferred_element_type=F32)


@functools.lru_cache(None)
def tables():
    xi = np.arange(4)[:, None, None]
    y = np.arange(32)[None, :, None]
    v = np.arange(32)[None, None, :]
    b = np.zeros((8, 2, 2, 4, 32, 2, 2, 2, 32))
    for step in range(8):
        for pair in range(2):
            j = PAIR_J[2 * step + pair]
            for half, jj in enumerate((j, partner(j))):
                w = unit((xi * jj + y * v) % 32 / 32) / 32
                b[step, half, 0, :, :, pair, half, 0] = w.real
                b[step, half, 0, :, :, pair, half, 1] = w.imag
                b[step, half, 1, :, :, pair, half, 0] = -w.imag
                b[step, half, 1, :, :, pair, half, 1] = w.real
    b = b.reshape(8, 2, 256, 256)
    i = np.arange(256)
    w = unit(i[:, None] * i[None, :] % 256 / 256)
    wc = np.stack([w.real.reshape(4, 64, 256), w.imag.reshape(4, 64, 256)], 1).reshape(512, 256)
    tw = unit(i[:, None] * (np.arange(128) % 32)[None, :] / 8192)
    d = unit(np.arange(32)[:, None] * np.arange(32)[None, :] % 32 / 32)
    coef = np.stack([np.stack([d, 1j * d]), np.stack([1j * d, -d])])
    f = np.zeros((2, 2, 2, 2, 32, 2, 2, 2, 32))

    def put(kind, which, half, pm, conj):
        for pq in range(2):
            for reim in range(2):
                c = coef[pq, reim]
                f[kind, which, pm, 0, :, pq, half, reim, :] = c.real
                f[kind, which, pm, 1, :, pq, half, reim, :] = -c.imag if conj else c.imag

    put(0, 0, 0, 0, False)
    put(0, 0, 1, 1, True)
    put(0, 1, 1, 0, True)
    put(0, 1, 0, 1, False)
    put(1, 0, 0, 0, False)
    put(1, 0, 1, 1, False)
    put(1, 1, 1, 1, True)
    put(1, 1, 0, 0, True)
    f = f.reshape(2, 2, 128, 256)
    fh, fl = split_np(f)
    f = np.concatenate([fh, fl], axis=2)
    k = np.arange(256)
    q, rp, t, pm = k // 64, k // 32 % 2, k // 2 % 16, k % 2
    r = 16 * (2 * q + rp) + t
    rr = np.where(pm == 0, r, 255 - r)
    l0 = np.arange(256)
    w = unit(rr[:, None] * l0[None, :] % 256 / 256) / 4096
    wr = np.concatenate([w.real, w.imag], axis=1)
    w0 = np.where((pm == 0)[:, None], unit(r[:, None] * l0[None, :] % 256 / 256), 0) / 4096
    w16 = np.where((pm == 1)[:, None], unit((32 * r[:, None] + 16) * l0[None, :] % 8192 / 8192), 0) / 4096
    ws = np.stack([np.concatenate([w0.real, w16.real], 1), np.concatenate([-w0.imag, -w16.imag], 1)])
    kx = np.arange(32)
    qx, row = kx // 8, kx % 8
    rx = 16 * (15 - (2 * qx + row))
    wx = np.where((row < 2)[:, None], unit(-(rx[:, None] * l0[None, :] % 256) / 256), 0) / 4096
    zero = np.zeros_like(wx.real)
    wx = np.stack([np.concatenate([wx.real, zero], 1), np.concatenate([-wx.imag, zero], 1)])
    tj = unit(np.array(PAIR_J)[:, None] * l0[None, :] / 8192)
    tj = np.stack([tj.real, tj.imag], 1).astype(np.float32)
    wr, ws = wr.reshape(4, 2, 32, 512), ws.reshape(2, 4, 2, 32, 512)
    wr = split_np(wr.transpose(1, 0, 2, 3).reshape(2, 128, 512))
    ws = split_np(ws.transpose(2, 0, 1, 3, 4).reshape(2, 2, 128, 512))
    return dict(
        b=split_np(b), wc=split_np(wc), tw=(tw.real.astype(np.float32), tw.imag.astype(np.float32)),
        f=f, wr=wr, ws=ws, wx=split_np(wx), tj=tj,
    )


def dft8(re, im):
    h = math.sqrt(0.5)

    def four(a, b):
        s0r, s0i = a[0] + a[2], b[0] + b[2]
        s1r, s1i = a[0] - a[2], b[0] - b[2]
        s2r, s2i = a[1] + a[3], b[1] + b[3]
        s3r, s3i = a[1] - a[3], b[1] - b[3]
        return (
            [s0r + s2r, s1r + s3i, s0r - s2r, s1r - s3i],
            [s0i + s2i, s1i - s3r, s0i - s2i, s1i + s3r],
        )

    er, ei = four(re[0::2], im[0::2])
    orr, oi = four(re[1::2], im[1::2])
    tr = [orr[0], (orr[1] + oi[1]) * h, oi[2], (oi[3] - orr[3]) * h]
    ti = [oi[0], (oi[1] - orr[1]) * h, -orr[2], -(oi[3] + orr[3]) * h]
    return (
        [er[k] + tr[k] for k in range(4)] + [er[k] - tr[k] for k in range(4)],
        [ei[k] + ti[k] for k in range(4)] + [ei[k] - ti[k] for k in range(4)],
    )


def place(tiles, count, tabs):
    row, col = tiles[0:1, :], tiles[1:2, :]
    block_row = lax.shift_right_logical(row, 4)
    low = block_row < 8
    near = jnp.where(low, block_row, 15 - block_row)
    block = (near * 2 + jnp.where(low, 0, 1)) * 8 + lax.shift_right_logical(col, 5)
    tile = (row & 15) * 32 + (col & 31)
    down = lax.broadcasted_iota(I32, (128, 128), 0)
    along = lax.broadcasted_iota(I32, (128, 128), 1)

    def column(x):
        return jnp.broadcast_to(x, (128, 128)).T

    earlier = (column(block) == block) & (down < along)
    rank = jnp.sum(jnp.where(earlier, 1.0, 0.0), axis=0, keepdims=True)
    slot = block * 2 + jnp.where(rank > 0.5, 1, 0)
    slot = jnp.where(along[0:1] < count, slot, -1)
    slots, tile = column(slot), column(tile).astype(F32)
    for q in range(4):
        tabs[q] = jnp.sum(jnp.where(slots == along + 64 * q, tile, 0.0), axis=0, keepdims=True).astype(I32)
    hit = jnp.where(lax.broadcasted_iota(I32, (256, 128), 0) == slot, 1.0, 0.0).astype(BF)
    return jnp.concatenate([hit, hit], axis=1)


def three(a, b):
    ah, al = split(a)
    return dot(ah, b[0]) + dot(al, b[0]) + dot(ah, b[1])


def halves(re, im):
    return [re[:, :128], re[:, 128:], im[:, :128], im[:, 128:]]


def row_dft(blocks, w, tj, group):
    a = jnp.concatenate([jnp.concatenate(b, axis=0).T for b in blocks], axis=0)
    u = three(a, (w[0][...], w[1][...]))
    outs = []
    for k in range(4):
        v = u[k * 128:k * 128 + 128]
        vr = v[:64, :256] - v[64:, 256:]
        vi = v[:64, 256:] + v[64:, :256]
        tr, ti = tj[4 * group + k, 0:1, :], tj[4 * group + k, 1:2, :]
        outs += halves(vr * tr - vi * ti, vr * ti + vi * tr)
    return outs


def row_dft_zero(block, w):
    a = jnp.concatenate(block, axis=0).T
    v = three(a[:64], (w[0][0], w[1][0])) + three(a[64:], (w[0][1], w[1][1]))
    return halves(v[:, :256], v[:, 256:])


def mix_pairs(load):
    index = {}
    for i, j in enumerate(PAIR_J):
        if i > 0:
            index[j if j < 16 else 32 - j] = (i, 1.0 if j < 16 else -1.0)
    zero, mid = load(0, 0), load(0, 1)
    re = {j: load(k, 0) for j, (k, _) in index.items()}
    im = {j: load(k, 1) for j, (k, _) in index.items()}

    def wave(fun, part, js, l1, signed):
        total = jnp.zeros((8, 128), F32)
        started = False
        for j in js:
            c = fun(2 * math.pi * (j * l1 % 32) / 32) * (index[j][1] if signed else 1.0)
            if abs(c) < 1e-12:
                continue
            term = part[j] if abs(abs(c) - 1) < 1e-12 else part[j] * abs(c)
            if started:
                total = total + term if c > 0 else total - term
            else:
                total = term if c > 0 else -term
            started = True
        return total

    odd, even, four = range(1, 16, 2), (2, 6, 10, 14), (4, 8, 12)
    ce, se = [None] * 9, [None] * 9
    for l1 in range(5):
        ee = wave(math.cos, re, four, l1, False) + (zero + mid if l1 % 2 == 0 else zero - mid)
        eo = wave(math.cos, re, even, l1, False)
        oe = wave(math.sin, im, four, l1, True)
        oo = wave(math.sin, im, even, l1, True)
        ce[l1], ce[8 - l1] = ee + eo, ee - eo
        se[l1], se[8 - l1] = oe + oo, oo - oe
    outs = []
    for l1 in range(9):
        co = wave(math.cos, re, odd, l1, False)
        so = wave(math.sin, im, odd, l1, True)
        p, m = ce[l1] + co, ce[l1] - co
        s, d = se[l1] + so, se[l1] - so
        outs += [(l1, p + s), (16 + l1, m + d)]
        if l1 > 0:
            outs.append((32 - l1, p - s))
            if l1 < 8:
                outs.append((16 - l1, m - d))
    return outs


def exchange_kernel(
    tiles, pair, time, chan, vc, cw, pixels_hbm, beams_hbm, bh_hbm, bl_hbm,
    wh_hbm, wl_hbm, twr_hbm, twi_hbm, fmat_hbm,
    wrh_hbm, wrl_hbm, wsh_hbm, wsl_hbm, xh_hbm, xl_hbm, tj_hbm, out,
    px, beams, bh, bl, wh, wl, twr, twi, fmat, wrh, wrl, wsh, wsl, xh, xl, tj,
    corr, lhi, llo, perm, send, tabs,
    recv, tabr, tabt, ghl, pqh, pql, held, stage, extra, got, gotx, image, ssem, rsem, lsem, csem
):
    me = lax.axis_index("row") * 8 + lax.axis_index("col")
    first = me < 8
    kind = jnp.where(first, 1, 0)
    barrier = pltpu.get_barrier_semaphore()
    loads = [
        pltpu.make_async_copy(src, dst, csem.at[i])
        for i, (src, dst) in enumerate((
            (beams_hbm, beams), (pixels_hbm, px), (bh_hbm, bh), (bl_hbm, bl), (wh_hbm, wh),
            (wl_hbm, wl), (twr_hbm, twr), (twi_hbm, twi), (fmat_hbm, fmat),
            (wrh_hbm, wrh), (wrl_hbm, wrl), (wsh_hbm, wsh), (wsl_hbm, wsl),
            (xh_hbm, xh), (xl_hbm, xl), (tj_hbm, tj),
        ))
    ]
    for load in loads:
        load.start()

    x, y = lax.div(lax.axis_index("row"), 4), lax.rem(lax.axis_index("row"), 4)
    z, core = lax.div(lax.axis_index("col"), 2), lax.rem(lax.axis_index("col"), 2)
    cols = [lax.rem(z + b // 2, 4) * 2 + lax.rem(core + b, 2) for b in range(8)]

    def each(fun):
        def step(a, _):
            def one(b):
                o = lax.rem(a + 5 * b, 16)
                row = lax.rem(x + lax.div(o, 4), 4) * 4 + lax.rem(y + o, 4)
                fun(row * 8 + cols[b], (row, cols[b]))

            for b in (3, 6, 1, 4, 7, 2, 5):
                one(b)

            @pl.when(a > 0)
            def _():
                one(0)

            return 0

        lax.fori_loop(0, 16, step, 0)

    def push(src, dst, k, dev):
        pltpu.make_async_remote_copy(
            src_ref=src, dst_ref=dst, send_sem=ssem.at[k], recv_sem=rsem.at[k],
            device_id=dev, device_id_type=pl.DeviceIdType.MESH,
        ).start()

    def wait(part, sem):
        pltpu.make_async_copy(part, part, sem).wait()

    def keep(src, dst):
        copy = pltpu.make_async_copy(src, dst, lsem)
        copy.start()
        copy.wait()

    each(lambda d, dev: pl.semaphore_signal(
        barrier, inc=1, device_id=dev, device_id_type=pl.DeviceIdType.MESH))
    perm[...] = place(tiles, vc[0], tabs)
    loads[0].wait()
    loads[1].wait()

    def correct(s, _):
        weight = jnp.where(s < vc[0], cw[chan[s]], 0.0)
        one = beams[pair[0, s] * 2 + time[s]].astype(F32)
        two = beams[pair[1, s] * 2 + time[s]].astype(F32)
        gr = (one[0] * two[0] + one[1] * two[1]) * weight
        gi = (one[1] * two[0] - one[0] * two[1]) * weight
        pr, pi = px[s, 0], px[s, 1]
        at = pl.multiple_of(s * 32, 32)
        corr[pl.ds(at, 16), :] = pr * gr - pi * gi
        corr[pl.ds(at + 16, 16), :] = pr * gi + pi * gr
        return 0

    lax.fori_loop(0, 128, correct, 0, unroll=4)

    def coarse(group, _):
        for f in range(2):
            base = group * 16 * 32 + f
            re = [corr[pl.ds(base + 2 * p, 16, stride=32), :] for p in range(8)]
            im = [corr[pl.ds(base + 16 + 2 * p, 16, stride=32), :] for p in range(8)]
            re, im = dft8(re, im)
            rows = pl.ds(pl.multiple_of(f * 128 + group * 16, 16), 16)
            for k in range(8):
                lhi[k, rows, :128], llo[k, rows, :128] = split(re[k])
                lhi[k, rows, 128:], llo[k, rows, 128:] = split(im[k])
        return 0

    lax.fori_loop(0, 8, coarse, 0)
    loads[2].wait()
    loads[3].wait()

    early, late = pl.ds(0, 32), pl.ds(32, 32)

    def fine(k, _):
        a = jnp.where(k == 0, 0, jnp.where(k == 1, 4, lax.div(k, 2)))
        b = jnp.where(k < 2, a, 8 - a)
        acc = None
        for half, at in enumerate((a, b)):
            h = bh[k, half]
            term = dot(lhi[at], h) + dot(llo[at], h) + dot(lhi[at], bl[k, half])
            acc = term if acc is None else acc + term
        hi, lo = split(acc)
        for f in range(2):
            rows = slice(f * 128, f * 128 + 128)
            padded = dot(perm[...], jnp.concatenate([hi[rows], lo[rows]], axis=0))
            for p in range(2):
                for q in range(4):
                    send[(k * 4 + p * 2 + f) * 4 + q] = (
                        padded[q * 64:(q + 1) * 64, p * 128:(p + 1) * 128]
                    )
        return 0

    lax.fori_loop(0, 8, fine, 0)
    pl.semaphore_wait(barrier, 127)
    each(lambda d, dev: push(send.at[d, early], recv.at[me, early], 1, dev))
    each(lambda d, dev: push(tabs.at[lax.rem(d, 4)], tabr.at[me], 0, dev))
    each(lambda d, dev: push(send.at[d, late], recv.at[me, late], 2, dev))
    keep(tabs.at[lax.rem(me, 4)], tabr.at[me])
    keep(send.at[me], recv.at[me])
    flat = recv.reshape(128 * 64, 128)

    extra[...] = jnp.zeros((1024, 128), F32)
    for load in loads[4:9]:
        load.wait()
    wait(tabr.at[pl.ds(0, 127)], rsem.at[0])
    tabt[...] = tabr[...].reshape(128, 128).T
    lane = lax.broadcasted_iota(I32, (32, 128), 1)
    low = lane < 64

    shifted = first & (lax.broadcasted_iota(I32, (64, 128), 1) < 64)

    def columns(pm, t):
        g = ghl[pm, pl.ds(pl.multiple_of(t * 256, 256), 256), :]
        for c in range(4):
            rows = slice(c * 128, c * 128 + 128)
            a = dot(wh[rows, :], g)
            b = dot(wl[rows, :], g[:, :128])
            u = a[:, :128] + a[:, 128:] + b
            ur, ui = u[:64], u[64:]
            m0 = slice(c * 64, c * 64 + 64)
            tr, ti = twr[m0, :], twi[m0, :]
            for lanes, value in (
                (slice(0, 128), tr * ur - ti * ui), (slice(128, 256), tr * ui + ti * ur)
            ):
                if pm == 1:
                    value, held[m0, lanes] = jnp.where(shifted, held[m0, lanes], value), value
                pqh[pm, m0, lanes], pql[pm, m0, lanes] = split(value)

    def mix(which, pm):
        both = fmat[kind, which]
        z = dot_nt(both, pqh[pm])
        return z[:128] + z[128:] + dot_nt(both[:128], pql[pm])

    def emit(dst, size, z, row, pms):
        for pm in pms:
            for tile in range(2):
                lanes = slice(tile * 128, tile * 128 + 128)
                re, im = z[pm * 64:pm * 64 + 32, lanes], z[pm * 64 + 32:pm * 64 + 64, lanes]
                even = jnp.where(low, re, pltpu.roll(im, 64, 1))
                odd = jnp.where(low, pltpu.roll(re, 64, 1), im)
                dst[pl.ds(2 * tile * size + row + pm, 32, stride=4 * size), :] = even
                dst[pl.ds((2 * tile + 1) * size + row + pm, 32, stride=4 * size), :] = odd

    def gather(rp):
        for pm in range(2):
            def block(c, _, pm=pm):
                at = rp * 32 + pm * 16 + 2 * c
                key = jnp.concatenate([tabt[pl.ds(at + k, 1), :] for k in range(2)], axis=1)
                parts = [split(flat[pl.ds(at + k, 128, stride=64), :]) for k in range(2)]
                rhs = jnp.concatenate([jnp.concatenate(p, axis=1) for p in parts], axis=0)
                for chunk in range(4):
                    tile = lax.broadcasted_iota(I32, (128, 256), 0) + chunk * 128
                    hit = jnp.where(tile == key, 1.0, 0.0).astype(BF)
                    s = dot(hit, rhs)
                    hi, lo = split(s[:, :128] + s[:, 128:])
                    for i in range(4):
                        to = pl.multiple_of((chunk * 4 + i) * 256 + c * 32, 32)
                        ghl[pm, pl.ds(to, 32), :128] = hi[i * 32:i * 32 + 32]
                        ghl[pm, pl.ds(to, 32), 128:] = lo[i * 32:i * 32 + 32]
                return 0

            lax.fori_loop(0, 8, block, 0)
        held[...] = jnp.zeros((256, 256), F32)

    def phase(p, _):
        rp, half = lax.div(p, 2), lax.rem(p, 2)

        @pl.when(half == 0)
        def _():
            gather(rp)

        def row(i, _):
            t = half * 8 + i

            columns(0, t)
            columns(1, 15 - t)
            emit(stage, 64, mix(0, 0) + mix(1, 1), rp * 32 + 2 * t, (0, 1))
            return 0

        lax.fori_loop(0, 8, row, 0)

        @pl.when(first & (half == 1))
        def _():
            for lanes in (slice(0, 128), slice(128, 256)):
                pqh[1, :, lanes], pql[1, :, lanes] = split(held[:, lanes])
            emit(extra, 8, mix(1, 1), rp, (0,))

        @pl.when(p == 1)
        def _():
            def piece(d):
                return stage.at[pl.ds(pl.multiple_of(d * 64, 64), 32), :]

            wait(recv.at[pl.ds(0, 127), late], rsem.at[2])
            each(lambda d, dev: push(piece(d), got.at[me, early], 4, dev))
            keep(piece(me), got.at[me, early])

        @pl.when(p > 1)
        def _():
            rows = pl.ds(pl.multiple_of(p * 16, 16), 16)

            def piece(d):
                return stage.at[pl.ds(pl.multiple_of(d * 64 + p * 16, 16), 16), :]

            each(lambda d, dev: push(piece(d), got.at[me, rows], 3 + p, dev))
            keep(piece(me), got.at[me, rows])

        return 0

    wait(recv.at[pl.ds(0, 127), early], rsem.at[1])
    lax.fori_loop(0, 4, phase, 0)

    def piece(d):
        return extra.at[pl.ds(pl.multiple_of(d * 8, 8), 8), :]

    @pl.when(first)
    def _():
        each(lambda d, dev: push(piece(d), gotx.at[me], 3, dev))
        keep(piece(me), gotx.at[me])

    wait(send.at[pl.ds(0, 127), early], ssem.at[1])
    wait(send.at[pl.ds(0, 127), late], ssem.at[2])
    for load in loads[9:]:
        load.wait()
    wait(got.at[pl.ds(0, 127), early], rsem.at[4])

    def transform(n, _, rp):
        f, group = lax.div(n, 4), lax.rem(n, 4)
        rows = slice(rp * 32, rp * 32 + 32)
        turned = row_dft(
            [[got[((4 * group + k) * 2 + f) * 4 + q, rows, :] for q in range(4)] for k in range(4)],
            (wrh.at[rp], wrl.at[rp]), tj, group,
        )

        def add(k, v):
            at = n * 16 + k
            send[at] = v if rp == 0 else send[at] + v

        for k in range(4, 16):
            add(k, turned[k])

        @pl.when(group > 0)
        def _():
            for k in range(4):
                add(k, turned[k])

        @pl.when(group == 0)
        def _():
            zero = row_dft_zero(
                [got[f * 4 + q, rows, :] for q in range(4)], (wsh.at[rp], wsl.at[rp])
            )
            if rp == 1:
                edge = jnp.concatenate([gotx[f * 4 + q] for q in range(4)], axis=0)
                edge = jnp.concatenate([edge, jnp.zeros((96, 128), F32)], axis=0).T[:, :32]
                v = three(edge[:64], (xh[0], xl[0])) + three(edge[64:], (xh[1], xl[1]))
                zero = [a + b for a, b in zip(zero, halves(v[:, :256], v[:, 256:]))]
            for k in range(4):
                add(k, zero[k])

        return 0

    lax.fori_loop(0, 8, functools.partial(transform, rp=0), 0)

    @pl.when(first)
    def _():
        wait(gotx.at[pl.ds(0, 7)], rsem.at[3])

    @pl.when(me >= 8)
    def _():
        wait(gotx, rsem.at[3])

    for p in range(2):
        wait(got.at[pl.ds(0, 127), pl.ds(p * 16, 16)], rsem.at[5 + p])

    def picture(f, _):
        lax.fori_loop(4 * f, 4 * f + 4, functools.partial(transform, rp=1), 0)

        def strip(i, _):
            at = pl.ds(pl.multiple_of(i * 8, 8), 8)
            for tile in range(2):
                mixed = mix_pairs(lambda k, part: send[f * 64 + 4 * k + 2 * part + tile, at, :])
                for l, value in mixed:
                    image[f, at, l * 256 + tile * 128:l * 256 + tile * 128 + 128] = value
            pltpu.make_async_copy(image.at[f, at, :], out.at[f, at, :], lsem).start()
            return 0

        lax.fori_loop(0, 8, strip, 0)
        return 0

    lax.fori_loop(0, 2, picture, 0)
    wait(out, lsem)
    @pl.when(first)
    def _():
        wait(extra.at[pl.ds(0, 127 * 8), :], ssem.at[3])

    wait(tabr.at[pl.ds(0, 127)], ssem.at[0])
    wait(got.at[pl.ds(0, 127), early], ssem.at[4])
    for p in range(2):
        wait(got.at[pl.ds(0, 127), pl.ds(p * 16, 16)], ssem.at[5 + p])


def exchange(tiles, pair, time, chan, count, weights, pixels, beams):
    t = tables()
    smem = pl.BlockSpec(memory_space=pltpu.SMEM)
    away = pl.BlockSpec(memory_space=pl.ANY)
    constants = (*t["b"], *t["wc"], *t["tw"], t["f"], *t["wr"], *t["ws"], *t["wx"], t["tj"])
    return pl.pallas_call(
        exchange_kernel,
        out_shape=jax.ShapeDtypeStruct((2, 64, 8192), F32),
        in_specs=[pl.BlockSpec(memory_space=pltpu.VMEM)] + [smem] * 5 + [away] * 16,
        out_specs=away,
        scratch_shapes=[
            pltpu.VMEM((128, 2, 16, 128), F32),
            pltpu.VMEM((1024, 2, 16, 128), BF),
            pltpu.VMEM((8, 2, 256, 256), BF),
            pltpu.VMEM((8, 2, 256, 256), BF),
            pltpu.VMEM((512, 256), BF),
            pltpu.VMEM((512, 256), BF),
            pltpu.VMEM((256, 128), F32),
            pltpu.VMEM((256, 128), F32),
            pltpu.VMEM((2, 2, 256, 256), BF),
            pltpu.VMEM((2, 128, 512), BF),
            pltpu.VMEM((2, 128, 512), BF),
            pltpu.VMEM((2, 2, 128, 512), BF),
            pltpu.VMEM((2, 2, 128, 512), BF),
            pltpu.VMEM((2, 32, 512), BF),
            pltpu.VMEM((2, 32, 512), BF),
            pltpu.VMEM((16, 2, 256), F32),
            pltpu.VMEM((128 * 32, 128), F32),
            pltpu.VMEM((8, 256, 256), BF),
            pltpu.VMEM((8, 256, 256), BF),
            pltpu.VMEM((256, 256), BF),
            pltpu.VMEM((128, 64, 128), F32),
            pltpu.VMEM((4, 1, 128), I32),
            pltpu.VMEM((128, 64, 128), F32),
            pltpu.VMEM((128, 1, 128), I32),
            pltpu.VMEM((128, 128), I32),
            pltpu.VMEM((2, 16 * 256, 256), BF),
            pltpu.VMEM((2, 256, 256), BF),
            pltpu.VMEM((2, 256, 256), BF),
            pltpu.VMEM((256, 256), F32),
            pltpu.VMEM((128 * 64, 128), F32),
            pltpu.VMEM((128 * 8, 128), F32),
            pltpu.VMEM((128, 64, 128), F32),
            pltpu.VMEM((8, 8, 128), F32),
            pltpu.VMEM((2, 64, 8192), F32),
            pltpu.SemaphoreType.DMA((8,)),
            pltpu.SemaphoreType.DMA((8,)),
            pltpu.SemaphoreType.DMA,
            pltpu.SemaphoreType.DMA((16,)),
        ],
        compiler_params=pltpu.CompilerParams(
            vmem_limit_bytes=VMEM, collective_id=0, has_side_effects=True
        ),
        name="exchange",
    )(tiles, pair, time, chan, count, weights, pixels, beams, *constants)


def pixel_view(pixels):
    x = pixels.reshape(128, 2, 2, 8, 128).transpose(0, 1, 3, 2, 4)
    return x.reshape(128, 2, 16, 128)


def beam_view(aterms):
    x = aterms.reshape(512, 2, 2, 2, 8, 128).transpose(0, 1, 2, 4, 3, 5)
    return x.reshape(1024, 2, 16, 128)


def local(
    subgrid_pixels, tile_offsets, station_pairs, time_blocks, channel_blocks, valid_counts,
    aterms, channel_weights,
):
    return exchange(
        tile_offsets.T, station_pairs.T, time_blocks, channel_blocks, valid_counts, channel_weights,
        pixel_view(subgrid_pixels), beam_view(aterms),
    )


def solution(mesh):
    in_specs = (
        P(("row", "col"), None, None, None),
        P(("row", "col"), None),
        P(("row", "col"), None),
        P(("row", "col")),
        P(("row", "col")),
        P(("row", "col")),
        P(),
        P(),
    )
    out_specs = P(None, ("row", "col"), None)
    return jax.shard_map(local, mesh=mesh, in_specs=in_specs, out_specs=out_specs, check_vma=False)
```

```python
import functools
import math

import jax
import jax.numpy as jnp
import ml_dtypes
import numpy as np
from jax import lax
from jax.experimental import pallas as pl
from jax.experimental.pallas import tpu as pltpu
from jax.sharding import PartitionSpec as P

BF = jnp.bfloat16
F32 = jnp.float32
I32 = jnp.int32

PAIR_J = (0, 8, 4, 12, 1, 9, 17, 25, 2, 10, 18, 26, 3, 11, 19, 27)
VMEM = 56 * 1024 * 1024


def partner(j):
    return 16 if j == 0 else 32 - j


def unit(turns):
    return np.exp(-2j * np.pi * turns)


def split_np(x):
    hi = np.asarray(x, np.float32).astype(ml_dtypes.bfloat16)
    lo = (np.asarray(x, np.float64) - hi.astype(np.float64)).astype(ml_dtypes.bfloat16)
    return hi, lo


def split(x):
    hi = x.astype(BF)
    return hi, (x - hi.astype(F32)).astype(BF)


def dot(a, b):
    return lax.dot_general(a, b, (((1,), (0,)), ((), ())), preferred_element_type=F32)


def dot_nt(a, b):
    return lax.dot_general(a, b, (((1,), (1,)), ((), ())), preferred_element_type=F32)


@functools.lru_cache(None)
def tables():
    xi = np.arange(4)[:, None, None]
    y = np.arange(32)[None, :, None]
    v = np.arange(32)[None, None, :]
    b = np.zeros((8, 2, 2, 4, 32, 2, 2, 2, 32))
    for step in range(8):
        for pair in range(2):
            j = PAIR_J[2 * step + pair]
            for half, jj in enumerate((j, partner(j))):
                w = unit((xi * jj + y * v) % 32 / 32) / 32
                b[step, half, 0, :, :, pair, half, 0] = w.real
                b[step, half, 0, :, :, pair, half, 1] = w.imag
                b[step, half, 1, :, :, pair, half, 0] = -w.imag
                b[step, half, 1, :, :, pair, half, 1] = w.real
    b = b.reshape(8, 2, 256, 256)
    i = np.arange(256)
    w = unit(i[:, None] * i[None, :] % 256 / 256)
    wc = np.stack([w.real.reshape(4, 64, 256), w.imag.reshape(4, 64, 256)], 1).reshape(512, 256)
    tw = unit(i[:, None] * (np.arange(128) % 32)[None, :] / 8192)
    d = unit(np.arange(32)[:, None] * np.arange(32)[None, :] % 32 / 32)
    coef = np.stack([np.stack([d, 1j * d]), np.stack([1j * d, -d])])
    f = np.zeros((2, 2, 2, 2, 32, 2, 2, 2, 32))

    def put(kind, which, half, pm, conj):
        for pq in range(2):
            for reim in range(2):
                c = coef[pq, reim]
                f[kind, which, pm, 0, :, pq, half, reim, :] = c.real
                f[kind, which, pm, 1, :, pq, half, reim, :] = -c.imag if conj else c.imag

    put(0, 0, 0, 0, False)
    put(0, 0, 1, 1, True)
    put(0, 1, 1, 0, True)
    put(0, 1, 0, 1, False)
    put(1, 0, 0, 0, False)
    put(1, 0, 1, 1, False)
    put(1, 1, 1, 1, True)
    put(1, 1, 0, 0, True)
    f = f.reshape(2, 2, 128, 256)
    fh, fl = split_np(f)
    f = np.concatenate([fh, fl], axis=2)
    k = np.arange(256)
    q, rp, t, pm = k // 64, k // 32 % 2, k // 2 % 16, k % 2
    r = 16 * (2 * q + rp) + t
    rr = np.where(pm == 0, r, 255 - r)
    l0 = np.arange(256)
    w = unit(rr[:, None] * l0[None, :] % 256 / 256) / 4096
    wr = np.concatenate([w.real, w.imag], axis=1)
    w0 = np.where((pm == 0)[:, None], unit(r[:, None] * l0[None, :] % 256 / 256), 0) / 4096
    w16 = np.where((pm == 1)[:, None], unit((32 * r[:, None] + 16) * l0[None, :] % 8192 / 8192), 0) / 4096
    ws = np.stack([np.concatenate([w0.real, w16.real], 1), np.concatenate([-w0.imag, -w16.imag], 1)])
    kx = np.arange(32)
    qx, row = kx // 2 % 4, kx % 2
    rx = 16 * (15 - (2 * qx + row))
    wx = np.where((kx < 8)[:, None], unit(-(rx[:, None] * l0[None, :] % 256) / 256), 0) / 4096
    zero = np.zeros_like(wx.real)
    wx = np.stack([np.concatenate([wx.real, zero], 1), np.concatenate([-wx.imag, zero], 1)])
    tj = unit(np.array(PAIR_J)[:, None] * l0[None, :] / 8192)
    tj = np.stack([tj.real, tj.imag], 1).astype(np.float32)
    wr, ws = wr.reshape(4, 2, 32, 512), ws.reshape(2, 4, 2, 32, 512)
    wr = split_np(wr.transpose(1, 0, 2, 3).reshape(2, 128, 512))
    ws = split_np(ws.transpose(2, 0, 1, 3, 4).reshape(2, 2, 128, 512))
    return dict(
        b=split_np(b), wc=split_np(wc), tw=(tw.real.astype(np.float32), tw.imag.astype(np.float32)),
        f=f, wr=wr, ws=ws, wx=split_np(wx), tj=tj,
    )


def dft8(re, im):
    h = math.sqrt(0.5)

    def four(a, b):
        s0r, s0i = a[0] + a[2], b[0] + b[2]
        s1r, s1i = a[0] - a[2], b[0] - b[2]
        s2r, s2i = a[1] + a[3], b[1] + b[3]
        s3r, s3i = a[1] - a[3], b[1] - b[3]
        return (
            [s0r + s2r, s1r + s3i, s0r - s2r, s1r - s3i],
            [s0i + s2i, s1i - s3r, s0i - s2i, s1i + s3r],
        )

    er, ei = four(re[0::2], im[0::2])
    orr, oi = four(re[1::2], im[1::2])
    tr = [orr[0], (orr[1] + oi[1]) * h, oi[2], (oi[3] - orr[3]) * h]
    ti = [oi[0], (oi[1] - orr[1]) * h, -orr[2], -(oi[3] + orr[3]) * h]
    return (
        [er[k] + tr[k] for k in range(4)] + [er[k] - tr[k] for k in range(4)],
        [ei[k] + ti[k] for k in range(4)] + [ei[k] - ti[k] for k in range(4)],
    )


def place(tiles, count, tabs):
    row, col = tiles[0:1, :], tiles[1:2, :]
    block_row = lax.shift_right_logical(row, 4)
    low = block_row < 8
    near = jnp.where(low, block_row, 15 - block_row)
    block = (near * 2 + jnp.where(low, 0, 1)) * 8 + lax.shift_right_logical(col, 5)
    tile = (row & 15) * 32 + (col & 31)
    down = lax.broadcasted_iota(I32, (128, 128), 0)
    along = lax.broadcasted_iota(I32, (128, 128), 1)

    def column(x):
        return jnp.broadcast_to(x, (128, 128)).T

    earlier = (column(block) == block) & (down < along)
    rank = jnp.sum(jnp.where(earlier, 1.0, 0.0), axis=0, keepdims=True)
    slot = block * 2 + jnp.where(rank > 0.5, 1, 0)
    slot = jnp.where(along[0:1] < count, slot, -1)
    slots, tile = column(slot), column(tile).astype(F32)
    for q in range(4):
        tabs[q] = jnp.sum(jnp.where(slots == along + 64 * q, tile, 0.0), axis=0, keepdims=True).astype(I32)
    hit = jnp.where(lax.broadcasted_iota(I32, (256, 128), 0) == slot, 1.0, 0.0).astype(BF)
    return jnp.concatenate([hit, hit], axis=1)


def three(a, b):
    ah, al = split(a)
    return dot(ah, b[0]) + dot(al, b[0]) + dot(ah, b[1])


def halves(re, im):
    return [re[:, :128], re[:, 128:], im[:, :128], im[:, 128:]]


def row_dft(blocks, w, tj, group):
    a = jnp.concatenate([jnp.concatenate(b, axis=0).T for b in blocks], axis=0)
    u = three(a, (w[0][...], w[1][...]))
    outs = []
    for k in range(4):
        v = u[k * 128:k * 128 + 128]
        vr = v[:64, :256] - v[64:, 256:]
        vi = v[:64, 256:] + v[64:, :256]
        tr, ti = tj[4 * group + k, 0:1, :], tj[4 * group + k, 1:2, :]
        outs += halves(vr * tr - vi * ti, vr * ti + vi * tr)
    return outs


def row_dft_zero(block, w):
    a = jnp.concatenate(block, axis=0).T
    v = three(a[:64], (w[0][0], w[1][0])) + three(a[64:], (w[0][1], w[1][1]))
    return halves(v[:, :256], v[:, 256:])


def mix_pairs(load):
    index = {}
    for i, j in enumerate(PAIR_J):
        if i > 0:
            index[j if j < 16 else 32 - j] = (i, 1.0 if j < 16 else -1.0)
    zero, mid = load(0, 0), load(0, 1)
    re = {j: load(k, 0) for j, (k, _) in index.items()}
    im = {j: load(k, 1) for j, (k, _) in index.items()}

    def wave(fun, part, js, l1, signed):
        total = jnp.zeros((8, 128), F32)
        started = False
        for j in js:
            c = fun(2 * math.pi * (j * l1 % 32) / 32) * (index[j][1] if signed else 1.0)
            if abs(c) < 1e-12:
                continue
            term = part[j] if abs(abs(c) - 1) < 1e-12 else part[j] * abs(c)
            if started:
                total = total + term if c > 0 else total - term
            else:
                total = term if c > 0 else -term
            started = True
        return total

    odd, even, four = range(1, 16, 2), (2, 6, 10, 14), (4, 8, 12)
    ce, se = [None] * 9, [None] * 9
    for l1 in range(5):
        ee = wave(math.cos, re, four, l1, False) + (zero + mid if l1 % 2 == 0 else zero - mid)
        eo = wave(math.cos, re, even, l1, False)
        oe = wave(math.sin, im, four, l1, True)
        oo = wave(math.sin, im, even, l1, True)
        ce[l1], ce[8 - l1] = ee + eo, ee - eo
        se[l1], se[8 - l1] = oe + oo, oo - oe
    outs = []
    for l1 in range(9):
        co = wave(math.cos, re, odd, l1, False)
        so = wave(math.sin, im, odd, l1, True)
        p, m = ce[l1] + co, ce[l1] - co
        s, d = se[l1] + so, se[l1] - so
        outs += [(l1, p + s), (16 + l1, m + d)]
        if l1 > 0:
            outs.append((32 - l1, p - s))
            if l1 < 8:
                outs.append((16 - l1, m - d))
    return outs


def exchange_kernel(
    tiles, pair, time, chan, vc, cw, pixels_hbm, beams_hbm, bh_hbm, bl_hbm,
    wh_hbm, wl_hbm, twr_hbm, twi_hbm, fmat_hbm,
    wrh_hbm, wrl_hbm, wsh_hbm, wsl_hbm, xh_hbm, xl_hbm, tj_hbm, out,
    px, beams, bh, bl, wh, wl, twr, twi, fmat, wrh, wrl, wsh, wsl, xh, xl, tj,
    corr, lhi, llo, perm, send, tabs,
    recv, tabr, tabt, ghl, pqh, pql, held, stage, extra, got, gotx, edges, image, ssem, rsem, lsem, csem
):
    line, column = lax.axis_index("row"), lax.axis_index("col")
    x, y = lax.div(line, 4), lax.rem(line, 4)
    z, core = lax.div(column, 2), lax.rem(column, 2)
    me = line * 8 + column

    def unit_of(row, col):
        turn = lax.rem(lax.div(row, 4) + row + lax.div(col, 2), 4)
        return (turn * 2 + lax.rem(col, 2)) * 16 + row

    mine = unit_of(line, column)
    first = mine < 8
    kind = jnp.where(first, 1, 0)
    barrier = pltpu.get_barrier_semaphore()
    loads = [
        pltpu.make_async_copy(src, dst, csem.at[i])
        for i, (src, dst) in enumerate((
            (beams_hbm, beams), (pixels_hbm, px), (bh_hbm, bh), (bl_hbm, bl), (wh_hbm, wh),
            (wl_hbm, wl), (twr_hbm, twr), (twi_hbm, twi), (fmat_hbm, fmat),
            (wrh_hbm, wrh), (wrl_hbm, wrl), (wsh_hbm, wsh), (wsl_hbm, wsl),
            (xh_hbm, xh), (xl_hbm, xl), (tj_hbm, tj),
        ))
    ]
    for load in loads:
        load.start()

    cols = [lax.rem(z + b // 2, 4) * 2 + lax.rem(core + b, 2) for b in range(8)]

    def each(fun):
        def step(a, _):
            def one(b):
                o = lax.rem(a + 5 * b, 16)
                row = lax.rem(x + lax.div(o, 4), 4) * 4 + lax.rem(y + o, 4)
                fun(row * 8 + cols[b], (row, cols[b]))

            for b in (3, 6, 1, 4, 7, 2, 5):
                one(b)

            @pl.when(a > 0)
            def _():
                one(0)

            return 0

        lax.fori_loop(0, 16, step, 0)

    def push(src, dst, k, dev):
        pltpu.make_async_remote_copy(
            src_ref=src, dst_ref=dst, send_sem=ssem.at[k], recv_sem=rsem.at[k],
            device_id=dev, device_id_type=pl.DeviceIdType.MESH,
        ).start()

    def wait(part, sem):
        pltpu.make_async_copy(part, part, sem).wait()

    def keep(src, dst):
        copy = pltpu.make_async_copy(src, dst, lsem)
        copy.start()
        copy.wait()

    each(lambda d, dev: pl.semaphore_signal(
        barrier, inc=1, device_id=dev, device_id_type=pl.DeviceIdType.MESH))
    perm[...] = place(tiles, vc[0], tabs)
    loads[0].wait()
    loads[1].wait()

    def correct(s, _):
        weight = jnp.where(s < vc[0], cw[chan[s]], 0.0)
        one = beams[pair[0, s] * 2 + time[s]].astype(F32)
        two = beams[pair[1, s] * 2 + time[s]].astype(F32)
        gr = (one[0] * two[0] + one[1] * two[1]) * weight
        gi = (one[1] * two[0] - one[0] * two[1]) * weight
        pr, pi = px[s, 0], px[s, 1]
        at = pl.multiple_of(s * 32, 32)
        corr[pl.ds(at, 16), :] = pr * gr - pi * gi
        corr[pl.ds(at + 16, 16), :] = pr * gi + pi * gr
        return 0

    lax.fori_loop(0, 128, correct, 0, unroll=4)

    def coarse(group, _):
        for f in range(2):
            base = group * 16 * 32 + f
            re = [corr[pl.ds(base + 2 * p, 16, stride=32), :] for p in range(8)]
            im = [corr[pl.ds(base + 16 + 2 * p, 16, stride=32), :] for p in range(8)]
            re, im = dft8(re, im)
            rows = pl.ds(pl.multiple_of(f * 128 + group * 16, 16), 16)
            for k in range(8):
                lhi[k, rows, :128], llo[k, rows, :128] = split(re[k])
                lhi[k, rows, 128:], llo[k, rows, 128:] = split(im[k])
        return 0

    lax.fori_loop(0, 8, coarse, 0)
    loads[2].wait()
    loads[3].wait()

    early, late = pl.ds(0, 32), pl.ds(32, 32)
    pl.semaphore_wait(barrier, 127)

    def fine(i, _):
        k = lax.rem(i + lax.div(mine, 16), 8)
        a = jnp.where(k == 0, 0, jnp.where(k == 1, 4, lax.div(k, 2)))
        b = jnp.where(k < 2, a, 8 - a)
        acc = None
        for half, at in enumerate((a, b)):
            h = bh[k, half]
            term = dot(lhi[at], h) + dot(llo[at], h) + dot(lhi[at], bl[k, half])
            acc = term if acc is None else acc + term
        hi, lo = split(acc)
        for f in range(2):
            rows = slice(f * 128, f * 128 + 128)
            padded = dot(perm[...], jnp.concatenate([hi[rows], lo[rows]], axis=0))
            for p in range(2):
                for q in range(4):
                    send[(k * 4 + p * 2 + f) * 4 + q] = (
                        padded[q * 64:(q + 1) * 64, p * 128:(p + 1) * 128]
                    )
        for n in range(16):
            o = n * 7 % 16
            tx, ty = lax.rem(x + o // 4, 4), lax.rem(y + o % 4, 4)
            tz = lax.rem(lax.div(k, 2) + 8 - tx - ty, 4)
            dev = (tx * 4 + ty, tz * 2 + lax.rem(k, 2))
            if o > 0:
                push(send.at[k * 16 + dev[0], early], recv.at[me, early], 1, dev)
            else:
                @pl.when(i > 0)
                def _(dev=dev):
                    push(send.at[k * 16 + dev[0], early], recv.at[me, early], 1, dev)

        return 0

    lax.fori_loop(0, 8, fine, 0)
    each(lambda d, dev: push(tabs.at[lax.rem(dev[0], 4)], tabr.at[me], 0, dev))
    each(lambda d, dev: push(send.at[unit_of(*dev), late], recv.at[me, late], 2, dev))
    keep(tabs.at[y], tabr.at[me])
    keep(send.at[mine], recv.at[me])
    flat = recv.reshape(128 * 64, 128)

    for load in loads[4:9]:
        load.wait()
    wait(tabr.at[pl.ds(0, 127)], rsem.at[0])
    tabt[...] = tabr[...].reshape(128, 128).T
    lane = lax.broadcasted_iota(I32, (32, 128), 1)
    low = lane < 64

    shifted = first & (lax.broadcasted_iota(I32, (64, 128), 1) < 64)

    def columns(pm, t):
        g = ghl[pm, pl.ds(pl.multiple_of(t * 256, 256), 256), :]
        for c in range(4):
            rows = slice(c * 128, c * 128 + 128)
            a = dot(wh[rows, :], g)
            b = dot(wl[rows, :], g[:, :128])
            u = a[:, :128] + a[:, 128:] + b
            ur, ui = u[:64], u[64:]
            m0 = slice(c * 64, c * 64 + 64)
            tr, ti = twr[m0, :], twi[m0, :]
            for lanes, value in (
                (slice(0, 128), tr * ur - ti * ui), (slice(128, 256), tr * ui + ti * ur)
            ):
                if pm == 1:
                    value, held[m0, lanes] = jnp.where(shifted, held[m0, lanes], value), value
                pqh[pm, m0, lanes], pql[pm, m0, lanes] = split(value)

    def mix(which, pm):
        both = fmat[kind, which]
        z = dot_nt(both, pqh[pm])
        return z[:128] + z[128:] + dot_nt(both[:128], pql[pm])

    def turn(z, pm, tile):
        lanes = slice(tile * 128, tile * 128 + 128)
        re, im = z[pm * 64:pm * 64 + 32, lanes], z[pm * 64 + 32:pm * 64 + 64, lanes]
        return (
            jnp.where(low, re, pltpu.roll(im, 64, 1)), jnp.where(low, pltpu.roll(re, 64, 1), im)
        )

    def emit(z, row):
        for pm in range(2):
            for tile in range(2):
                for q, rows in enumerate(turn(z, pm, tile)):
                    stage[pl.ds((2 * tile + q) * 64 + row + pm, 32, stride=256), :] = rows

    def gather(rp):
        for pm in range(2):
            def block(c, _, pm=pm):
                at = rp * 32 + pm * 16 + 2 * c
                key = jnp.concatenate([tabt[pl.ds(at + k, 1), :] for k in range(2)], axis=1)
                parts = [split(flat[pl.ds(at + k, 128, stride=64), :]) for k in range(2)]
                rhs = jnp.concatenate([jnp.concatenate(p, axis=1) for p in parts], axis=0)
                for chunk in range(4):
                    tile = lax.broadcasted_iota(I32, (128, 256), 0) + chunk * 128
                    hit = jnp.where(tile == key, 1.0, 0.0).astype(BF)
                    s = dot(hit, rhs)
                    hi, lo = split(s[:, :128] + s[:, 128:])
                    for i in range(4):
                        to = pl.multiple_of((chunk * 4 + i) * 256 + c * 32, 32)
                        ghl[pm, pl.ds(to, 32), :128] = hi[i * 32:i * 32 + 32]
                        ghl[pm, pl.ds(to, 32), 128:] = lo[i * 32:i * 32 + 32]
                return 0

            lax.fori_loop(0, 8, block, 0)
        held[...] = jnp.zeros((256, 256), F32)

    def phase(p, _):
        rp, half = lax.div(p, 2), lax.rem(p, 2)

        @pl.when(half == 0)
        def _():
            gather(rp)

        def row(i, _):
            t = half * 8 + i

            columns(0, t)
            columns(1, 15 - t)
            emit(mix(0, 0) + mix(1, 1), rp * 32 + 2 * t)
            return 0

        lax.fori_loop(0, 8, row, 0)

        @pl.when(first & (half == 1))
        def _():
            for lanes in (slice(0, 128), slice(128, 256)):
                pqh[1, :, lanes], pql[1, :, lanes] = split(held[:, lanes])
            edge = mix(1, 1)
            for tile in range(2):
                for q, rows in enumerate(turn(edge, 0, tile)):
                    for m in range(32):
                        extra[m * 4 + 2 * tile + q, pl.ds(rp, 1), :] = rows[m:m + 1]

        @pl.when(p == 1)
        def _():
            def piece(d):
                return stage.at[pl.ds(pl.multiple_of(d * 64, 64), 32), :]

            wait(recv.at[pl.ds(0, 127), late], rsem.at[2])
            each(lambda d, dev: push(piece(d), got.at[mine, early], 4, dev))
            keep(piece(me), got.at[mine, early])

        @pl.when(p > 1)
        def _():
            rows = pl.ds(pl.multiple_of(p * 16, 16), 16)

            def piece(d):
                return stage.at[pl.ds(pl.multiple_of(d * 64 + p * 16, 16), 16), :]

            each(lambda d, dev: push(piece(d), got.at[mine, rows], 3 + p, dev))
            keep(piece(me), got.at[mine, rows])

        return 0

    wait(recv.at[pl.ds(0, 127), early], rsem.at[1])
    lax.fori_loop(0, 4, phase, 0)

    @pl.when(first)
    def _():
        each(lambda d, dev: push(extra.at[d], gotx.at[mine], 3, dev))
        keep(extra.at[me], gotx.at[mine])

    wait(send.at[pl.ds(0, 127), early], ssem.at[1])
    wait(send.at[pl.ds(0, 127), late], ssem.at[2])
    for load in loads[9:]:
        load.wait()
    wait(got.at[pl.ds(0, 127), early], rsem.at[4])

    def transform(n, _, rp):
        f, group = lax.div(n, 4), lax.rem(n, 4)
        rows = slice(rp * 32, rp * 32 + 32)
        turned = row_dft(
            [[got[((4 * group + k) * 2 + f) * 4 + q, rows, :] for q in range(4)] for k in range(4)],
            (wrh.at[rp], wrl.at[rp]), tj, group,
        )

        def add(k, v):
            at = n * 16 + k
            send[at] = v if rp == 0 else send[at] + v

        for k in range(4, 16):
            add(k, turned[k])

        @pl.when(group > 0)
        def _():
            for k in range(4):
                add(k, turned[k])

        @pl.when(group == 0)
        def _():
            zero = row_dft_zero(
                [got[f * 4 + q, rows, :] for q in range(4)], (wsh.at[rp], wsl.at[rp])
            )
            if rp == 1:
                for q in range(4):
                    edges[2 * q:2 * q + 2, :] = gotx[f * 4 + q]
                edge = jnp.concatenate([edges[...], jnp.zeros((120, 128), F32)], axis=0).T[:, :32]
                v = three(edge[:64], (xh[0], xl[0])) + three(edge[64:], (xh[1], xl[1]))
                zero = [a + b for a, b in zip(zero, halves(v[:, :256], v[:, 256:]))]
            for k in range(4):
                add(k, zero[k])

        return 0

    lax.fori_loop(0, 8, functools.partial(transform, rp=0), 0)

    @pl.when(first)
    def _():
        wait(gotx.at[pl.ds(0, 7)], rsem.at[3])

    @pl.when(mine >= 8)
    def _():
        wait(gotx, rsem.at[3])

    for p in range(2):
        wait(got.at[pl.ds(0, 127), pl.ds(p * 16, 16)], rsem.at[5 + p])

    def picture(f, _):
        lax.fori_loop(4 * f, 4 * f + 4, functools.partial(transform, rp=1), 0)

        def strip(i, _):
            at = pl.ds(pl.multiple_of(i * 8, 8), 8)
            for tile in range(2):
                mixed = mix_pairs(lambda k, part: send[f * 64 + 4 * k + 2 * part + tile, at, :])
                for l, value in mixed:
                    image[f, at, l * 256 + tile * 128:l * 256 + tile * 128 + 128] = value
            pltpu.make_async_copy(image.at[f, at, :], out.at[f, at, :], lsem).start()
            return 0

        lax.fori_loop(0, 8, strip, 0)
        return 0

    lax.fori_loop(0, 2, picture, 0)
    wait(out, lsem)
    @pl.when(first)
    def _():
        wait(extra.at[pl.ds(0, 127)], ssem.at[3])

    wait(tabr.at[pl.ds(0, 127)], ssem.at[0])
    wait(got.at[pl.ds(0, 127), early], ssem.at[4])
    for p in range(2):
        wait(got.at[pl.ds(0, 127), pl.ds(p * 16, 16)], ssem.at[5 + p])


def exchange(tiles, pair, time, chan, count, weights, pixels, beams):
    t = tables()
    smem = pl.BlockSpec(memory_space=pltpu.SMEM)
    away = pl.BlockSpec(memory_space=pl.ANY)
    constants = (*t["b"], *t["wc"], *t["tw"], t["f"], *t["wr"], *t["ws"], *t["wx"], t["tj"])
    return pl.pallas_call(
        exchange_kernel,
        out_shape=jax.ShapeDtypeStruct((2, 64, 8192), F32),
        in_specs=[pl.BlockSpec(memory_space=pltpu.VMEM)] + [smem] * 5 + [away] * 16,
        out_specs=away,
        scratch_shapes=[
            pltpu.VMEM((128, 2, 16, 128), F32),
            pltpu.VMEM((1024, 2, 16, 128), BF),
            pltpu.VMEM((8, 2, 256, 256), BF),
            pltpu.VMEM((8, 2, 256, 256), BF),
            pltpu.VMEM((512, 256), BF),
            pltpu.VMEM((512, 256), BF),
            pltpu.VMEM((256, 128), F32),
            pltpu.VMEM((256, 128), F32),
            pltpu.VMEM((2, 2, 256, 256), BF),
            pltpu.VMEM((2, 128, 512), BF),
            pltpu.VMEM((2, 128, 512), BF),
            pltpu.VMEM((2, 2, 128, 512), BF),
            pltpu.VMEM((2, 2, 128, 512), BF),
            pltpu.VMEM((2, 32, 512), BF),
            pltpu.VMEM((2, 32, 512), BF),
            pltpu.VMEM((16, 2, 256), F32),
            pltpu.VMEM((128 * 32, 128), F32),
            pltpu.VMEM((8, 256, 256), BF),
            pltpu.VMEM((8, 256, 256), BF),
            pltpu.VMEM((256, 256), BF),
            pltpu.VMEM((128, 64, 128), F32),
            pltpu.VMEM((4, 1, 128), I32),
            pltpu.VMEM((128, 64, 128), F32),
            pltpu.VMEM((128, 1, 128), I32),
            pltpu.VMEM((128, 128), I32),
            pltpu.VMEM((2, 16 * 256, 256), BF),
            pltpu.VMEM((2, 256, 256), BF),
            pltpu.VMEM((2, 256, 256), BF),
            pltpu.VMEM((256, 256), F32),
            pltpu.VMEM((128 * 64, 128), F32),
            pltpu.VMEM((128, 2, 128), F32),
            pltpu.VMEM((128, 64, 128), F32),
            pltpu.VMEM((8, 2, 128), F32),
            pltpu.VMEM((8, 128), F32),
            pltpu.VMEM((2, 64, 8192), F32),
            pltpu.SemaphoreType.DMA((8,)),
            pltpu.SemaphoreType.DMA((8,)),
            pltpu.SemaphoreType.DMA,
            pltpu.SemaphoreType.DMA((16,)),
        ],
        compiler_params=pltpu.CompilerParams(
            vmem_limit_bytes=VMEM, collective_id=0, has_side_effects=True
        ),
        name="exchange",
    )(tiles, pair, time, chan, count, weights, pixels, beams, *constants)


def pixel_view(pixels):
    x = pixels.reshape(128, 2, 2, 8, 128).transpose(0, 1, 3, 2, 4)
    return x.reshape(128, 2, 16, 128)


def beam_view(aterms):
    x = aterms.reshape(512, 2, 2, 2, 8, 128).transpose(0, 1, 2, 4, 3, 5)
    return x.reshape(1024, 2, 16, 128)


def local(
    subgrid_pixels, tile_offsets, station_pairs, time_blocks, channel_blocks, valid_counts,
    aterms, channel_weights,
):
    return exchange(
        tile_offsets.T, station_pairs.T, time_blocks, channel_blocks, valid_counts, channel_weights,
        pixel_view(subgrid_pixels), beam_view(aterms),
    )


def solution(mesh):
    in_specs = (
        P(("row", "col"), None, None, None),
        P(("row", "col"), None),
        P(("row", "col"), None),
        P(("row", "col")),
        P(("row", "col")),
        P(("row", "col")),
        P(),
        P(),
    )
    out_specs = P(None, ("row", "col"), None)
    return jax.shard_map(local, mesh=mesh, in_specs=in_specs, out_specs=out_specs, check_vma=False)
```

```python
import functools
import math

import jax
import jax.numpy as jnp
import ml_dtypes
import numpy as np
from jax import lax
from jax.experimental import pallas as pl
from jax.experimental.pallas import tpu as pltpu
from jax.sharding import PartitionSpec as P

BF = jnp.bfloat16
F32 = jnp.float32
I32 = jnp.int32

PAIR_J = (0, 8, 4, 12, 1, 9, 17, 25, 2, 10, 18, 26, 3, 11, 19, 27)
VMEM = 56 * 1024 * 1024


def partner(j):
    return 16 if j == 0 else 32 - j


def unit(turns):
    return np.exp(-2j * np.pi * turns)


def split_np(x):
    hi = np.asarray(x, np.float32).astype(ml_dtypes.bfloat16)
    lo = (np.asarray(x, np.float64) - hi.astype(np.float64)).astype(ml_dtypes.bfloat16)
    return hi, lo


def split(x):
    hi = x.astype(BF)
    return hi, (x - hi.astype(F32)).astype(BF)


def dot(a, b):
    return lax.dot_general(a, b, (((1,), (0,)), ((), ())), preferred_element_type=F32)


def dot_nt(a, b):
    return lax.dot_general(a, b, (((1,), (1,)), ((), ())), preferred_element_type=F32)


@functools.lru_cache(None)
def tables():
    xi = np.arange(4)[:, None, None]
    y = np.arange(32)[None, :, None]
    v = np.arange(32)[None, None, :]
    b = np.zeros((8, 2, 2, 4, 32, 2, 2, 2, 32))
    for step in range(8):
        for pair in range(2):
            j = PAIR_J[2 * step + pair]
            for half, jj in enumerate((j, partner(j))):
                w = unit((xi * jj + y * v) % 32 / 32) / 32
                b[step, half, 0, :, :, pair, half, 0] = w.real
                b[step, half, 0, :, :, pair, half, 1] = w.imag
                b[step, half, 1, :, :, pair, half, 0] = -w.imag
                b[step, half, 1, :, :, pair, half, 1] = w.real
    b = b.reshape(8, 2, 256, 256)
    i = np.arange(256)
    w = unit(i[:, None] * i[None, :] % 256 / 256)
    wc = np.stack([w.real.reshape(4, 64, 256), w.imag.reshape(4, 64, 256)], 1).reshape(512, 256)
    tw = unit(i[:, None] * (np.arange(128) % 32)[None, :] / 8192)
    d = unit(np.arange(32)[:, None] * np.arange(32)[None, :] % 32 / 32)
    coef = np.stack([np.stack([d, 1j * d]), np.stack([1j * d, -d])])
    f = np.zeros((2, 2, 2, 2, 32, 2, 2, 2, 32))

    def put(kind, which, half, pm, conj):
        for pq in range(2):
            for reim in range(2):
                c = coef[pq, reim]
                f[kind, which, pm, 0, :, pq, half, reim, :] = c.real
                f[kind, which, pm, 1, :, pq, half, reim, :] = -c.imag if conj else c.imag

    put(0, 0, 0, 0, False)
    put(0, 0, 1, 1, True)
    put(0, 1, 1, 0, True)
    put(0, 1, 0, 1, False)
    put(1, 0, 0, 0, False)
    put(1, 0, 1, 1, False)
    put(1, 1, 1, 1, True)
    put(1, 1, 0, 0, True)
    f = f.reshape(2, 2, 128, 256)
    fh, fl = split_np(f)
    f = np.concatenate([fh, fl], axis=2)
    k = np.arange(256)
    q, rp, t, pm = k // 64, k // 32 % 2, k // 2 % 16, k % 2
    r = 16 * (2 * q + rp) + t
    rr = np.where(pm == 0, r, 255 - r)
    l0 = np.arange(256)
    w = unit(rr[:, None] * l0[None, :] % 256 / 256) / 4096
    wr = np.concatenate([w.real, w.imag], axis=1)
    w0 = np.where((pm == 0)[:, None], unit(r[:, None] * l0[None, :] % 256 / 256), 0) / 4096
    w16 = np.where((pm == 1)[:, None], unit((32 * r[:, None] + 16) * l0[None, :] % 8192 / 8192), 0) / 4096
    ws = np.stack([np.concatenate([w0.real, w16.real], 1), np.concatenate([-w0.imag, -w16.imag], 1)])
    kx = np.arange(32)
    qx, row = kx // 2 % 4, kx % 2
    rx = 16 * (15 - (2 * qx + row))
    wx = np.where((kx < 8)[:, None], unit(-(rx[:, None] * l0[None, :] % 256) / 256), 0) / 4096
    zero = np.zeros_like(wx.real)
    wx = np.stack([np.concatenate([wx.real, zero], 1), np.concatenate([-wx.imag, zero], 1)])
    tj = unit(np.array(PAIR_J)[:, None] * l0[None, :] / 8192)
    tj = np.stack([tj.real, tj.imag], 1).astype(np.float32)
    wr, ws = wr.reshape(4, 2, 32, 512), ws.reshape(2, 4, 2, 32, 512)
    late = [w.reshape(*w.shape[:-2], 16, 2, 512) for w in (wr[:, 1], ws[:, :, 1])]
    wr = split_np(wr[:, 0].reshape(128, 512))
    ws = split_np(ws[:, :, 0].reshape(2, 128, 512))

    def doubled(w):
        h, l = split_np(w)
        shape = (*w.shape[:-4], 256, 512)
        return (
            np.stack([h, h], axis=-4).reshape(shape),
            np.stack([l, np.zeros_like(l)], axis=-4).reshape(shape),
        )

    vr = doubled(late[0].transpose(2, 0, 1, 3))
    vs = doubled(late[1].transpose(0, 3, 1, 2, 4))
    return dict(
        b=split_np(b), wc=split_np(wc), tw=(tw.real.astype(np.float32), tw.imag.astype(np.float32)),
        f=f, wr=wr, ws=ws, vr=vr, vs=vs, wx=split_np(wx), tj=tj,
    )


def dft8(re, im):
    h = math.sqrt(0.5)

    def four(a, b):
        s0r, s0i = a[0] + a[2], b[0] + b[2]
        s1r, s1i = a[0] - a[2], b[0] - b[2]
        s2r, s2i = a[1] + a[3], b[1] + b[3]
        s3r, s3i = a[1] - a[3], b[1] - b[3]
        return (
            [s0r + s2r, s1r + s3i, s0r - s2r, s1r - s3i],
            [s0i + s2i, s1i - s3r, s0i - s2i, s1i + s3r],
        )

    er, ei = four(re[0::2], im[0::2])
    orr, oi = four(re[1::2], im[1::2])
    tr = [orr[0], (orr[1] + oi[1]) * h, oi[2], (oi[3] - orr[3]) * h]
    ti = [oi[0], (oi[1] - orr[1]) * h, -orr[2], -(oi[3] + orr[3]) * h]
    return (
        [er[k] + tr[k] for k in range(4)] + [er[k] - tr[k] for k in range(4)],
        [ei[k] + ti[k] for k in range(4)] + [ei[k] - ti[k] for k in range(4)],
    )


def place(tiles, count, tabs):
    row, col = tiles[0:1, :], tiles[1:2, :]
    block_row = lax.shift_right_logical(row, 4)
    low = block_row < 8
    near = jnp.where(low, block_row, 15 - block_row)
    block = (near * 2 + jnp.where(low, 0, 1)) * 8 + lax.shift_right_logical(col, 5)
    tile = (row & 15) * 32 + (col & 31)
    down = lax.broadcasted_iota(I32, (128, 128), 0)
    along = lax.broadcasted_iota(I32, (128, 128), 1)

    def column(x):
        return jnp.broadcast_to(x, (128, 128)).T

    earlier = (column(block) == block) & (down < along)
    rank = jnp.sum(jnp.where(earlier, 1.0, 0.0), axis=0, keepdims=True)
    slot = block * 2 + jnp.where(rank > 0.5, 1, 0)
    slot = jnp.where(along[0:1] < count, slot, -1)
    slots, tile = column(slot), column(tile).astype(F32)
    for q in range(4):
        tabs[q] = jnp.sum(jnp.where(slots == along + 64 * q, tile, 0.0), axis=0, keepdims=True).astype(I32)
    hit = jnp.where(lax.broadcasted_iota(I32, (256, 128), 0) == slot, 1.0, 0.0).astype(BF)
    return jnp.concatenate([hit, hit], axis=1)


def three(a, b):
    ah, al = split(a)
    return dot(ah, b[0]) + dot(al, b[0]) + dot(ah, b[1])


def halves(re, im):
    return [re[:, :128], re[:, 128:], im[:, :128], im[:, 128:]]


def row_dft(blocks, w, tj, group):
    a = jnp.concatenate([jnp.concatenate(b, axis=0).T for b in blocks], axis=0)
    u = three(a, (w[0][...], w[1][...]))
    outs = []
    for k in range(4):
        v = u[k * 128:k * 128 + 128]
        vr = v[:64, :256] - v[64:, 256:]
        vi = v[:64, 256:] + v[64:, :256]
        tr, ti = tj[4 * group + k, 0:1, :], tj[4 * group + k, 1:2, :]
        outs += halves(vr * tr - vi * ti, vr * ti + vi * tr)
    return outs


def row_dft_zero(block, w):
    a = jnp.concatenate(block, axis=0).T
    v = three(a[:64], (w[0][0], w[1][0])) + three(a[64:], (w[0][1], w[1][1]))
    return halves(v[:, :256], v[:, 256:])


def mix_pairs(load):
    index = {}
    for i, j in enumerate(PAIR_J):
        if i > 0:
            index[j if j < 16 else 32 - j] = (i, 1.0 if j < 16 else -1.0)
    zero, mid = load(0, 0), load(0, 1)
    re = {j: load(k, 0) for j, (k, _) in index.items()}
    im = {j: load(k, 1) for j, (k, _) in index.items()}

    def wave(fun, part, js, l1, signed):
        total = jnp.zeros((8, 128), F32)
        started = False
        for j in js:
            c = fun(2 * math.pi * (j * l1 % 32) / 32) * (index[j][1] if signed else 1.0)
            if abs(c) < 1e-12:
                continue
            term = part[j] if abs(abs(c) - 1) < 1e-12 else part[j] * abs(c)
            if started:
                total = total + term if c > 0 else total - term
            else:
                total = term if c > 0 else -term
            started = True
        return total

    odd, even, four = range(1, 16, 2), (2, 6, 10, 14), (4, 8, 12)
    ce, se = [None] * 9, [None] * 9
    for l1 in range(5):
        ee = wave(math.cos, re, four, l1, False) + (zero + mid if l1 % 2 == 0 else zero - mid)
        eo = wave(math.cos, re, even, l1, False)
        oe = wave(math.sin, im, four, l1, True)
        oo = wave(math.sin, im, even, l1, True)
        ce[l1], ce[8 - l1] = ee + eo, ee - eo
        se[l1], se[8 - l1] = oe + oo, oo - oe
    outs = []
    for l1 in range(9):
        co = wave(math.cos, re, odd, l1, False)
        so = wave(math.sin, im, odd, l1, True)
        p, m = ce[l1] + co, ce[l1] - co
        s, d = se[l1] + so, se[l1] - so
        outs += [(l1, p + s), (16 + l1, m + d)]
        if l1 > 0:
            outs.append((32 - l1, p - s))
            if l1 < 8:
                outs.append((16 - l1, m - d))
    return outs


def exchange_kernel(
    tiles, pair, time, chan, vc, cw, pixels_hbm, beams_hbm, bh_hbm, bl_hbm,
    wh_hbm, wl_hbm, twr_hbm, twi_hbm, fmat_hbm,
    wrh_hbm, wrl_hbm, wsh_hbm, wsl_hbm, vrh_hbm, vrl_hbm, vsh_hbm, vsl_hbm, xh_hbm, xl_hbm, tj_hbm, out,
    px, beams, bh, bl, wh, wl, twr, twi, fmat, wrh, wrl, wsh, wsl, vrh, vrl, vsh, vsl, xh, xl, tj,
    corr, lhi, llo, perm, send, tabs,
    recv, tabr, tabt, ghl, pqh, pql, held, stage, extra, got, gotx, edges, image, ssem, rsem, lsem, csem
):
    line, column = lax.axis_index("row"), lax.axis_index("col")
    x, y = lax.div(line, 4), lax.rem(line, 4)
    z, core = lax.div(column, 2), lax.rem(column, 2)
    me = line * 8 + column

    def unit_of(row, col):
        turn = lax.rem(lax.div(row, 4) + row + lax.div(col, 2), 4)
        return (turn * 2 + lax.rem(col, 2)) * 16 + row

    mine = unit_of(line, column)
    first = mine < 8
    kind = jnp.where(first, 1, 0)
    barrier = pltpu.get_barrier_semaphore()
    loads = [
        pltpu.make_async_copy(src, dst, csem.at[i])
        for i, (src, dst) in enumerate((
            (beams_hbm, beams), (pixels_hbm, px), (bh_hbm, bh), (bl_hbm, bl), (wh_hbm, wh),
            (wl_hbm, wl), (twr_hbm, twr), (twi_hbm, twi), (fmat_hbm, fmat),
            (wrh_hbm, wrh), (wrl_hbm, wrl), (wsh_hbm, wsh), (wsl_hbm, wsl),
            (vrh_hbm, vrh), (vrl_hbm, vrl), (vsh_hbm, vsh), (vsl_hbm, vsl),
            (xh_hbm, xh), (xl_hbm, xl), (tj_hbm, tj),
        ))
    ]
    for load in loads:
        load.start()

    cols = [lax.rem(z + b // 2, 4) * 2 + lax.rem(core + b, 2) for b in range(8)]

    def each(fun):
        def step(a, _):
            def one(b):
                o = lax.rem(a + 5 * b, 16)
                row = lax.rem(x + lax.div(o, 4), 4) * 4 + lax.rem(y + o, 4)
                fun(row * 8 + cols[b], (row, cols[b]))

            for b in (3, 6, 1, 4, 7, 2, 5):
                one(b)

            @pl.when(a > 0)
            def _():
                one(0)

            return 0

        lax.fori_loop(0, 16, step, 0)

    def push(src, dst, k, dev):
        pltpu.make_async_remote_copy(
            src_ref=src, dst_ref=dst, send_sem=ssem.at[k], recv_sem=rsem.at[k],
            device_id=dev, device_id_type=pl.DeviceIdType.MESH,
        ).start()

    def wait(part, sem):
        pltpu.make_async_copy(part, part, sem).wait()

    def keep(src, dst):
        copy = pltpu.make_async_copy(src, dst, lsem)
        copy.start()
        copy.wait()

    each(lambda d, dev: pl.semaphore_signal(
        barrier, inc=1, device_id=dev, device_id_type=pl.DeviceIdType.MESH))
    perm[...] = place(tiles, vc[0], tabs)
    loads[0].wait()
    loads[1].wait()

    def correct(s, _):
        weight = jnp.where(s < vc[0], cw[chan[s]], 0.0)
        one = beams[pair[0, s] * 2 + time[s]].astype(F32)
        two = beams[pair[1, s] * 2 + time[s]].astype(F32)
        gr = (one[0] * two[0] + one[1] * two[1]) * weight
        gi = (one[1] * two[0] - one[0] * two[1]) * weight
        pr, pi = px[s, 0], px[s, 1]
        at = pl.multiple_of(s * 32, 32)
        corr[pl.ds(at, 16), :] = pr * gr - pi * gi
        corr[pl.ds(at + 16, 16), :] = pr * gi + pi * gr
        return 0

    lax.fori_loop(0, 128, correct, 0, unroll=4)

    def coarse(group, _):
        for f in range(2):
            base = group * 16 * 32 + f
            re = [corr[pl.ds(base + 2 * p, 16, stride=32), :] for p in range(8)]
            im = [corr[pl.ds(base + 16 + 2 * p, 16, stride=32), :] for p in range(8)]
            re, im = dft8(re, im)
            rows = pl.ds(pl.multiple_of(f * 128 + group * 16, 16), 16)
            for k in range(8):
                lhi[k, rows, :128], llo[k, rows, :128] = split(re[k])
                lhi[k, rows, 128:], llo[k, rows, 128:] = split(im[k])
        return 0

    lax.fori_loop(0, 8, coarse, 0)
    loads[2].wait()
    loads[3].wait()

    early, late = pl.ds(0, 32), pl.ds(32, 32)
    pl.semaphore_wait(barrier, 127)

    def fine(i, _):
        k = lax.rem(i + lax.div(mine, 16), 8)
        a = jnp.where(k == 0, 0, jnp.where(k == 1, 4, lax.div(k, 2)))
        b = jnp.where(k < 2, a, 8 - a)
        acc = None
        for half, at in enumerate((a, b)):
            h = bh[k, half]
            term = dot(lhi[at], h) + dot(llo[at], h) + dot(lhi[at], bl[k, half])
            acc = term if acc is None else acc + term
        hi, lo = split(acc)
        for f in range(2):
            rows = slice(f * 128, f * 128 + 128)
            padded = dot(perm[...], jnp.concatenate([hi[rows], lo[rows]], axis=0))
            for p in range(2):
                for q in range(4):
                    send[(k * 4 + p * 2 + f) * 4 + q] = (
                        padded[q * 64:(q + 1) * 64, p * 128:(p + 1) * 128]
                    )
        for n in range(16):
            o = n * 7 % 16
            tx, ty = lax.rem(x + o // 4, 4), lax.rem(y + o % 4, 4)
            tz = lax.rem(lax.div(k, 2) + 8 - tx - ty, 4)
            dev = (tx * 4 + ty, tz * 2 + lax.rem(k, 2))
            if o > 0:
                push(send.at[k * 16 + dev[0], early], recv.at[me, early], 1, dev)
            else:
                @pl.when(i > 0)
                def _(dev=dev):
                    push(send.at[k * 16 + dev[0], early], recv.at[me, early], 1, dev)

        return 0

    lax.fori_loop(0, 8, fine, 0)
    each(lambda d, dev: push(tabs.at[lax.rem(dev[0], 4)], tabr.at[me], 0, dev))
    each(lambda d, dev: push(send.at[unit_of(*dev), late], recv.at[me, late], 2, dev))
    keep(tabs.at[y], tabr.at[me])
    keep(send.at[mine], recv.at[me])
    flat = recv.reshape(128 * 64, 128)

    for load in loads[4:9]:
        load.wait()
    wait(tabr.at[pl.ds(0, 127)], rsem.at[0])
    tabt[...] = tabr[...].reshape(128, 128).T
    lane = lax.broadcasted_iota(I32, (32, 128), 1)
    low = lane < 64
    even = (lane & 32) == 0

    shifted = first & (lax.broadcasted_iota(I32, (64, 128), 1) < 64)

    def columns(pm, t):
        g = ghl[pm, pl.ds(pl.multiple_of(t * 256, 256), 256), :]
        for c in range(4):
            rows = slice(c * 128, c * 128 + 128)
            a = dot(wh[rows, :], g)
            b = dot(wl[rows, :], g[:, :128])
            u = a[:, :128] + a[:, 128:] + b
            ur, ui = u[:64], u[64:]
            m0 = slice(c * 64, c * 64 + 64)
            tr, ti = twr[m0, :], twi[m0, :]
            for lanes, value in (
                (slice(0, 128), tr * ur - ti * ui), (slice(128, 256), tr * ui + ti * ur)
            ):
                if pm == 1:
                    value, held[m0, lanes] = jnp.where(shifted, held[m0, lanes], value), value
                pqh[pm, m0, lanes], pql[pm, m0, lanes] = split(value)

    def mix(which, pm):
        both = fmat[kind, which]
        z = dot_nt(both, pqh[pm])
        return z[:128] + z[128:] + dot_nt(both[:128], pql[pm])

    def turn(z, pm, tile):
        lanes = slice(tile * 128, tile * 128 + 128)
        re, im = z[pm * 64:pm * 64 + 32, lanes], z[pm * 64 + 32:pm * 64 + 64, lanes]
        return (
            jnp.where(low, re, pltpu.roll(im, 64, 1)), jnp.where(low, pltpu.roll(re, 64, 1), im)
        )

    def emit(z, t):
        for pm in range(2):
            for tile in range(2):
                for q, rows in enumerate(turn(z, pm, tile)):
                    stage[pl.ds((2 * tile + q) * 64 + 2 * t + pm, 32, stride=256), :] = rows

    def emit_by_m(z, t):
        for tile in range(2):
            a = [z[i * 32:i * 32 + 32, tile * 128:tile * 128 + 128] for i in range(4)]
            c = [
                jnp.where(low, a[0], pltpu.roll(a[2], 64, 1)), jnp.where(low, a[1], pltpu.roll(a[3], 64, 1)),
                jnp.where(low, pltpu.roll(a[0], 64, 1), a[2]), jnp.where(low, pltpu.roll(a[1], 64, 1), a[3]),
            ]
            for q in range(2):
                b = (
                    jnp.where(even, c[2 * q], pltpu.roll(c[2 * q + 1], 32, 1)),
                    jnp.where(even, pltpu.roll(c[2 * q], 96, 1), c[2 * q + 1]),
                )
                for h in range(2):
                    at = (2 * tile + q) * 64 + 32 + 16 * h
                    stage[pl.ds(at + t, 32, stride=256), :] = b[h]

    def gather(rp):
        for pm in range(2):
            def block(c, _, pm=pm):
                at = rp * 32 + pm * 16 + 2 * c
                key = jnp.concatenate([tabt[pl.ds(at + k, 1), :] for k in range(2)], axis=1)
                parts = [split(flat[pl.ds(at + k, 128, stride=64), :]) for k in range(2)]
                rhs = jnp.concatenate([jnp.concatenate(p, axis=1) for p in parts], axis=0)
                for chunk in range(4):
                    tile = lax.broadcasted_iota(I32, (128, 256), 0) + chunk * 128
                    hit = jnp.where(tile == key, 1.0, 0.0).astype(BF)
                    s = dot(hit, rhs)
                    hi, lo = split(s[:, :128] + s[:, 128:])
                    for i in range(4):
                        to = pl.multiple_of((chunk * 4 + i) * 256 + c * 32, 32)
                        ghl[pm, pl.ds(to, 32), :128] = hi[i * 32:i * 32 + 32]
                        ghl[pm, pl.ds(to, 32), 128:] = lo[i * 32:i * 32 + 32]
                return 0

            lax.fori_loop(0, 8, block, 0)
        held[...] = jnp.zeros((256, 256), F32)

    def phase(rp):
        gather(rp)

        def row(t, _):
            columns(0, t)
            columns(1, 15 - t)
            z = mix(0, 0) + mix(1, 1)
            if rp == 0:
                emit(z, t)
            else:
                emit_by_m(z, t)
            return 0

        lax.fori_loop(0, 16, row, 0)

        @pl.when(first)
        def _():
            for lanes in (slice(0, 128), slice(128, 256)):
                pqh[1, :, lanes], pql[1, :, lanes] = split(held[:, lanes])
            edge = mix(1, 1)
            for tile in range(2):
                for q, rows in enumerate(turn(edge, 0, tile)):
                    for m in range(32):
                        extra[m * 4 + 2 * tile + q, rp:rp + 1, :] = rows[m:m + 1]

    def deliver(start, size, k):
        rows = pl.ds(start, size)

        def piece(d):
            return stage.at[pl.ds(pl.multiple_of(d * 64 + start, 16), size), :]

        each(lambda d, dev: push(piece(d), got.at[mine, rows], k, dev))
        keep(piece(me), got.at[mine, rows])

    wait(recv.at[pl.ds(0, 127), early], rsem.at[1])
    phase(0)
    wait(recv.at[pl.ds(0, 127), late], rsem.at[2])
    deliver(0, 32, 4)
    phase(1)
    deliver(32, 16, 5)
    deliver(48, 16, 6)

    @pl.when(first)
    def _():
        each(lambda d, dev: push(extra.at[d], gotx.at[mine], 3, dev))
        keep(extra.at[me], gotx.at[mine])

    wait(send.at[pl.ds(0, 127), early], ssem.at[1])
    wait(send.at[pl.ds(0, 127), late], ssem.at[2])
    for load in loads[9:]:
        load.wait()
    wait(got.at[pl.ds(0, 127), early], rsem.at[4])

    def transform(n, _):
        f, group = lax.div(n, 4), lax.rem(n, 4)
        turned = row_dft(
            [[got[((4 * group + k) * 2 + f) * 4 + q, :32, :] for q in range(4)] for k in range(4)],
            (wrh, wrl), tj, group,
        )
        for k in range(16):
            send[n * 16 + k] = turned[k]

        @pl.when(group == 0)
        def _():
            for k, v in enumerate(row_dft_zero([got[f * 4 + q, :32, :] for q in range(4)], (wsh, wsl))):
                send[n * 16 + k] = v

        return 0

    lax.fori_loop(0, 8, transform, 0)

    def finish(n, _, h):
        f, group = lax.div(n, 4), lax.rem(n, 4)
        here = slice(h * 32, h * 32 + 32)
        parts = []
        for k in range(4):
            base = ((4 * group + k) * 2 + f) * 4
            v = jnp.concatenate(
                [got[base + q, 32 + 16 * h:48 + 16 * h, :] for q in range(4)], axis=0
            )
            hi = v.astype(BF).astype(F32)
            a = jnp.concatenate([hi, v - hi], axis=0).T.astype(BF)
            parts.append(jnp.concatenate([a[:64], a[64:]], axis=1))
        a = jnp.concatenate(parts, axis=0)
        u = dot(a, vrh[...]) + dot(a, vrl[...])

        def add(k, pieces):
            for i, v in enumerate(pieces):
                send[n * 16 + 4 * k + i, here, :] += v

        for k in range(4):
            v = u[k * 64:k * 64 + 64]
            re, im = v[:32, :256] - v[32:, 256:], v[:32, 256:] + v[32:, :256]
            tr, ti = tj[4 * group + k, 0:1, :], tj[4 * group + k, 1:2, :]
            pieces = halves(re * tr - im * ti, re * ti + im * tr)
            if k > 0:
                add(k, pieces)
            else:
                @pl.when(group > 0)
                def _(pieces=pieces):
                    add(0, pieces)

        @pl.when(group == 0)
        def _():
            for q in range(4):
                edges[2 * q:2 * q + 2, :] = gotx[f * 4 + q]
            edge = jnp.concatenate([edges[...], jnp.zeros((120, 128), F32)], axis=0).T[:, :32]
            v = three(edge[h * 32:h * 32 + 32], (xh[0], xl[0]))
            v = v + three(edge[64 + h * 32:96 + h * 32], (xh[1], xl[1]))
            for i in range(2):
                one = parts[0][i * 32:i * 32 + 32]
                v = v + dot(one, vsh[i]) + dot(one, vsl[i])
            add(0, halves(v[:, :256], v[:, 256:]))

        return 0

    @pl.when(first)
    def _():
        wait(gotx.at[pl.ds(0, 7)], rsem.at[3])

    @pl.when(mine >= 8)
    def _():
        wait(gotx, rsem.at[3])

    for h in range(2):
        wait(got.at[pl.ds(0, 127), pl.ds(h * 16, 16)], rsem.at[5 + h])

        def picture(f, _, h=h):
            lax.fori_loop(4 * f, 4 * f + 4, functools.partial(finish, h=h), 0)

            def strip(i, _):
                at = pl.ds(pl.multiple_of(h * 32 + i * 8, 8), 8)
                for tile in range(2):
                    mixed = mix_pairs(lambda k, part: send[f * 64 + 4 * k + 2 * part + tile, at, :])
                    for l, value in mixed:
                        image[f, at, l * 256 + tile * 128:l * 256 + tile * 128 + 128] = value
                pltpu.make_async_copy(image.at[f, at, :], out.at[f, at, :], lsem).start()
                return 0

            lax.fori_loop(0, 4, strip, 0)
            return 0

        lax.fori_loop(0, 2, picture, 0)
    wait(out, lsem)
    @pl.when(first)
    def _():
        wait(extra.at[pl.ds(0, 127)], ssem.at[3])

    wait(tabr.at[pl.ds(0, 127)], ssem.at[0])
    wait(got.at[pl.ds(0, 127), early], ssem.at[4])
    for p in range(2):
        wait(got.at[pl.ds(0, 127), pl.ds(p * 16, 16)], ssem.at[5 + p])


def exchange(tiles, pair, time, chan, count, weights, pixels, beams):
    t = tables()
    smem = pl.BlockSpec(memory_space=pltpu.SMEM)
    away = pl.BlockSpec(memory_space=pl.ANY)
    constants = (*t["b"], *t["wc"], *t["tw"], t["f"], *t["wr"], *t["ws"], *t["vr"], *t["vs"], *t["wx"], t["tj"])
    return pl.pallas_call(
        exchange_kernel,
        out_shape=jax.ShapeDtypeStruct((2, 64, 8192), F32),
        in_specs=[pl.BlockSpec(memory_space=pltpu.VMEM)] + [smem] * 5 + [away] * 20,
        out_specs=away,
        scratch_shapes=[
            pltpu.VMEM((128, 2, 16, 128), F32),
            pltpu.VMEM((1024, 2, 16, 128), BF),
            pltpu.VMEM((8, 2, 256, 256), BF),
            pltpu.VMEM((8, 2, 256, 256), BF),
            pltpu.VMEM((512, 256), BF),
            pltpu.VMEM((512, 256), BF),
            pltpu.VMEM((256, 128), F32),
            pltpu.VMEM((256, 128), F32),
            pltpu.VMEM((2, 2, 256, 256), BF),
            pltpu.VMEM((128, 512), BF),
            pltpu.VMEM((128, 512), BF),
            pltpu.VMEM((2, 128, 512), BF),
            pltpu.VMEM((2, 128, 512), BF),
            pltpu.VMEM((256, 512), BF),
            pltpu.VMEM((256, 512), BF),
            pltpu.VMEM((2, 256, 512), BF),
            pltpu.VMEM((2, 256, 512), BF),
            pltpu.VMEM((2, 32, 512), BF),
            pltpu.VMEM((2, 32, 512), BF),
            pltpu.VMEM((16, 2, 256), F32),
            pltpu.VMEM((128 * 32, 128), F32),
            pltpu.VMEM((8, 256, 256), BF),
            pltpu.VMEM((8, 256, 256), BF),
            pltpu.VMEM((256, 256), BF),
            pltpu.VMEM((128, 64, 128), F32),
            pltpu.VMEM((4, 1, 128), I32),
            pltpu.VMEM((128, 64, 128), F32),
            pltpu.VMEM((128, 1, 128), I32),
            pltpu.VMEM((128, 128), I32),
            pltpu.VMEM((2, 16 * 256, 256), BF),
            pltpu.VMEM((2, 256, 256), BF),
            pltpu.VMEM((2, 256, 256), BF),
            pltpu.VMEM((256, 256), F32),
            pltpu.VMEM((128 * 64, 128), F32),
            pltpu.VMEM((128, 2, 128), F32),
            pltpu.VMEM((128, 64, 128), F32),
            pltpu.VMEM((8, 2, 128), F32),
            pltpu.VMEM((8, 128), F32),
            pltpu.VMEM((2, 64, 8192), F32),
            pltpu.SemaphoreType.DMA((8,)),
            pltpu.SemaphoreType.DMA((8,)),
            pltpu.SemaphoreType.DMA,
            pltpu.SemaphoreType.DMA((20,)),
        ],
        compiler_params=pltpu.CompilerParams(
            vmem_limit_bytes=VMEM, collective_id=0, has_side_effects=True
        ),
        name="exchange",
    )(tiles, pair, time, chan, count, weights, pixels, beams, *constants)


def pixel_view(pixels):
    x = pixels.reshape(128, 2, 2, 8, 128).transpose(0, 1, 3, 2, 4)
    return x.reshape(128, 2, 16, 128)


def beam_view(aterms):
    x = aterms.reshape(512, 2, 2, 2, 8, 128).transpose(0, 1, 2, 4, 3, 5)
    return x.reshape(1024, 2, 16, 128)


def local(
    subgrid_pixels, tile_offsets, station_pairs, time_blocks, channel_blocks, valid_counts,
    aterms, channel_weights,
):
    return exchange(
        tile_offsets.T, station_pairs.T, time_blocks, channel_blocks, valid_counts, channel_weights,
        pixel_view(subgrid_pixels), beam_view(aterms),
    )


def solution(mesh):
    in_specs = (
        P(("row", "col"), None, None, None),
        P(("row", "col"), None),
        P(("row", "col"), None),
        P(("row", "col")),
        P(("row", "col")),
        P(("row", "col")),
        P(),
        P(),
    )
    out_specs = P(None, ("row", "col"), None)
    return jax.shard_map(local, mesh=mesh, in_specs=in_specs, out_specs=out_specs, check_vma=False)
```

```python
import functools
import math

import jax
import jax.numpy as jnp
import ml_dtypes
import numpy as np
from jax import lax
from jax.experimental import pallas as pl
from jax.experimental.pallas import tpu as pltpu
from jax.sharding import PartitionSpec as P

BF = jnp.bfloat16
F32 = jnp.float32
I32 = jnp.int32

PAIR_J = (0, 8, 4, 12, 1, 9, 17, 25, 2, 10, 18, 26, 3, 11, 19, 27)
VMEM = 56 * 1024 * 1024


def partner(j):
    return 16 if j == 0 else 32 - j


def unit(turns):
    return np.exp(-2j * np.pi * turns)


def split_np(x):
    hi = np.asarray(x, np.float32).astype(ml_dtypes.bfloat16)
    lo = (np.asarray(x, np.float64) - hi.astype(np.float64)).astype(ml_dtypes.bfloat16)
    return hi, lo


def split(x):
    hi = x.astype(BF)
    return hi, (x - hi.astype(F32)).astype(BF)


def dot(a, b):
    return lax.dot_general(a, b, (((1,), (0,)), ((), ())), preferred_element_type=F32)


def dot_nt(a, b):
    return lax.dot_general(a, b, (((1,), (1,)), ((), ())), preferred_element_type=F32)


@functools.lru_cache(None)
def tables():
    xi = np.arange(4)[:, None, None]
    y = np.arange(32)[None, :, None]
    v = np.arange(32)[None, None, :]
    b = np.zeros((8, 2, 2, 4, 32, 2, 2, 2, 32))
    for step in range(8):
        for pair in range(2):
            j = PAIR_J[2 * step + pair]
            for half, jj in enumerate((j, partner(j))):
                w = unit((xi * jj + y * v) % 32 / 32) / 32
                b[step, half, 0, :, :, pair, half, 0] = w.real
                b[step, half, 0, :, :, pair, half, 1] = w.imag
                b[step, half, 1, :, :, pair, half, 0] = -w.imag
                b[step, half, 1, :, :, pair, half, 1] = w.real
    b = b.reshape(8, 2, 256, 256)
    i = np.arange(256)
    w = unit(i[:, None] * i[None, :] % 256 / 256)
    wc = np.stack([w.real.reshape(4, 64, 256), w.imag.reshape(4, 64, 256)], 1).reshape(512, 256)
    tw = unit(i[:, None] * (np.arange(128) % 32)[None, :] / 8192)
    d = unit(np.arange(32)[:, None] * np.arange(32)[None, :] % 32 / 32)
    coef = np.stack([np.stack([d, 1j * d]), np.stack([1j * d, -d])])
    f = np.zeros((2, 2, 2, 2, 32, 2, 2, 2, 32))

    def put(kind, which, half, pm, conj):
        for pq in range(2):
            for reim in range(2):
                c = coef[pq, reim]
                f[kind, which, pm, 0, :, pq, half, reim, :] = c.real
                f[kind, which, pm, 1, :, pq, half, reim, :] = -c.imag if conj else c.imag

    put(0, 0, 0, 0, False)
    put(0, 0, 1, 1, True)
    put(0, 1, 1, 0, True)
    put(0, 1, 0, 1, False)
    put(1, 0, 0, 0, False)
    put(1, 0, 1, 1, False)
    put(1, 1, 1, 1, True)
    put(1, 1, 0, 0, True)
    f = f.reshape(2, 2, 128, 256)
    fh, fl = split_np(f)
    f = np.concatenate([fh, fl], axis=2)
    k = np.arange(256)
    q, rp, t, pm = k // 64, k // 32 % 2, k // 2 % 16, k % 2
    r = 16 * (2 * q + rp) + t
    rr = np.where(pm == 0, r, 255 - r)
    l0 = np.arange(256)
    w = unit(rr[:, None] * l0[None, :] % 256 / 256) / 4096
    wr = np.concatenate([w.real, w.imag], axis=1)
    w0 = np.where((pm == 0)[:, None], unit(r[:, None] * l0[None, :] % 256 / 256), 0) / 4096
    w16 = np.where((pm == 1)[:, None], unit((32 * r[:, None] + 16) * l0[None, :] % 8192 / 8192), 0) / 4096
    ws = np.stack([np.concatenate([w0.real, w16.real], 1), np.concatenate([-w0.imag, -w16.imag], 1)])
    kx = np.arange(32)
    qx, row = kx // 2 % 4, kx % 2
    rx = 16 * (15 - (2 * qx + row))
    wx = np.where((kx < 8)[:, None], unit(-(rx[:, None] * l0[None, :] % 256) / 256), 0) / 4096
    zero = np.zeros_like(wx.real)
    wx = np.stack([np.concatenate([wx.real, zero], 1), np.concatenate([-wx.imag, zero], 1)])
    tj = unit(np.array(PAIR_J)[:, None] * l0[None, :] / 8192)
    tj = np.stack([tj.real, tj.imag], 1).astype(np.float32)
    wr, ws = wr.reshape(4, 2, 32, 512), ws.reshape(2, 4, 2, 32, 512)
    late = [w.reshape(*w.shape[:-2], 16, 2, 512) for w in (wr[:, 1], ws[:, :, 1])]
    wr = split_np(wr[:, 0].reshape(128, 512))
    ws = split_np(ws[:, :, 0].reshape(2, 128, 512))

    def doubled(w):
        h, l = split_np(w)
        shape = (*w.shape[:-4], 256, 512)
        return (
            np.stack([h, h], axis=-4).reshape(shape),
            np.stack([l, np.zeros_like(l)], axis=-4).reshape(shape),
        )

    vr = doubled(late[0].transpose(2, 0, 1, 3))
    vs = doubled(late[1].transpose(0, 3, 1, 2, 4))
    return dict(
        b=split_np(b), wc=split_np(wc), tw=(tw.real.astype(np.float32), tw.imag.astype(np.float32)),
        f=f, wr=wr, ws=ws, vr=vr, vs=vs, wx=split_np(wx), tj=tj,
    )


def dft8(re, im):
    h = math.sqrt(0.5)

    def four(a, b):
        s0r, s0i = a[0] + a[2], b[0] + b[2]
        s1r, s1i = a[0] - a[2], b[0] - b[2]
        s2r, s2i = a[1] + a[3], b[1] + b[3]
        s3r, s3i = a[1] - a[3], b[1] - b[3]
        return (
            [s0r + s2r, s1r + s3i, s0r - s2r, s1r - s3i],
            [s0i + s2i, s1i - s3r, s0i - s2i, s1i + s3r],
        )

    er, ei = four(re[0::2], im[0::2])
    orr, oi = four(re[1::2], im[1::2])
    tr = [orr[0], (orr[1] + oi[1]) * h, oi[2], (oi[3] - orr[3]) * h]
    ti = [oi[0], (oi[1] - orr[1]) * h, -orr[2], -(oi[3] + orr[3]) * h]
    return (
        [er[k] + tr[k] for k in range(4)] + [er[k] - tr[k] for k in range(4)],
        [ei[k] + ti[k] for k in range(4)] + [ei[k] - ti[k] for k in range(4)],
    )


def place(tiles, count, tabs):
    row, col = tiles[0:1, :], tiles[1:2, :]
    block_row = lax.shift_right_logical(row, 4)
    low = block_row < 8
    near = jnp.where(low, block_row, 15 - block_row)
    block = (near * 2 + jnp.where(low, 0, 1)) * 8 + lax.shift_right_logical(col, 5)
    tile = (row & 15) * 32 + (col & 31)
    down = lax.broadcasted_iota(I32, (128, 128), 0)
    along = lax.broadcasted_iota(I32, (128, 128), 1)

    def column(x):
        return jnp.broadcast_to(x, (128, 128)).T

    earlier = (column(block) == block) & (down < along)
    rank = jnp.sum(jnp.where(earlier, 1.0, 0.0), axis=0, keepdims=True)
    slot = block * 2 + jnp.where(rank > 0.5, 1, 0)
    slot = jnp.where(along[0:1] < count, slot, -1)
    slots, tile = column(slot), column(tile).astype(F32)
    for q in range(4):
        tabs[q] = jnp.sum(jnp.where(slots == along + 64 * q, tile, 0.0), axis=0, keepdims=True).astype(I32)
    hit = jnp.where(lax.broadcasted_iota(I32, (256, 128), 0) == slot, 1.0, 0.0).astype(BF)
    return jnp.concatenate([hit, hit], axis=1)


def three(a, b):
    ah, al = split(a)
    return dot(ah, b[0]) + dot(al, b[0]) + dot(ah, b[1])


def halves(re, im):
    return [re[:, :128], re[:, 128:], im[:, :128], im[:, 128:]]


def row_dft(blocks, w, tj, group):
    a = jnp.concatenate([jnp.concatenate(b, axis=0).T for b in blocks], axis=0)
    u = three(a, (w[0][...], w[1][...]))
    outs = []
    for k in range(4):
        v = u[k * 128:k * 128 + 128]
        vr = v[:64, :256] - v[64:, 256:]
        vi = v[:64, 256:] + v[64:, :256]
        tr, ti = tj[4 * group + k, 0:1, :], tj[4 * group + k, 1:2, :]
        outs += halves(vr * tr - vi * ti, vr * ti + vi * tr)
    return outs


def row_dft_zero(block, w):
    a = jnp.concatenate(block, axis=0).T
    v = three(a[:64], (w[0][0], w[1][0])) + three(a[64:], (w[0][1], w[1][1]))
    return halves(v[:, :256], v[:, 256:])


def mix_pairs(load):
    index = {}
    for i, j in enumerate(PAIR_J):
        if i > 0:
            index[j if j < 16 else 32 - j] = (i, 1.0 if j < 16 else -1.0)
    zero, mid = load(0, 0), load(0, 1)
    re = {j: load(k, 0) for j, (k, _) in index.items()}
    im = {j: load(k, 1) for j, (k, _) in index.items()}

    def wave(fun, part, js, l1, signed):
        total = jnp.zeros((8, 128), F32)
        started = False
        for j in js:
            c = fun(2 * math.pi * (j * l1 % 32) / 32) * (index[j][1] if signed else 1.0)
            if abs(c) < 1e-12:
                continue
            term = part[j] if abs(abs(c) - 1) < 1e-12 else part[j] * abs(c)
            if started:
                total = total + term if c > 0 else total - term
            else:
                total = term if c > 0 else -term
            started = True
        return total

    odd, even, four = range(1, 16, 2), (2, 6, 10, 14), (4, 8, 12)
    ce, se = [None] * 9, [None] * 9
    for l1 in range(5):
        ee = wave(math.cos, re, four, l1, False) + (zero + mid if l1 % 2 == 0 else zero - mid)
        eo = wave(math.cos, re, even, l1, False)
        oe = wave(math.sin, im, four, l1, True)
        oo = wave(math.sin, im, even, l1, True)
        ce[l1], ce[8 - l1] = ee + eo, ee - eo
        se[l1], se[8 - l1] = oe + oo, oo - oe
    outs = []
    for l1 in range(9):
        co = wave(math.cos, re, odd, l1, False)
        so = wave(math.sin, im, odd, l1, True)
        p, m = ce[l1] + co, ce[l1] - co
        s, d = se[l1] + so, se[l1] - so
        outs += [(l1, p + s), (16 + l1, m + d)]
        if l1 > 0:
            outs.append((32 - l1, p - s))
            if l1 < 8:
                outs.append((16 - l1, m - d))
    return outs


def paint(load, image, out, sem):
    def strip(i, _):
        at = pl.ds(pl.multiple_of(i * 8, 8), 8)
        for tile in range(2):
            for l, value in mix_pairs(lambda k, part: load(4 * k + 2 * part + tile, at)):
                image[at, l * 256 + tile * 128:l * 256 + tile * 128 + 128] = value
        pltpu.make_async_copy(image.at[at, :], out.at[at, :], sem).start()
        return 0

    lax.fori_loop(0, 4, strip, 0)


def exchange_kernel(
    tiles, pair, time, chan, vc, cw, pixels_hbm, beams_hbm, bh_hbm, bl_hbm,
    wh_hbm, wl_hbm, twr_hbm, twi_hbm, fmat_hbm,
    wrh_hbm, wrl_hbm, wsh_hbm, wsl_hbm, vrh_hbm, vrl_hbm, vsh_hbm, vsl_hbm, xh_hbm, xl_hbm, tj_hbm, out, rest,
    px, beams, bh, bl, wh, wl, twr, twi, fmat, wrh, wrl, wsh, wsl, vrh, vrl, vsh, vsl, xh, xl, tj,
    corr, lhi, llo, perm, send, tabs,
    recv, tabr, tabt, ghl, pqh, pql, held, stage, extra, got, gotx, edges, image, ssem, rsem, lsem, msem, csem
):
    line, column = lax.axis_index("row"), lax.axis_index("col")
    x, y = lax.div(line, 4), lax.rem(line, 4)
    z, core = lax.div(column, 2), lax.rem(column, 2)
    me = line * 8 + column

    def unit_of(row, col):
        turn = lax.rem(lax.div(row, 4) + row + lax.div(col, 2), 4)
        return (turn * 2 + lax.rem(col, 2)) * 16 + row

    mine = unit_of(line, column)
    first = mine < 8
    kind = jnp.where(first, 1, 0)
    barrier = pltpu.get_barrier_semaphore()
    loads = [
        pltpu.make_async_copy(src, dst, csem.at[i])
        for i, (src, dst) in enumerate((
            (beams_hbm, beams), (pixels_hbm, px), (bh_hbm, bh), (bl_hbm, bl), (wh_hbm, wh),
            (wl_hbm, wl), (twr_hbm, twr), (twi_hbm, twi), (fmat_hbm, fmat),
            (wrh_hbm, wrh), (wrl_hbm, wrl), (wsh_hbm, wsh), (wsl_hbm, wsl),
            (vrh_hbm, vrh), (vrl_hbm, vrl), (vsh_hbm, vsh), (vsl_hbm, vsl),
            (xh_hbm, xh), (xl_hbm, xl), (tj_hbm, tj),
        ))
    ]
    for load in loads:
        load.start()

    cols = [lax.rem(z + b // 2, 4) * 2 + lax.rem(core + b, 2) for b in range(8)]

    def each(fun):
        def step(a, _):
            def one(b):
                o = lax.rem(a + 5 * b, 16)
                row = lax.rem(x + lax.div(o, 4), 4) * 4 + lax.rem(y + o, 4)
                fun(row * 8 + cols[b], (row, cols[b]))

            for b in (3, 6, 1, 4, 7, 2, 5):
                one(b)

            @pl.when(a > 0)
            def _():
                one(0)

            return 0

        lax.fori_loop(0, 16, step, 0)

    def push(src, dst, k, dev):
        pltpu.make_async_remote_copy(
            src_ref=src, dst_ref=dst, send_sem=ssem.at[k], recv_sem=rsem.at[k],
            device_id=dev, device_id_type=pl.DeviceIdType.MESH,
        ).start()

    def wait(part, sem):
        pltpu.make_async_copy(part, part, sem).wait()

    def keep(src, dst):
        copy = pltpu.make_async_copy(src, dst, lsem)
        copy.start()
        copy.wait()

    each(lambda d, dev: pl.semaphore_signal(
        barrier, inc=1, device_id=dev, device_id_type=pl.DeviceIdType.MESH))
    perm[...] = place(tiles, vc[0], tabs)
    loads[0].wait()
    loads[1].wait()

    def correct(s, _):
        weight = jnp.where(s < vc[0], cw[chan[s]], 0.0)
        one = beams[pair[0, s] * 2 + time[s]].astype(F32)
        two = beams[pair[1, s] * 2 + time[s]].astype(F32)
        gr = (one[0] * two[0] + one[1] * two[1]) * weight
        gi = (one[1] * two[0] - one[0] * two[1]) * weight
        pr, pi = px[s, 0], px[s, 1]
        at = pl.multiple_of(s * 32, 32)
        corr[pl.ds(at, 16), :] = pr * gr - pi * gi
        corr[pl.ds(at + 16, 16), :] = pr * gi + pi * gr
        return 0

    lax.fori_loop(0, 128, correct, 0, unroll=4)

    def coarse(group, _):
        for f in range(2):
            base = group * 16 * 32 + f
            re = [corr[pl.ds(base + 2 * p, 16, stride=32), :] for p in range(8)]
            im = [corr[pl.ds(base + 16 + 2 * p, 16, stride=32), :] for p in range(8)]
            re, im = dft8(re, im)
            rows = pl.ds(pl.multiple_of(f * 128 + group * 16, 16), 16)
            for k in range(8):
                lhi[k, rows, :128], llo[k, rows, :128] = split(re[k])
                lhi[k, rows, 128:], llo[k, rows, 128:] = split(im[k])
        return 0

    lax.fori_loop(0, 8, coarse, 0)
    loads[2].wait()
    loads[3].wait()

    early, late = pl.ds(0, 32), pl.ds(32, 32)
    pl.semaphore_wait(barrier, 127)

    def fine(i, _):
        k = lax.rem(i + lax.div(mine, 16), 8)
        a = jnp.where(k == 0, 0, jnp.where(k == 1, 4, lax.div(k, 2)))
        b = jnp.where(k < 2, a, 8 - a)
        acc = None
        for half, at in enumerate((a, b)):
            h = bh[k, half]
            term = dot(lhi[at], h) + dot(llo[at], h) + dot(lhi[at], bl[k, half])
            acc = term if acc is None else acc + term
        hi, lo = split(acc)
        for f in range(2):
            rows = slice(f * 128, f * 128 + 128)
            padded = dot(perm[...], jnp.concatenate([hi[rows], lo[rows]], axis=0))
            for p in range(2):
                for q in range(4):
                    send[(k * 4 + p * 2 + f) * 4 + q] = (
                        padded[q * 64:(q + 1) * 64, p * 128:(p + 1) * 128]
                    )
        for n in range(16):
            o = n * 7 % 16
            tx, ty = lax.rem(x + o // 4, 4), lax.rem(y + o % 4, 4)
            tz = lax.rem(lax.div(k, 2) + 8 - tx - ty, 4)
            dev = (tx * 4 + ty, tz * 2 + lax.rem(k, 2))
            if o > 0:
                push(send.at[k * 16 + dev[0], early], recv.at[me, early], 1, dev)
            else:
                @pl.when(i > 0)
                def _(dev=dev):
                    push(send.at[k * 16 + dev[0], early], recv.at[me, early], 1, dev)

        return 0

    lax.fori_loop(0, 8, fine, 0)
    each(lambda d, dev: push(tabs.at[lax.rem(dev[0], 4)], tabr.at[me], 0, dev))
    each(lambda d, dev: push(send.at[unit_of(*dev), late], recv.at[me, late], 2, dev))
    keep(tabs.at[y], tabr.at[me])
    keep(send.at[mine], recv.at[me])
    flat = recv.reshape(128 * 64, 128)

    for load in loads[4:9]:
        load.wait()
    wait(tabr.at[pl.ds(0, 127)], rsem.at[0])
    tabt[...] = tabr[...].reshape(128, 128).T
    lane = lax.broadcasted_iota(I32, (32, 128), 1)
    low = lane < 64
    even = (lane & 32) == 0

    shifted = first & (lax.broadcasted_iota(I32, (64, 128), 1) < 64)

    def columns(pm, t):
        g = ghl[pm, pl.ds(pl.multiple_of(t * 256, 256), 256), :]
        for c in range(4):
            rows = slice(c * 128, c * 128 + 128)
            a = dot(wh[rows, :], g)
            b = dot(wl[rows, :], g[:, :128])
            u = a[:, :128] + a[:, 128:] + b
            ur, ui = u[:64], u[64:]
            m0 = slice(c * 64, c * 64 + 64)
            tr, ti = twr[m0, :], twi[m0, :]
            for lanes, value in (
                (slice(0, 128), tr * ur - ti * ui), (slice(128, 256), tr * ui + ti * ur)
            ):
                if pm == 1:
                    value, held[m0, lanes] = jnp.where(shifted, held[m0, lanes], value), value
                pqh[pm, m0, lanes], pql[pm, m0, lanes] = split(value)

    def mix(which, pm):
        both = fmat[kind, which]
        z = dot_nt(both, pqh[pm])
        return z[:128] + z[128:] + dot_nt(both[:128], pql[pm])

    def turn(z, pm, tile):
        lanes = slice(tile * 128, tile * 128 + 128)
        re, im = z[pm * 64:pm * 64 + 32, lanes], z[pm * 64 + 32:pm * 64 + 64, lanes]
        return (
            jnp.where(low, re, pltpu.roll(im, 64, 1)), jnp.where(low, pltpu.roll(re, 64, 1), im)
        )

    def emit(z, t):
        for pm in range(2):
            for tile in range(2):
                for q, rows in enumerate(turn(z, pm, tile)):
                    stage[pl.ds((2 * tile + q) * 64 + 2 * t + pm, 32, stride=256), :] = rows

    def emit_by_m(z, t):
        for tile in range(2):
            a = [z[i * 32:i * 32 + 32, tile * 128:tile * 128 + 128] for i in range(4)]
            c = [
                jnp.where(low, a[0], pltpu.roll(a[2], 64, 1)), jnp.where(low, a[1], pltpu.roll(a[3], 64, 1)),
                jnp.where(low, pltpu.roll(a[0], 64, 1), a[2]), jnp.where(low, pltpu.roll(a[1], 64, 1), a[3]),
            ]
            for q in range(2):
                b = (
                    jnp.where(even, c[2 * q], pltpu.roll(c[2 * q + 1], 32, 1)),
                    jnp.where(even, pltpu.roll(c[2 * q], 96, 1), c[2 * q + 1]),
                )
                for h in range(2):
                    at = (2 * tile + q) * 64 + 32 + 16 * h
                    stage[pl.ds(at + t, 32, stride=256), :] = b[h]

    def gather(rp):
        for pm in range(2):
            def block(c, _, pm=pm):
                at = rp * 32 + pm * 16 + 2 * c
                key = jnp.concatenate([tabt[pl.ds(at + k, 1), :] for k in range(2)], axis=1)
                parts = [split(flat[pl.ds(at + k, 128, stride=64), :]) for k in range(2)]
                rhs = jnp.concatenate([jnp.concatenate(p, axis=1) for p in parts], axis=0)
                for chunk in range(4):
                    tile = lax.broadcasted_iota(I32, (128, 256), 0) + chunk * 128
                    hit = jnp.where(tile == key, 1.0, 0.0).astype(BF)
                    s = dot(hit, rhs)
                    hi, lo = split(s[:, :128] + s[:, 128:])
                    for i in range(4):
                        to = pl.multiple_of((chunk * 4 + i) * 256 + c * 32, 32)
                        ghl[pm, pl.ds(to, 32), :128] = hi[i * 32:i * 32 + 32]
                        ghl[pm, pl.ds(to, 32), 128:] = lo[i * 32:i * 32 + 32]
                return 0

            lax.fori_loop(0, 8, block, 0)
        held[...] = jnp.zeros((256, 256), F32)

    def phase(rp):
        gather(rp)

        def row(t, _):
            columns(0, t)
            columns(1, 15 - t)
            z = mix(0, 0) + mix(1, 1)
            if rp == 0:
                emit(z, t)
            else:
                emit_by_m(z, t)
            return 0

        lax.fori_loop(0, 16, row, 0)

        @pl.when(first)
        def _():
            for lanes in (slice(0, 128), slice(128, 256)):
                pqh[1, :, lanes], pql[1, :, lanes] = split(held[:, lanes])
            edge = mix(1, 1)
            for tile in range(2):
                for q, rows in enumerate(turn(edge, 0, tile)):
                    for m in range(32):
                        extra[m * 4 + 2 * tile + q, rp:rp + 1, :] = rows[m:m + 1]

    def deliver(start, size, k):
        rows = pl.ds(start, size)

        def piece(d):
            return stage.at[pl.ds(pl.multiple_of(d * 64 + start, 16), size), :]

        each(lambda d, dev: push(piece(d), got.at[mine, rows], k, dev))
        keep(piece(me), got.at[mine, rows])

    wait(recv.at[pl.ds(0, 127), early], rsem.at[1])
    phase(0)
    deliver(0, 32, 4)
    wait(recv.at[pl.ds(0, 127), late], rsem.at[2])
    phase(1)
    deliver(32, 16, 5)
    deliver(48, 16, 6)

    @pl.when(first)
    def _():
        each(lambda d, dev: push(extra.at[d], gotx.at[mine], 3, dev))
        keep(extra.at[me], gotx.at[mine])

    wait(send.at[pl.ds(0, 127), early], ssem.at[1])
    wait(send.at[pl.ds(0, 127), late], ssem.at[2])
    for load in loads[9:]:
        load.wait()
    wait(got.at[pl.ds(0, 127), early], rsem.at[4])

    def transform(n, _):
        f, group = lax.div(n, 4), lax.rem(n, 4)
        turned = row_dft(
            [[got[((4 * group + k) * 2 + f) * 4 + q, :32, :] for q in range(4)] for k in range(4)],
            (wrh, wrl), tj, group,
        )
        for k in range(16):
            send[n * 16 + k] = turned[k]

        @pl.when(group == 0)
        def _():
            for k, v in enumerate(row_dft_zero([got[f * 4 + q, :32, :] for q in range(4)], (wsh, wsl))):
                send[n * 16 + k] = v

        return 0

    lax.fori_loop(0, 8, transform, 0)

    def finish(n, _, h):
        f, group = lax.div(n, 4), lax.rem(n, 4)
        here = slice(h * 32, h * 32 + 32)
        parts = []
        for k in range(4):
            base = ((4 * group + k) * 2 + f) * 4
            v = jnp.concatenate(
                [got[base + q, 32 + 16 * h:48 + 16 * h, :] for q in range(4)], axis=0
            )
            hi = v.astype(BF).astype(F32)
            a = jnp.concatenate([hi, v - hi], axis=0).T.astype(BF)
            parts.append(jnp.concatenate([a[:64], a[64:]], axis=1))
        a = jnp.concatenate(parts, axis=0)
        u = dot(a, vrh[...]) + dot(a, vrl[...])

        def add(k, pieces):
            for i, v in enumerate(pieces):
                send[n * 16 + 4 * k + i, here, :] += v

        for k in range(4):
            v = u[k * 64:k * 64 + 64]
            re, im = v[:32, :256] - v[32:, 256:], v[:32, 256:] + v[32:, :256]
            tr, ti = tj[4 * group + k, 0:1, :], tj[4 * group + k, 1:2, :]
            pieces = halves(re * tr - im * ti, re * ti + im * tr)
            if k > 0:
                add(k, pieces)
            else:
                @pl.when(group > 0)
                def _(pieces=pieces):
                    add(0, pieces)

        @pl.when(group == 0)
        def _():
            for q in range(4):
                edges[2 * q:2 * q + 2, :] = gotx[f * 4 + q]
            edge = jnp.concatenate([edges[...], jnp.zeros((120, 128), F32)], axis=0).T[:, :32]
            v = three(edge[h * 32:h * 32 + 32], (xh[0], xl[0]))
            v = v + three(edge[64 + h * 32:96 + h * 32], (xh[1], xl[1]))
            for i in range(2):
                one = parts[0][i * 32:i * 32 + 32]
                v = v + dot(one, vsh[i]) + dot(one, vsl[i])
            add(0, halves(v[:, :256], v[:, 256:]))

        return 0

    @pl.when(first)
    def _():
        wait(gotx.at[pl.ds(0, 7)], rsem.at[3])

    @pl.when(mine >= 8)
    def _():
        wait(gotx, rsem.at[3])

    for h in range(2):
        wait(got.at[pl.ds(0, 127), pl.ds(h * 16, 16)], rsem.at[5 + h])

        def picture(f, _, h=h):
            lax.fori_loop(4 * f, 4 * f + 4, functools.partial(finish, h=h), 0)

            if h == 0:
                paint(lambda k, at: send[f * 64 + k, at, :], image.at[f], out.at[f], lsem)
            else:
                mine_f = pl.ds(f * 64, 64)
                pltpu.make_async_copy(send.at[mine_f, late], rest.at[mine_f], msem).start()
            return 0

        lax.fori_loop(0, 2, picture, 0)
    wait(out, lsem)
    wait(rest, msem)

    @pl.when(first)
    def _():
        wait(extra.at[pl.ds(0, 127)], ssem.at[3])

    wait(tabr.at[pl.ds(0, 127)], ssem.at[0])
    wait(got.at[pl.ds(0, 127), early], ssem.at[4])
    for p in range(2):
        wait(got.at[pl.ds(0, 127), pl.ds(p * 16, 16)], ssem.at[5 + p])


def exchange(tiles, pair, time, chan, count, weights, pixels, beams):
    t = tables()
    smem = pl.BlockSpec(memory_space=pltpu.SMEM)
    away = pl.BlockSpec(memory_space=pl.ANY)
    constants = (*t["b"], *t["wc"], *t["tw"], t["f"], *t["wr"], *t["ws"], *t["vr"], *t["vs"], *t["wx"], t["tj"])
    return pl.pallas_call(
        exchange_kernel,
        out_shape=(
            jax.ShapeDtypeStruct((2, 32, 8192), F32), jax.ShapeDtypeStruct((128, 32, 128), F32)
        ),
        in_specs=[pl.BlockSpec(memory_space=pltpu.VMEM)] + [smem] * 5 + [away] * 20,
        out_specs=(away, away),
        scratch_shapes=[
            pltpu.VMEM((128, 2, 16, 128), F32),
            pltpu.VMEM((1024, 2, 16, 128), BF),
            pltpu.VMEM((8, 2, 256, 256), BF),
            pltpu.VMEM((8, 2, 256, 256), BF),
            pltpu.VMEM((512, 256), BF),
            pltpu.VMEM((512, 256), BF),
            pltpu.VMEM((256, 128), F32),
            pltpu.VMEM((256, 128), F32),
            pltpu.VMEM((2, 2, 256, 256), BF),
            pltpu.VMEM((128, 512), BF),
            pltpu.VMEM((128, 512), BF),
            pltpu.VMEM((2, 128, 512), BF),
            pltpu.VMEM((2, 128, 512), BF),
            pltpu.VMEM((256, 512), BF),
            pltpu.VMEM((256, 512), BF),
            pltpu.VMEM((2, 256, 512), BF),
            pltpu.VMEM((2, 256, 512), BF),
            pltpu.VMEM((2, 32, 512), BF),
            pltpu.VMEM((2, 32, 512), BF),
            pltpu.VMEM((16, 2, 256), F32),
            pltpu.VMEM((128 * 32, 128), F32),
            pltpu.VMEM((8, 256, 256), BF),
            pltpu.VMEM((8, 256, 256), BF),
            pltpu.VMEM((256, 256), BF),
            pltpu.VMEM((128, 64, 128), F32),
            pltpu.VMEM((4, 1, 128), I32),
            pltpu.VMEM((128, 64, 128), F32),
            pltpu.VMEM((128, 1, 128), I32),
            pltpu.VMEM((128, 128), I32),
            pltpu.VMEM((2, 16 * 256, 256), BF),
            pltpu.VMEM((2, 256, 256), BF),
            pltpu.VMEM((2, 256, 256), BF),
            pltpu.VMEM((256, 256), F32),
            pltpu.VMEM((128 * 64, 128), F32),
            pltpu.VMEM((128, 2, 128), F32),
            pltpu.VMEM((128, 64, 128), F32),
            pltpu.VMEM((8, 2, 128), F32),
            pltpu.VMEM((8, 128), F32),
            pltpu.VMEM((2, 32, 8192), F32),
            pltpu.SemaphoreType.DMA((8,)),
            pltpu.SemaphoreType.DMA((8,)),
            pltpu.SemaphoreType.DMA,
            pltpu.SemaphoreType.DMA,
            pltpu.SemaphoreType.DMA((20,)),
        ],
        compiler_params=pltpu.CompilerParams(
            vmem_limit_bytes=VMEM, collective_id=0, has_side_effects=True
        ),
        name="exchange",
    )(tiles, pair, time, chan, count, weights, pixels, beams, *constants)


def final_kernel(half, rest, out, val, through, image, sems):
    parts = [(rest.at[pl.ds(f * 64, 64)], val.at[f]) for f in range(2)]
    parts += [(half.at[f], through.at[f]) for f in range(2)]
    loads = [pltpu.make_async_copy(src, dst, sems.at[i]) for i, (src, dst) in enumerate(parts)]
    for load in loads:
        load.start()
    for f in range(2):
        loads[f].wait()
        paint(lambda k, at: val[f, k, at, :], image.at[f], out.at[f, pl.ds(32, 32), :], sems.at[4])
        loads[2 + f].wait()
        pltpu.make_async_copy(through.at[f], out.at[f, pl.ds(0, 32), :], sems.at[5]).start()
    pltpu.make_async_copy(image, image, sems.at[4]).wait()
    pltpu.make_async_copy(through, through, sems.at[5]).wait()


def final(half, rest):
    away = pl.BlockSpec(memory_space=pl.ANY)
    return pl.pallas_call(
        final_kernel,
        out_shape=jax.ShapeDtypeStruct((2, 64, 8192), F32),
        in_specs=[away, away],
        out_specs=away,
        scratch_shapes=[
            pltpu.VMEM((2, 64, 32, 128), F32),
            pltpu.VMEM((2, 32, 8192), F32),
            pltpu.VMEM((2, 32, 8192), F32),
            pltpu.SemaphoreType.DMA((6,)),
        ],
        compiler_params=pltpu.CompilerParams(vmem_limit_bytes=VMEM),
        name="final",
    )(half, rest)


def pixel_view(pixels):
    x = pixels.reshape(128, 2, 2, 8, 128).transpose(0, 1, 3, 2, 4)
    return x.reshape(128, 2, 16, 128)


def beam_view(aterms):
    x = aterms.reshape(512, 2, 2, 2, 8, 128).transpose(0, 1, 2, 4, 3, 5)
    return x.reshape(1024, 2, 16, 128)


def local(
    subgrid_pixels, tile_offsets, station_pairs, time_blocks, channel_blocks, valid_counts,
    aterms, channel_weights,
):
    return final(*exchange(
        tile_offsets.T, station_pairs.T, time_blocks, channel_blocks, valid_counts, channel_weights,
        pixel_view(subgrid_pixels), beam_view(aterms),
    ))


def solution(mesh):
    in_specs = (
        P(("row", "col"), None, None, None),
        P(("row", "col"), None),
        P(("row", "col"), None),
        P(("row", "col")),
        P(("row", "col")),
        P(("row", "col")),
        P(),
        P(),
    )
    out_specs = P(None, ("row", "col"), None)
    return jax.shard_map(local, mesh=mesh, in_specs=in_specs, out_specs=out_specs, check_vma=False)
```

```python
import functools
import math

import jax
import jax.numpy as jnp
import ml_dtypes
import numpy as np
from jax import lax
from jax.experimental import pallas as pl
from jax.experimental.pallas import tpu as pltpu
from jax.sharding import PartitionSpec as P

BF = jnp.bfloat16
F32 = jnp.float32
I32 = jnp.int32

PAIR_J = (0, 8, 4, 12, 1, 9, 17, 25, 2, 10, 18, 26, 3, 11, 19, 27)
VMEM = 56 * 1024 * 1024


def partner(j):
    return 16 if j == 0 else 32 - j


def unit(turns):
    return np.exp(-2j * np.pi * turns)


def split_np(x):
    hi = np.asarray(x, np.float32).astype(ml_dtypes.bfloat16)
    lo = (np.asarray(x, np.float64) - hi.astype(np.float64)).astype(ml_dtypes.bfloat16)
    return hi, lo


def split(x):
    hi = x.astype(BF)
    return hi, (x - hi.astype(F32)).astype(BF)


def dot(a, b):
    return lax.dot_general(a, b, (((1,), (0,)), ((), ())), preferred_element_type=F32)


def dot_nt(a, b):
    return lax.dot_general(a, b, (((1,), (1,)), ((), ())), preferred_element_type=F32)


@functools.lru_cache(None)
def tables():
    xi = np.arange(4)[:, None, None]
    y = np.arange(32)[None, :, None]
    v = np.arange(32)[None, None, :]
    b = np.zeros((8, 2, 2, 4, 32, 2, 2, 2, 32))
    for step in range(8):
        for pair in range(2):
            j = PAIR_J[2 * step + pair]
            for half, jj in enumerate((j, partner(j))):
                w = unit((xi * jj + y * v) % 32 / 32) / 32
                b[step, half, 0, :, :, pair, half, 0] = w.real
                b[step, half, 0, :, :, pair, half, 1] = w.imag
                b[step, half, 1, :, :, pair, half, 0] = -w.imag
                b[step, half, 1, :, :, pair, half, 1] = w.real
    b = b.reshape(8, 2, 256, 256)
    i = np.arange(256)
    w = unit(i[:, None] * i[None, :] % 256 / 256)
    wc = np.stack([w.real.reshape(4, 64, 256), w.imag.reshape(4, 64, 256)], 1).reshape(512, 256)
    tw = unit(i[:, None] * (np.arange(128) % 32)[None, :] / 8192)
    d = unit(np.arange(32)[:, None] * np.arange(32)[None, :] % 32 / 32)
    coef = np.stack([np.stack([d, 1j * d]), np.stack([1j * d, -d])])
    f = np.zeros((2, 2, 2, 2, 32, 2, 2, 2, 32))

    def put(kind, which, half, pm, conj):
        for pq in range(2):
            for reim in range(2):
                c = coef[pq, reim]
                f[kind, which, pm, 0, :, pq, half, reim, :] = c.real
                f[kind, which, pm, 1, :, pq, half, reim, :] = -c.imag if conj else c.imag

    put(0, 0, 0, 0, False)
    put(0, 0, 1, 1, True)
    put(0, 1, 1, 0, True)
    put(0, 1, 0, 1, False)
    put(1, 0, 0, 0, False)
    put(1, 0, 1, 1, False)
    put(1, 1, 1, 1, True)
    put(1, 1, 0, 0, True)
    f = f.reshape(2, 2, 128, 256)
    fh, fl = split_np(f)
    f = np.concatenate([fh, fl], axis=2)
    k = np.arange(256)
    q, rp, t, pm = k // 64, k // 32 % 2, k // 2 % 16, k % 2
    r = 16 * (2 * q + rp) + t
    rr = np.where(pm == 0, r, 255 - r)
    l0 = np.arange(256)
    w = unit(rr[:, None] * l0[None, :] % 256 / 256) / 4096
    wr = np.concatenate([w.real, w.imag], axis=1)
    w0 = np.where((pm == 0)[:, None], unit(r[:, None] * l0[None, :] % 256 / 256), 0) / 4096
    w16 = np.where((pm == 1)[:, None], unit((32 * r[:, None] + 16) * l0[None, :] % 8192 / 8192), 0) / 4096
    ws = np.stack([np.concatenate([w0.real, w16.real], 1), np.concatenate([-w0.imag, -w16.imag], 1)])
    kx = np.arange(32)
    qx, row = kx // 2 % 4, kx % 2
    rx = 16 * (15 - (2 * qx + row))
    wx = np.where((kx < 8)[:, None], unit(-(rx[:, None] * l0[None, :] % 256) / 256), 0) / 4096
    zero = np.zeros_like(wx.real)
    wx = np.stack([np.concatenate([wx.real, zero], 1), np.concatenate([-wx.imag, zero], 1)])
    tj = unit(np.array(PAIR_J)[:, None] * l0[None, :] / 8192)
    tj = np.stack([tj.real, tj.imag], 1).astype(np.float32)
    wr, ws = wr.reshape(4, 2, 32, 512), ws.reshape(2, 4, 2, 32, 512)
    late = [w.reshape(*w.shape[:-2], 16, 2, 512) for w in (wr[:, 1], ws[:, :, 1])]
    wr = split_np(wr[:, 0].reshape(128, 512))
    ws = split_np(ws[:, :, 0].reshape(2, 128, 512))

    def doubled(w):
        h, l = split_np(w)
        shape = (*w.shape[:-4], 256, 512)
        return (
            np.stack([h, h], axis=-4).reshape(shape),
            np.stack([l, np.zeros_like(l)], axis=-4).reshape(shape),
        )

    vr = doubled(late[0].transpose(2, 0, 1, 3))
    vs = doubled(late[1].transpose(0, 3, 1, 2, 4))
    return dict(
        b=split_np(b), wc=split_np(wc), tw=(tw.real.astype(np.float32), tw.imag.astype(np.float32)),
        f=f, wr=wr, ws=ws, vr=vr, vs=vs, wx=split_np(wx), tj=tj,
    )


def dft8(re, im):
    h = math.sqrt(0.5)

    def four(a, b):
        s0r, s0i = a[0] + a[2], b[0] + b[2]
        s1r, s1i = a[0] - a[2], b[0] - b[2]
        s2r, s2i = a[1] + a[3], b[1] + b[3]
        s3r, s3i = a[1] - a[3], b[1] - b[3]
        return (
            [s0r + s2r, s1r + s3i, s0r - s2r, s1r - s3i],
            [s0i + s2i, s1i - s3r, s0i - s2i, s1i + s3r],
        )

    er, ei = four(re[0::2], im[0::2])
    orr, oi = four(re[1::2], im[1::2])
    tr = [orr[0], (orr[1] + oi[1]) * h, oi[2], (oi[3] - orr[3]) * h]
    ti = [oi[0], (oi[1] - orr[1]) * h, -orr[2], -(oi[3] + orr[3]) * h]
    return (
        [er[k] + tr[k] for k in range(4)] + [er[k] - tr[k] for k in range(4)],
        [ei[k] + ti[k] for k in range(4)] + [ei[k] - ti[k] for k in range(4)],
    )


def place(tiles, count, tabs):
    row, col = tiles[0:1, :], tiles[1:2, :]
    block_row = lax.shift_right_logical(row, 4)
    low = block_row < 8
    near = jnp.where(low, block_row, 15 - block_row)
    block = (near * 2 + jnp.where(low, 0, 1)) * 8 + lax.shift_right_logical(col, 5)
    tile = (row & 15) * 32 + (col & 31)
    down = lax.broadcasted_iota(I32, (128, 128), 0)
    along = lax.broadcasted_iota(I32, (128, 128), 1)

    def column(x):
        return jnp.broadcast_to(x, (128, 128)).T

    earlier = (column(block) == block) & (down < along)
    rank = jnp.sum(jnp.where(earlier, 1.0, 0.0), axis=0, keepdims=True)
    slot = block * 2 + jnp.where(rank > 0.5, 1, 0)
    slot = jnp.where(along[0:1] < count, slot, -1)
    slots, tile = column(slot), column(tile).astype(F32)
    for q in range(4):
        tabs[q] = jnp.sum(jnp.where(slots == along + 64 * q, tile, 0.0), axis=0, keepdims=True).astype(I32)
    hit = jnp.where(lax.broadcasted_iota(I32, (256, 128), 0) == slot, 1.0, 0.0).astype(BF)
    return jnp.concatenate([hit, hit], axis=1)


def three(a, b):
    ah, al = split(a)
    return dot(ah, b[0]) + dot(al, b[0]) + dot(ah, b[1])


def halves(re, im):
    return [re[:, :128], re[:, 128:], im[:, :128], im[:, 128:]]


def row_dft(blocks, w, tj, group):
    a = jnp.concatenate([jnp.concatenate(b, axis=0).T for b in blocks], axis=0)
    u = three(a, (w[0][...], w[1][...]))
    outs = []
    for k in range(4):
        v = u[k * 128:k * 128 + 128]
        vr = v[:64, :256] - v[64:, 256:]
        vi = v[:64, 256:] + v[64:, :256]
        tr, ti = tj[4 * group + k, 0:1, :], tj[4 * group + k, 1:2, :]
        outs += halves(vr * tr - vi * ti, vr * ti + vi * tr)
    return outs


def row_dft_zero(block, w):
    a = jnp.concatenate(block, axis=0).T
    v = three(a[:64], (w[0][0], w[1][0])) + three(a[64:], (w[0][1], w[1][1]))
    return halves(v[:, :256], v[:, 256:])


def mix_pairs(load):
    index = {}
    for i, j in enumerate(PAIR_J):
        if i > 0:
            index[j if j < 16 else 32 - j] = (i, 1.0 if j < 16 else -1.0)
    zero, mid = load(0, 0), load(0, 1)
    re = {j: load(k, 0) for j, (k, _) in index.items()}
    im = {j: load(k, 1) for j, (k, _) in index.items()}

    def wave(fun, part, js, l1, signed):
        total = jnp.zeros((8, 128), F32)
        started = False
        for j in js:
            c = fun(2 * math.pi * (j * l1 % 32) / 32) * (index[j][1] if signed else 1.0)
            if abs(c) < 1e-12:
                continue
            term = part[j] if abs(abs(c) - 1) < 1e-12 else part[j] * abs(c)
            if started:
                total = total + term if c > 0 else total - term
            else:
                total = term if c > 0 else -term
            started = True
        return total

    odd, even, four = range(1, 16, 2), (2, 6, 10, 14), (4, 8, 12)
    ce, se = [None] * 9, [None] * 9
    for l1 in range(5):
        ee = wave(math.cos, re, four, l1, False) + (zero + mid if l1 % 2 == 0 else zero - mid)
        eo = wave(math.cos, re, even, l1, False)
        oe = wave(math.sin, im, four, l1, True)
        oo = wave(math.sin, im, even, l1, True)
        ce[l1], ce[8 - l1] = ee + eo, ee - eo
        se[l1], se[8 - l1] = oe + oo, oo - oe
    outs = []
    for l1 in range(9):
        co = wave(math.cos, re, odd, l1, False)
        so = wave(math.sin, im, odd, l1, True)
        p, m = ce[l1] + co, ce[l1] - co
        s, d = se[l1] + so, se[l1] - so
        outs += [(l1, p + s), (16 + l1, m + d)]
        if l1 > 0:
            outs.append((32 - l1, p - s))
            if l1 < 8:
                outs.append((16 - l1, m - d))
    return outs


def paint(load, image, out, sem):
    def strip(i, _):
        at = pl.ds(pl.multiple_of(i * 8, 8), 8)
        for tile in range(2):
            for l, value in mix_pairs(lambda k, part: load(4 * k + 2 * part + tile, at)):
                image[at, l * 256 + tile * 128:l * 256 + tile * 128 + 128] = value
        pltpu.make_async_copy(image.at[at, :], out.at[at, :], sem).start()
        return 0

    lax.fori_loop(0, 4, strip, 0)


def exchange_kernel(
    tiles, pair, time, chan, vc, cw, pixels_hbm, beams_hbm, bh_hbm, bl_hbm,
    wh_hbm, wl_hbm, twr_hbm, twi_hbm, fmat_hbm,
    wrh_hbm, wrl_hbm, wsh_hbm, wsl_hbm, vrh_hbm, vrl_hbm, vsh_hbm, vsl_hbm, xh_hbm, xl_hbm, tj_hbm, out, rest,
    px, beams, bh, bl, wh, wl, twr, twi, fmat, wrh, wrl, wsh, wsl, vrh, vrl, vsh, vsl, xh, xl, tj,
    corr, lhi, llo, perm, send, tabs,
    recv, tabr, tabt, ghl, pqh, pql, held, stage, extra, got, gotx, edges, image, ssem, rsem, lsem, msem, csem
):
    line, column = lax.axis_index("row"), lax.axis_index("col")
    x, y = lax.div(line, 4), lax.rem(line, 4)
    z, core = lax.div(column, 2), lax.rem(column, 2)
    me = line * 8 + column
    group = (x * 4 + z) * 2 + core
    order = group * 4 + y

    def unit_of(row, col):
        turn = lax.rem(lax.div(row, 4) + row + lax.div(col, 2), 4)
        return (turn * 2 + lax.rem(col, 2)) * 16 + row

    mine = unit_of(line, column)
    first = mine < 8
    kind = jnp.where(first, 1, 0)
    barrier = pltpu.get_barrier_semaphore()
    loads = [
        pltpu.make_async_copy(src, dst, csem.at[i])
        for i, (src, dst) in enumerate((
            (beams_hbm, beams), (pixels_hbm, px), (bh_hbm, bh), (bl_hbm, bl), (wh_hbm, wh),
            (wl_hbm, wl), (twr_hbm, twr), (twi_hbm, twi), (fmat_hbm, fmat),
            (wrh_hbm, wrh), (wrl_hbm, wrl), (wsh_hbm, wsh), (wsl_hbm, wsl),
            (vrh_hbm, vrh), (vrl_hbm, vrl), (vsh_hbm, vsh), (vsl_hbm, vsl),
            (xh_hbm, xh), (xl_hbm, xl), (tj_hbm, tj),
        ))
    ]
    for load in loads:
        load.start()

    cols = [lax.rem(z + b // 2, 4) * 2 + lax.rem(core + b, 2) for b in range(8)]

    def each(fun):
        def step(a, _):
            def one(b):
                o = lax.rem(a + 5 * b, 16)
                row = lax.rem(x + lax.div(o, 4), 4) * 4 + lax.rem(y + o, 4)
                fun(row * 8 + cols[b], (row, cols[b]))

            for b in (3, 6, 1, 4, 7, 2, 5):
                one(b)

            @pl.when(a > 0)
            def _():
                one(0)

            return 0

        lax.fori_loop(0, 16, step, 0)

    def push(src, dst, k, dev):
        pltpu.make_async_remote_copy(
            src_ref=src, dst_ref=dst, send_sem=ssem.at[k], recv_sem=rsem.at[k],
            device_id=dev, device_id_type=pl.DeviceIdType.MESH,
        ).start()

    def wait(part, sem):
        pltpu.make_async_copy(part, part, sem).wait()

    def keep(src, dst):
        copy = pltpu.make_async_copy(src, dst, lsem)
        copy.start()
        copy.wait()

    each(lambda d, dev: pl.semaphore_signal(
        barrier, inc=1, device_id=dev, device_id_type=pl.DeviceIdType.MESH))
    perm[...] = place(tiles, vc[0], tabs)
    loads[0].wait()
    loads[1].wait()

    def correct(s, _):
        weight = jnp.where(s < vc[0], cw[chan[s]], 0.0)
        one = beams[pair[0, s] * 2 + time[s]].astype(F32)
        two = beams[pair[1, s] * 2 + time[s]].astype(F32)
        gr = (one[0] * two[0] + one[1] * two[1]) * weight
        gi = (one[1] * two[0] - one[0] * two[1]) * weight
        pr, pi = px[s, 0], px[s, 1]
        at = pl.multiple_of(s * 32, 32)
        corr[pl.ds(at, 16), :] = pr * gr - pi * gi
        corr[pl.ds(at + 16, 16), :] = pr * gi + pi * gr
        return 0

    lax.fori_loop(0, 128, correct, 0, unroll=4)

    def coarse(group, _):
        for f in range(2):
            base = group * 16 * 32 + f
            re = [corr[pl.ds(base + 2 * p, 16, stride=32), :] for p in range(8)]
            im = [corr[pl.ds(base + 16 + 2 * p, 16, stride=32), :] for p in range(8)]
            re, im = dft8(re, im)
            rows = pl.ds(pl.multiple_of(f * 128 + group * 16, 16), 16)
            for k in range(8):
                lhi[k, rows, :128], llo[k, rows, :128] = split(re[k])
                lhi[k, rows, 128:], llo[k, rows, 128:] = split(im[k])
        return 0

    lax.fori_loop(0, 8, coarse, 0)
    loads[2].wait()
    loads[3].wait()

    early, late = pl.ds(0, 32), pl.ds(32, 32)
    pl.semaphore_wait(barrier, 127)
    for i in range(1, 4):
        to = lax.rem(y + i, 4)
        push(tabs.at[to], tabr.at[order], 0, (x * 4 + to, column))
    keep(tabs.at[y], tabr.at[order])

    def fine(i, _):
        k = lax.rem(i + lax.div(mine, 16), 8)
        a = jnp.where(k == 0, 0, jnp.where(k == 1, 4, lax.div(k, 2)))
        b = jnp.where(k < 2, a, 8 - a)
        acc = None
        for half, at in enumerate((a, b)):
            h = bh[k, half]
            term = dot(lhi[at], h) + dot(llo[at], h) + dot(lhi[at], bl[k, half])
            acc = term if acc is None else acc + term
        hi, lo = split(acc)
        for f in range(2):
            rows = slice(f * 128, f * 128 + 128)
            padded = dot(perm[...], jnp.concatenate([hi[rows], lo[rows]], axis=0))
            for p in range(2):
                for q in range(4):
                    send[(k * 4 + p * 2 + f) * 4 + q] = (
                        padded[q * 64:(q + 1) * 64, p * 128:(p + 1) * 128]
                    )
        for n in range(16):
            o = n * 7 % 16
            tx, ty = lax.rem(x + o // 4, 4), lax.rem(y + o % 4, 4)
            tz = lax.rem(lax.div(k, 2) + 8 - tx - ty, 4)
            dev = (tx * 4 + ty, tz * 2 + lax.rem(k, 2))
            if o > 0:
                push(send.at[k * 16 + dev[0], early], recv.at[order, early], 1, dev)
            else:
                @pl.when(i > 0)
                def _(dev=dev):
                    push(send.at[k * 16 + dev[0], early], recv.at[order, early], 1, dev)

        return 0

    lax.fori_loop(0, 8, fine, 0)
    wait(tabr.at[pl.ds(0, 3)], rsem.at[0])
    block = tabr.at[pl.ds(group * 4, 4)]

    def share(i, _):
        row = lax.rem(x + lax.div(i, 8), 4) * 4 + y
        col = lax.rem(z + lax.div(i, 2), 4) * 2 + lax.rem(core + i, 2)
        push(block, block, 7, (row, col))
        return 0

    lax.fori_loop(1, 32, share, 0)
    each(lambda d, dev: push(send.at[unit_of(*dev), late], recv.at[order, late], 2, dev))
    keep(send.at[mine], recv.at[order])
    flat = recv.reshape(128 * 64, 128)

    for load in loads[4:9]:
        load.wait()
    wait(tabr.at[pl.ds(0, 124)], rsem.at[7])
    tabt[...] = tabr[...].reshape(128, 128).T
    lane = lax.broadcasted_iota(I32, (32, 128), 1)
    low = lane < 64
    even = (lane & 32) == 0

    shifted = first & (lax.broadcasted_iota(I32, (64, 128), 1) < 64)

    def columns(pm, t):
        g = ghl[pm, pl.ds(pl.multiple_of(t * 256, 256), 256), :]
        for c in range(4):
            rows = slice(c * 128, c * 128 + 128)
            a = dot(wh[rows, :], g)
            b = dot(wl[rows, :], g[:, :128])
            u = a[:, :128] + a[:, 128:] + b
            ur, ui = u[:64], u[64:]
            m0 = slice(c * 64, c * 64 + 64)
            tr, ti = twr[m0, :], twi[m0, :]
            for lanes, value in (
                (slice(0, 128), tr * ur - ti * ui), (slice(128, 256), tr * ui + ti * ur)
            ):
                if pm == 1:
                    value, held[m0, lanes] = jnp.where(shifted, held[m0, lanes], value), value
                pqh[pm, m0, lanes], pql[pm, m0, lanes] = split(value)

    def mix(which, pm):
        both = fmat[kind, which]
        z = dot_nt(both, pqh[pm])
        return z[:128] + z[128:] + dot_nt(both[:128], pql[pm])

    def turn(z, pm, tile):
        lanes = slice(tile * 128, tile * 128 + 128)
        re, im = z[pm * 64:pm * 64 + 32, lanes], z[pm * 64 + 32:pm * 64 + 64, lanes]
        return (
            jnp.where(low, re, pltpu.roll(im, 64, 1)), jnp.where(low, pltpu.roll(re, 64, 1), im)
        )

    def emit(z, t):
        for pm in range(2):
            for tile in range(2):
                for q, rows in enumerate(turn(z, pm, tile)):
                    stage[pl.ds((2 * tile + q) * 64 + 2 * t + pm, 32, stride=256), :] = rows

    def emit_by_m(z, t):
        for tile in range(2):
            a = [z[i * 32:i * 32 + 32, tile * 128:tile * 128 + 128] for i in range(4)]
            c = [
                jnp.where(low, a[0], pltpu.roll(a[2], 64, 1)), jnp.where(low, a[1], pltpu.roll(a[3], 64, 1)),
                jnp.where(low, pltpu.roll(a[0], 64, 1), a[2]), jnp.where(low, pltpu.roll(a[1], 64, 1), a[3]),
            ]
            for q in range(2):
                b = (
                    jnp.where(even, c[2 * q], pltpu.roll(c[2 * q + 1], 32, 1)),
                    jnp.where(even, pltpu.roll(c[2 * q], 96, 1), c[2 * q + 1]),
                )
                for h in range(2):
                    at = (2 * tile + q) * 64 + 32 + 16 * h
                    stage[pl.ds(at + t, 32, stride=256), :] = b[h]

    def gather(rp):
        for pm in range(2):
            def block(c, _, pm=pm):
                at = rp * 32 + pm * 16 + 2 * c
                key = jnp.concatenate([tabt[pl.ds(at + k, 1), :] for k in range(2)], axis=1)
                parts = [split(flat[pl.ds(at + k, 128, stride=64), :]) for k in range(2)]
                rhs = jnp.concatenate([jnp.concatenate(p, axis=1) for p in parts], axis=0)
                for chunk in range(4):
                    tile = lax.broadcasted_iota(I32, (128, 256), 0) + chunk * 128
                    hit = jnp.where(tile == key, 1.0, 0.0).astype(BF)
                    s = dot(hit, rhs)
                    hi, lo = split(s[:, :128] + s[:, 128:])
                    for i in range(4):
                        to = pl.multiple_of((chunk * 4 + i) * 256 + c * 32, 32)
                        ghl[pm, pl.ds(to, 32), :128] = hi[i * 32:i * 32 + 32]
                        ghl[pm, pl.ds(to, 32), 128:] = lo[i * 32:i * 32 + 32]
                return 0

            lax.fori_loop(0, 8, block, 0)
        held[...] = jnp.zeros((256, 256), F32)

    def phase(rp):
        gather(rp)

        def row(t, _):
            columns(0, t)
            columns(1, 15 - t)
            z = mix(0, 0) + mix(1, 1)
            if rp == 0:
                emit(z, t)
            else:
                emit_by_m(z, t)
            return 0

        lax.fori_loop(0, 16, row, 0)

        @pl.when(first)
        def _():
            for lanes in (slice(0, 128), slice(128, 256)):
                pqh[1, :, lanes], pql[1, :, lanes] = split(held[:, lanes])
            edge = mix(1, 1)
            for tile in range(2):
                for q, rows in enumerate(turn(edge, 0, tile)):
                    for m in range(32):
                        extra[m * 4 + 2 * tile + q, rp:rp + 1, :] = rows[m:m + 1]

    def deliver(start, size, k):
        rows = pl.ds(start, size)

        def piece(d):
            return stage.at[pl.ds(pl.multiple_of(d * 64 + start, 16), size), :]

        each(lambda d, dev: push(piece(d), got.at[mine, rows], k, dev))
        keep(piece(me), got.at[mine, rows])

    wait(recv.at[pl.ds(0, 127), early], rsem.at[1])
    phase(0)
    deliver(0, 32, 4)
    wait(recv.at[pl.ds(0, 127), late], rsem.at[2])
    phase(1)
    deliver(32, 16, 5)
    deliver(48, 16, 6)

    @pl.when(first)
    def _():
        each(lambda d, dev: push(extra.at[d], gotx.at[mine], 3, dev))
        keep(extra.at[me], gotx.at[mine])

    wait(send.at[pl.ds(0, 127), early], ssem.at[1])
    wait(send.at[pl.ds(0, 127), late], ssem.at[2])
    for load in loads[9:]:
        load.wait()
    wait(got.at[pl.ds(0, 127), early], rsem.at[4])

    def transform(n, _):
        f, group = lax.div(n, 4), lax.rem(n, 4)
        turned = row_dft(
            [[got[((4 * group + k) * 2 + f) * 4 + q, :32, :] for q in range(4)] for k in range(4)],
            (wrh, wrl), tj, group,
        )
        for k in range(16):
            send[n * 16 + k] = turned[k]

        @pl.when(group == 0)
        def _():
            for k, v in enumerate(row_dft_zero([got[f * 4 + q, :32, :] for q in range(4)], (wsh, wsl))):
                send[n * 16 + k] = v

        return 0

    lax.fori_loop(0, 8, transform, 0)

    def finish(n, _, h):
        f, group = lax.div(n, 4), lax.rem(n, 4)
        here = slice(h * 32, h * 32 + 32)
        parts = []
        for k in range(4):
            base = ((4 * group + k) * 2 + f) * 4
            v = jnp.concatenate(
                [got[base + q, 32 + 16 * h:48 + 16 * h, :] for q in range(4)], axis=0
            )
            hi = v.astype(BF).astype(F32)
            a = jnp.concatenate([hi, v - hi], axis=0).T.astype(BF)
            parts.append(jnp.concatenate([a[:64], a[64:]], axis=1))
        a = jnp.concatenate(parts, axis=0)
        u = dot(a, vrh[...]) + dot(a, vrl[...])

        def add(k, pieces):
            for i, v in enumerate(pieces):
                send[n * 16 + 4 * k + i, here, :] += v

        for k in range(4):
            v = u[k * 64:k * 64 + 64]
            re, im = v[:32, :256] - v[32:, 256:], v[:32, 256:] + v[32:, :256]
            tr, ti = tj[4 * group + k, 0:1, :], tj[4 * group + k, 1:2, :]
            pieces = halves(re * tr - im * ti, re * ti + im * tr)
            if k > 0:
                add(k, pieces)
            else:
                @pl.when(group > 0)
                def _(pieces=pieces):
                    add(0, pieces)

        @pl.when(group == 0)
        def _():
            for q in range(4):
                edges[2 * q:2 * q + 2, :] = gotx[f * 4 + q]
            edge = jnp.concatenate([edges[...], jnp.zeros((120, 128), F32)], axis=0).T[:, :32]
            v = three(edge[h * 32:h * 32 + 32], (xh[0], xl[0]))
            v = v + three(edge[64 + h * 32:96 + h * 32], (xh[1], xl[1]))
            for i in range(2):
                one = parts[0][i * 32:i * 32 + 32]
                v = v + dot(one, vsh[i]) + dot(one, vsl[i])
            add(0, halves(v[:, :256], v[:, 256:]))

        return 0

    @pl.when(first)
    def _():
        wait(gotx.at[pl.ds(0, 7)], rsem.at[3])

    @pl.when(mine >= 8)
    def _():
        wait(gotx, rsem.at[3])

    for h in range(2):
        wait(got.at[pl.ds(0, 127), pl.ds(h * 16, 16)], rsem.at[5 + h])

        def picture(f, _, h=h):
            lax.fori_loop(4 * f, 4 * f + 4, functools.partial(finish, h=h), 0)

            if h == 0:
                paint(lambda k, at: send[f * 64 + k, at, :], image.at[f], out.at[f], lsem)
            else:
                mine_f = pl.ds(f * 64, 64)
                pltpu.make_async_copy(send.at[mine_f, late], rest.at[mine_f], msem).start()
            return 0

        lax.fori_loop(0, 2, picture, 0)
    wait(out, lsem)
    wait(rest, msem)

    @pl.when(first)
    def _():
        wait(extra.at[pl.ds(0, 127)], ssem.at[3])

    wait(tabr.at[pl.ds(0, 3)], ssem.at[0])
    wait(tabr.at[pl.ds(0, 124)], ssem.at[7])
    wait(got.at[pl.ds(0, 127), early], ssem.at[4])
    for p in range(2):
        wait(got.at[pl.ds(0, 127), pl.ds(p * 16, 16)], ssem.at[5 + p])


def exchange(tiles, pair, time, chan, count, weights, pixels, beams):
    t = tables()
    smem = pl.BlockSpec(memory_space=pltpu.SMEM)
    away = pl.BlockSpec(memory_space=pl.ANY)
    constants = (*t["b"], *t["wc"], *t["tw"], t["f"], *t["wr"], *t["ws"], *t["vr"], *t["vs"], *t["wx"], t["tj"])
    return pl.pallas_call(
        exchange_kernel,
        out_shape=(
            jax.ShapeDtypeStruct((2, 32, 8192), F32), jax.ShapeDtypeStruct((128, 32, 128), F32)
        ),
        in_specs=[pl.BlockSpec(memory_space=pltpu.VMEM)] + [smem] * 5 + [away] * 20,
        out_specs=(away, away),
        scratch_shapes=[
            pltpu.VMEM((128, 2, 16, 128), F32),
            pltpu.VMEM((1024, 2, 16, 128), BF),
            pltpu.VMEM((8, 2, 256, 256), BF),
            pltpu.VMEM((8, 2, 256, 256), BF),
            pltpu.VMEM((512, 256), BF),
            pltpu.VMEM((512, 256), BF),
            pltpu.VMEM((256, 128), F32),
            pltpu.VMEM((256, 128), F32),
            pltpu.VMEM((2, 2, 256, 256), BF),
            pltpu.VMEM((128, 512), BF),
            pltpu.VMEM((128, 512), BF),
            pltpu.VMEM((2, 128, 512), BF),
            pltpu.VMEM((2, 128, 512), BF),
            pltpu.VMEM((256, 512), BF),
            pltpu.VMEM((256, 512), BF),
            pltpu.VMEM((2, 256, 512), BF),
            pltpu.VMEM((2, 256, 512), BF),
            pltpu.VMEM((2, 32, 512), BF),
            pltpu.VMEM((2, 32, 512), BF),
            pltpu.VMEM((16, 2, 256), F32),
            pltpu.VMEM((128 * 32, 128), F32),
            pltpu.VMEM((8, 256, 256), BF),
            pltpu.VMEM((8, 256, 256), BF),
            pltpu.VMEM((256, 256), BF),
            pltpu.VMEM((128, 64, 128), F32),
            pltpu.VMEM((4, 1, 128), I32),
            pltpu.VMEM((128, 64, 128), F32),
            pltpu.VMEM((128, 1, 128), I32),
            pltpu.VMEM((128, 128), I32),
            pltpu.VMEM((2, 16 * 256, 256), BF),
            pltpu.VMEM((2, 256, 256), BF),
            pltpu.VMEM((2, 256, 256), BF),
            pltpu.VMEM((256, 256), F32),
            pltpu.VMEM((128 * 64, 128), F32),
            pltpu.VMEM((128, 2, 128), F32),
            pltpu.VMEM((128, 64, 128), F32),
            pltpu.VMEM((8, 2, 128), F32),
            pltpu.VMEM((8, 128), F32),
            pltpu.VMEM((2, 32, 8192), F32),
            pltpu.SemaphoreType.DMA((8,)),
            pltpu.SemaphoreType.DMA((8,)),
            pltpu.SemaphoreType.DMA,
            pltpu.SemaphoreType.DMA,
            pltpu.SemaphoreType.DMA((20,)),
        ],
        compiler_params=pltpu.CompilerParams(
            vmem_limit_bytes=VMEM, collective_id=0, has_side_effects=True
        ),
        name="exchange",
    )(tiles, pair, time, chan, count, weights, pixels, beams, *constants)


def final_kernel(half, rest, out, val, through, image, sems):
    parts = [(rest.at[pl.ds(f * 64, 64)], val.at[f]) for f in range(2)]
    parts += [(half.at[f], through.at[f]) for f in range(2)]
    loads = [pltpu.make_async_copy(src, dst, sems.at[i]) for i, (src, dst) in enumerate(parts)]
    for load in loads:
        load.start()
    for f in range(2):
        loads[f].wait()
        paint(lambda k, at: val[f, k, at, :], image.at[f], out.at[f, pl.ds(32, 32), :], sems.at[4])
        loads[2 + f].wait()
        pltpu.make_async_copy(through.at[f], out.at[f, pl.ds(0, 32), :], sems.at[5]).start()
    pltpu.make_async_copy(image, image, sems.at[4]).wait()
    pltpu.make_async_copy(through, through, sems.at[5]).wait()


def final(half, rest):
    away = pl.BlockSpec(memory_space=pl.ANY)
    return pl.pallas_call(
        final_kernel,
        out_shape=jax.ShapeDtypeStruct((2, 64, 8192), F32),
        in_specs=[away, away],
        out_specs=away,
        scratch_shapes=[
            pltpu.VMEM((2, 64, 32, 128), F32),
            pltpu.VMEM((2, 32, 8192), F32),
            pltpu.VMEM((2, 32, 8192), F32),
            pltpu.SemaphoreType.DMA((6,)),
        ],
        compiler_params=pltpu.CompilerParams(vmem_limit_bytes=VMEM),
        name="final",
    )(half, rest)


def pixel_view(pixels):
    x = pixels.reshape(128, 2, 2, 8, 128).transpose(0, 1, 3, 2, 4)
    return x.reshape(128, 2, 16, 128)


def beam_view(aterms):
    x = aterms.reshape(512, 2, 2, 2, 8, 128).transpose(0, 1, 2, 4, 3, 5)
    return x.reshape(1024, 2, 16, 128)


def local(
    subgrid_pixels, tile_offsets, station_pairs, time_blocks, channel_blocks, valid_counts,
    aterms, channel_weights,
):
    return final(*exchange(
        tile_offsets.T, station_pairs.T, time_blocks, channel_blocks, valid_counts, channel_weights,
        pixel_view(subgrid_pixels), beam_view(aterms),
    ))


def solution(mesh):
    in_specs = (
        P(("row", "col"), None, None, None),
        P(("row", "col"), None),
        P(("row", "col"), None),
        P(("row", "col")),
        P(("row", "col")),
        P(("row", "col")),
        P(),
        P(),
    )
    out_specs = P(None, ("row", "col"), None)
    return jax.shard_map(local, mesh=mesh, in_specs=in_specs, out_specs=out_specs, check_vma=False)
```

```python
import functools
import math

import jax
import jax.numpy as jnp
import ml_dtypes
import numpy as np
from jax import lax
from jax.experimental import pallas as pl
from jax.experimental.pallas import tpu as pltpu
from jax.sharding import PartitionSpec as P

BF = jnp.bfloat16
F32 = jnp.float32
I32 = jnp.int32

PAIR_J = (0, 8, 4, 12, 1, 9, 17, 25, 2, 10, 18, 26, 3, 11, 19, 27)
VMEM = 56 * 1024 * 1024


def partner(j):
    return 16 if j == 0 else 32 - j


def unit(turns):
    return np.exp(-2j * np.pi * turns)


def split_np(x):
    hi = np.asarray(x, np.float32).astype(ml_dtypes.bfloat16)
    lo = (np.asarray(x, np.float64) - hi.astype(np.float64)).astype(ml_dtypes.bfloat16)
    return hi, lo


def split(x):
    hi = x.astype(BF)
    return hi, (x - hi.astype(F32)).astype(BF)


def dot(a, b):
    return lax.dot_general(a, b, (((1,), (0,)), ((), ())), preferred_element_type=F32)


def dot_nt(a, b):
    return lax.dot_general(a, b, (((1,), (1,)), ((), ())), preferred_element_type=F32)


@functools.lru_cache(None)
def tables():
    xi = np.arange(4)[:, None, None]
    y = np.arange(32)[None, :, None]
    v = np.arange(32)[None, None, :]
    b = np.zeros((8, 2, 2, 4, 32, 2, 2, 2, 32))
    for step in range(8):
        for pair in range(2):
            j = PAIR_J[2 * step + pair]
            for half, jj in enumerate((j, partner(j))):
                w = unit((xi * jj + y * v) % 32 / 32) / 32
                b[step, half, 0, :, :, pair, half, 0] = w.real
                b[step, half, 0, :, :, pair, half, 1] = w.imag
                b[step, half, 1, :, :, pair, half, 0] = -w.imag
                b[step, half, 1, :, :, pair, half, 1] = w.real
    b = b.reshape(8, 2, 256, 256)
    i = np.arange(256)
    w = unit(i[:, None] * i[None, :] % 256 / 256)
    wc = np.stack([w.real.reshape(4, 64, 256), w.imag.reshape(4, 64, 256)], 1).reshape(512, 256)
    tw = unit(i[:, None] * (np.arange(128) % 32)[None, :] / 8192)
    d = unit(np.arange(32)[:, None] * np.arange(32)[None, :] % 32 / 32)
    coef = np.stack([np.stack([d, 1j * d]), np.stack([1j * d, -d])])
    f = np.zeros((2, 2, 2, 2, 32, 2, 2, 2, 32))

    def put(kind, which, half, pm, conj):
        for pq in range(2):
            for reim in range(2):
                c = coef[pq, reim]
                f[kind, which, pm, 0, :, pq, half, reim, :] = c.real
                f[kind, which, pm, 1, :, pq, half, reim, :] = -c.imag if conj else c.imag

    put(0, 0, 0, 0, False)
    put(0, 0, 1, 1, True)
    put(0, 1, 1, 0, True)
    put(0, 1, 0, 1, False)
    put(1, 0, 0, 0, False)
    put(1, 0, 1, 1, False)
    put(1, 1, 1, 1, True)
    put(1, 1, 0, 0, True)
    f = f.reshape(2, 2, 128, 256)
    fh, fl = split_np(f)
    f = np.concatenate([fh, fl], axis=2)
    k = np.arange(256)
    q, rp, t, pm = k // 64, k // 32 % 2, k // 2 % 16, k % 2
    r = 16 * (2 * q + rp) + t
    rr = np.where(pm == 0, r, 255 - r)
    l0 = np.arange(256)
    w = unit(rr[:, None] * l0[None, :] % 256 / 256) / 4096
    wr = np.concatenate([w.real, w.imag], axis=1)
    w0 = np.where((pm == 0)[:, None], unit(r[:, None] * l0[None, :] % 256 / 256), 0) / 4096
    w16 = np.where((pm == 1)[:, None], unit((32 * r[:, None] + 16) * l0[None, :] % 8192 / 8192), 0) / 4096
    ws = np.stack([np.concatenate([w0.real, w16.real], 1), np.concatenate([-w0.imag, -w16.imag], 1)])
    kx = np.arange(32)
    qx, row = kx // 2 % 4, kx % 2
    rx = 16 * (15 - (2 * qx + row))
    wx = np.where((kx < 8)[:, None], unit(-(rx[:, None] * l0[None, :] % 256) / 256), 0) / 4096
    zero = np.zeros_like(wx.real)
    wx = np.stack([np.concatenate([wx.real, zero], 1), np.concatenate([-wx.imag, zero], 1)])
    tj = unit(np.array(PAIR_J)[:, None] * l0[None, :] / 8192)
    tj = np.stack([tj.real, tj.imag], 1).astype(np.float32)
    wr, ws = wr.reshape(4, 2, 32, 512), ws.reshape(2, 4, 2, 32, 512)
    late = [w.reshape(*w.shape[:-2], 16, 2, 512) for w in (wr[:, 1], ws[:, :, 1])]
    wr = split_np(wr[:, 0].reshape(128, 512))
    ws = split_np(ws[:, :, 0].reshape(2, 128, 512))

    def doubled(w):
        h, l = split_np(w)
        shape = (*w.shape[:-4], 256, 512)
        return (
            np.stack([h, h], axis=-4).reshape(shape),
            np.stack([l, np.zeros_like(l)], axis=-4).reshape(shape),
        )

    vr = doubled(late[0].transpose(2, 0, 1, 3))
    vs = doubled(late[1].transpose(0, 3, 1, 2, 4))
    return dict(
        b=split_np(b), wc=split_np(wc), tw=(tw.real.astype(np.float32), tw.imag.astype(np.float32)),
        f=f, wr=wr, ws=ws, vr=vr, vs=vs, wx=split_np(wx), tj=tj,
    )


def dft8(re, im):
    h = math.sqrt(0.5)

    def four(a, b):
        s0r, s0i = a[0] + a[2], b[0] + b[2]
        s1r, s1i = a[0] - a[2], b[0] - b[2]
        s2r, s2i = a[1] + a[3], b[1] + b[3]
        s3r, s3i = a[1] - a[3], b[1] - b[3]
        return (
            [s0r + s2r, s1r + s3i, s0r - s2r, s1r - s3i],
            [s0i + s2i, s1i - s3r, s0i - s2i, s1i + s3r],
        )

    er, ei = four(re[0::2], im[0::2])
    orr, oi = four(re[1::2], im[1::2])
    tr = [orr[0], (orr[1] + oi[1]) * h, oi[2], (oi[3] - orr[3]) * h]
    ti = [oi[0], (oi[1] - orr[1]) * h, -orr[2], -(oi[3] + orr[3]) * h]
    return (
        [er[k] + tr[k] for k in range(4)] + [er[k] - tr[k] for k in range(4)],
        [ei[k] + ti[k] for k in range(4)] + [ei[k] - ti[k] for k in range(4)],
    )


def place(tiles, count, tabs):
    row, col = tiles[0:1, :], tiles[1:2, :]
    block_row = lax.shift_right_logical(row, 4)
    low = block_row < 8
    near = jnp.where(low, block_row, 15 - block_row)
    block = (near * 2 + jnp.where(low, 0, 1)) * 8 + lax.shift_right_logical(col, 5)
    tile = (row & 15) * 32 + (col & 31)
    down = lax.broadcasted_iota(I32, (128, 128), 0)
    along = lax.broadcasted_iota(I32, (128, 128), 1)

    def column(x):
        return jnp.broadcast_to(x, (128, 128)).T

    earlier = (column(block) == block) & (down < along)
    rank = jnp.sum(jnp.where(earlier, 1.0, 0.0), axis=0, keepdims=True)
    slot = block * 2 + jnp.where(rank > 0.5, 1, 0)
    slot = jnp.where(along[0:1] < count, slot, -1)
    slots, tile = column(slot), column(tile).astype(F32)
    for q in range(4):
        tabs[q] = jnp.sum(jnp.where(slots == along + 64 * q, tile, 0.0), axis=0, keepdims=True).astype(I32)
    hit = jnp.where(lax.broadcasted_iota(I32, (256, 128), 0) == slot, 1.0, 0.0).astype(BF)
    return jnp.concatenate([hit, hit], axis=1)


def three(a, b):
    ah, al = split(a)
    return dot(ah, b[0]) + dot(al, b[0]) + dot(ah, b[1])


def halves(re, im):
    return [re[:, :128], re[:, 128:], im[:, :128], im[:, 128:]]


def row_dft(blocks, w, tj, group):
    a = jnp.concatenate([jnp.concatenate(b, axis=0).T for b in blocks], axis=0)
    u = three(a, (w[0][...], w[1][...]))
    outs = []
    for k in range(4):
        v = u[k * 128:k * 128 + 128]
        vr = v[:64, :256] - v[64:, 256:]
        vi = v[:64, 256:] + v[64:, :256]
        tr, ti = tj[4 * group + k, 0:1, :], tj[4 * group + k, 1:2, :]
        outs += halves(vr * tr - vi * ti, vr * ti + vi * tr)
    return outs


def row_dft_zero(block, w):
    a = jnp.concatenate(block, axis=0).T
    v = three(a[:64], (w[0][0], w[1][0])) + three(a[64:], (w[0][1], w[1][1]))
    return halves(v[:, :256], v[:, 256:])


def mix_pairs(load):
    index = {}
    for i, j in enumerate(PAIR_J):
        if i > 0:
            index[j if j < 16 else 32 - j] = (i, 1.0 if j < 16 else -1.0)
    zero, mid = load(0, 0), load(0, 1)
    re = {j: load(k, 0) for j, (k, _) in index.items()}
    im = {j: load(k, 1) for j, (k, _) in index.items()}

    def wave(fun, part, js, l1, signed):
        total = jnp.zeros((8, 128), F32)
        started = False
        for j in js:
            c = fun(2 * math.pi * (j * l1 % 32) / 32) * (index[j][1] if signed else 1.0)
            if abs(c) < 1e-12:
                continue
            term = part[j] if abs(abs(c) - 1) < 1e-12 else part[j] * abs(c)
            if started:
                total = total + term if c > 0 else total - term
            else:
                total = term if c > 0 else -term
            started = True
        return total

    odd, even, four = range(1, 16, 2), (2, 6, 10, 14), (4, 8, 12)
    ce, se = [None] * 9, [None] * 9
    for l1 in range(5):
        ee = wave(math.cos, re, four, l1, False) + (zero + mid if l1 % 2 == 0 else zero - mid)
        eo = wave(math.cos, re, even, l1, False)
        oe = wave(math.sin, im, four, l1, True)
        oo = wave(math.sin, im, even, l1, True)
        ce[l1], ce[8 - l1] = ee + eo, ee - eo
        se[l1], se[8 - l1] = oe + oo, oo - oe
    outs = []
    for l1 in range(9):
        co = wave(math.cos, re, odd, l1, False)
        so = wave(math.sin, im, odd, l1, True)
        p, m = ce[l1] + co, ce[l1] - co
        s, d = se[l1] + so, se[l1] - so
        outs += [(l1, p + s), (16 + l1, m + d)]
        if l1 > 0:
            outs.append((32 - l1, p - s))
            if l1 < 8:
                outs.append((16 - l1, m - d))
    return outs


def paint(load, image, out, sem):
    def strip(i, _):
        at = pl.ds(pl.multiple_of(i * 8, 8), 8)
        for tile in range(2):
            for l, value in mix_pairs(lambda k, part: load(4 * k + 2 * part + tile, at)):
                image[at, l * 256 + tile * 128:l * 256 + tile * 128 + 128] = value
        pltpu.make_async_copy(image.at[at, :], out.at[at, :], sem).start()
        return 0

    lax.fori_loop(0, 4, strip, 0)


def exchange_kernel(
    tiles, pair, time, chan, vc, cw, pixels_hbm, beams_hbm, bh_hbm, bl_hbm,
    wh_hbm, wl_hbm, twr_hbm, twi_hbm, fmat_hbm,
    wrh_hbm, wrl_hbm, wsh_hbm, wsl_hbm, vrh_hbm, vrl_hbm, vsh_hbm, vsl_hbm, xh_hbm, xl_hbm, tj_hbm, out, rest,
    px, beams, bh, bl, wh, wl, twr, twi, fmat, wrh, wrl, wsh, wsl, vrh, vrl, vsh, vsl, xh, xl, tj,
    corr, lhi, llo, perm, send, tabs,
    recv, tabr, tabt, ghl, pqh, pql, held, stage, extra, got, gotx, edges, image, ssem, rsem, lsem, msem, csem
):
    line, column = lax.axis_index("row"), lax.axis_index("col")
    x, y = lax.div(line, 4), lax.rem(line, 4)
    z, core = lax.div(column, 2), lax.rem(column, 2)
    me = line * 8 + column
    group = (x * 4 + z) * 2 + core
    order = group * 4 + y

    def unit_of(row, col):
        turn = lax.rem(lax.div(row, 4) + row + lax.div(col, 2), 4)
        return (turn * 2 + lax.rem(col, 2)) * 16 + row

    mine = unit_of(line, column)
    first = mine < 8
    kind = jnp.where(first, 1, 0)
    barrier = pltpu.get_barrier_semaphore()
    loads = [
        pltpu.make_async_copy(src, dst, csem.at[i])
        for i, (src, dst) in enumerate((
            (beams_hbm, beams), (pixels_hbm, px), (bh_hbm, bh), (bl_hbm, bl), (wh_hbm, wh),
            (wl_hbm, wl), (twr_hbm, twr), (twi_hbm, twi), (fmat_hbm, fmat),
            (wrh_hbm, wrh), (wrl_hbm, wrl), (wsh_hbm, wsh), (wsl_hbm, wsl),
            (vrh_hbm, vrh), (vrl_hbm, vrl), (vsh_hbm, vsh), (vsl_hbm, vsl),
            (xh_hbm, xh), (xl_hbm, xl), (tj_hbm, tj),
        ))
    ]
    for load in loads:
        load.start()

    cols = [lax.rem(z + b // 2, 4) * 2 + lax.rem(core + b, 2) for b in range(8)]

    def each(fun):
        def step(a, _):
            def one(b):
                o = lax.rem(a + 5 * b, 16)
                row = lax.rem(x + lax.div(o, 4), 4) * 4 + lax.rem(y + o, 4)
                fun(row * 8 + cols[b], (row, cols[b]))

            for b in (3, 6, 1, 4, 7, 2, 5):
                one(b)

            @pl.when(a > 0)
            def _():
                one(0)

            return 0

        lax.fori_loop(0, 16, step, 0)

    def push(src, dst, k, dev):
        pltpu.make_async_remote_copy(
            src_ref=src, dst_ref=dst, send_sem=ssem.at[k], recv_sem=rsem.at[k],
            device_id=dev, device_id_type=pl.DeviceIdType.MESH,
        ).start()

    def wait(part, sem):
        pltpu.make_async_copy(part, part, sem).wait()

    def keep(src, dst):
        copy = pltpu.make_async_copy(src, dst, lsem)
        copy.start()
        copy.wait()

    each(lambda d, dev: pl.semaphore_signal(
        barrier, inc=1, device_id=dev, device_id_type=pl.DeviceIdType.MESH))
    perm[...] = place(tiles, vc[0], tabs)
    loads[0].wait()
    loads[1].wait()

    def correct(s, _):
        weight = jnp.where(s < vc[0], cw[chan[s]], 0.0)
        one = beams[pair[0, s] * 2 + time[s]].astype(F32)
        two = beams[pair[1, s] * 2 + time[s]].astype(F32)
        gr = (one[0] * two[0] + one[1] * two[1]) * weight
        gi = (one[1] * two[0] - one[0] * two[1]) * weight
        pr, pi = px[s, 0], px[s, 1]
        at = pl.multiple_of(s * 32, 32)
        corr[pl.ds(at, 16), :] = pr * gr - pi * gi
        corr[pl.ds(at + 16, 16), :] = pr * gi + pi * gr
        return 0

    lax.fori_loop(0, 128, correct, 0, unroll=4)

    def coarse(group, _):
        for f in range(2):
            base = group * 16 * 32 + f
            re = [corr[pl.ds(base + 2 * p, 16, stride=32), :] for p in range(8)]
            im = [corr[pl.ds(base + 16 + 2 * p, 16, stride=32), :] for p in range(8)]
            re, im = dft8(re, im)
            rows = pl.ds(pl.multiple_of(f * 128 + group * 16, 16), 16)
            for k in range(8):
                lhi[k, rows, :128], llo[k, rows, :128] = split(re[k])
                lhi[k, rows, 128:], llo[k, rows, 128:] = split(im[k])
        return 0

    lax.fori_loop(0, 8, coarse, 0)
    loads[2].wait()
    loads[3].wait()

    early, late = pl.ds(0, 32), pl.ds(32, 32)
    pl.semaphore_wait(barrier, 127)
    for i in range(1, 4):
        to = lax.rem(y + i, 4)
        push(tabs.at[to], tabr.at[order], 0, (x * 4 + to, column))
    tabr[order] = tabs[y]

    def fine(i, _):
        @pl.when(i == 2)
        def _():
            wait(tabr.at[pl.ds(0, 3)], rsem.at[0])
            block = tabr.at[pl.ds(group * 4, 4)]

            def share(i, _):
                row = lax.rem(x + lax.div(i, 8), 4) * 4 + y
                col = lax.rem(z + lax.div(i, 2), 4) * 2 + lax.rem(core + i, 2)
                push(block, block, 7, (row, col))
                return 0

            lax.fori_loop(1, 32, share, 0)

        k = lax.rem(i + lax.div(mine, 16), 8)
        a = jnp.where(k == 0, 0, jnp.where(k == 1, 4, lax.div(k, 2)))
        b = jnp.where(k < 2, a, 8 - a)
        acc = None
        for half, at in enumerate((a, b)):
            h = bh[k, half]
            term = dot(lhi[at], h) + dot(llo[at], h) + dot(lhi[at], bl[k, half])
            acc = term if acc is None else acc + term
        hi, lo = split(acc)
        for f in range(2):
            rows = slice(f * 128, f * 128 + 128)
            padded = dot(perm[...], jnp.concatenate([hi[rows], lo[rows]], axis=0))
            for p in range(2):
                for q in range(4):
                    send[(k * 4 + p * 2 + f) * 4 + q] = (
                        padded[q * 64:(q + 1) * 64, p * 128:(p + 1) * 128]
                    )
        for n in range(16):
            o = n * 7 % 16
            tx, ty = lax.rem(x + o // 4, 4), lax.rem(y + o % 4, 4)
            tz = lax.rem(lax.div(k, 2) + 8 - tx - ty, 4)
            dev = (tx * 4 + ty, tz * 2 + lax.rem(k, 2))
            if o > 0:
                push(send.at[k * 16 + dev[0], early], recv.at[order, early], 1, dev)
            else:
                @pl.when(i > 0)
                def _(dev=dev):
                    push(send.at[k * 16 + dev[0], early], recv.at[order, early], 1, dev)

        return 0

    lax.fori_loop(0, 8, fine, 0)
    each(lambda d, dev: push(send.at[unit_of(*dev), late], recv.at[order, late], 2, dev))
    keep(send.at[mine], recv.at[order])
    flat = recv.reshape(128 * 64, 128)

    for load in loads[4:9]:
        load.wait()
    wait(tabr.at[pl.ds(0, 124)], rsem.at[7])
    tabt[...] = tabr[...].reshape(128, 128).T
    lane = lax.broadcasted_iota(I32, (32, 128), 1)
    low = lane < 64
    even = (lane & 32) == 0

    shifted = first & (lax.broadcasted_iota(I32, (64, 128), 1) < 64)

    def columns(pm, t):
        g = ghl[pm, pl.ds(pl.multiple_of(t * 256, 256), 256), :]
        for c in range(4):
            rows = slice(c * 128, c * 128 + 128)
            a = dot(wh[rows, :], g)
            b = dot(wl[rows, :], g[:, :128])
            u = a[:, :128] + a[:, 128:] + b
            ur, ui = u[:64], u[64:]
            m0 = slice(c * 64, c * 64 + 64)
            tr, ti = twr[m0, :], twi[m0, :]
            for lanes, value in (
                (slice(0, 128), tr * ur - ti * ui), (slice(128, 256), tr * ui + ti * ur)
            ):
                if pm == 1:
                    value, held[m0, lanes] = jnp.where(shifted, held[m0, lanes], value), value
                pqh[pm, m0, lanes], pql[pm, m0, lanes] = split(value)

    def mix(which, pm):
        both = fmat[kind, which]
        z = dot_nt(both, pqh[pm])
        return z[:128] + z[128:] + dot_nt(both[:128], pql[pm])

    def turn(z, pm, tile):
        lanes = slice(tile * 128, tile * 128 + 128)
        re, im = z[pm * 64:pm * 64 + 32, lanes], z[pm * 64 + 32:pm * 64 + 64, lanes]
        return (
            jnp.where(low, re, pltpu.roll(im, 64, 1)), jnp.where(low, pltpu.roll(re, 64, 1), im)
        )

    def emit(z, t):
        for pm in range(2):
            for tile in range(2):
                for q, rows in enumerate(turn(z, pm, tile)):
                    stage[pl.ds((2 * tile + q) * 64 + 2 * t + pm, 32, stride=256), :] = rows

    def emit_by_m(z, t):
        for tile in range(2):
            a = [z[i * 32:i * 32 + 32, tile * 128:tile * 128 + 128] for i in range(4)]
            c = [
                jnp.where(low, a[0], pltpu.roll(a[2], 64, 1)), jnp.where(low, a[1], pltpu.roll(a[3], 64, 1)),
                jnp.where(low, pltpu.roll(a[0], 64, 1), a[2]), jnp.where(low, pltpu.roll(a[1], 64, 1), a[3]),
            ]
            for q in range(2):
                b = (
                    jnp.where(even, c[2 * q], pltpu.roll(c[2 * q + 1], 32, 1)),
                    jnp.where(even, pltpu.roll(c[2 * q], 96, 1), c[2 * q + 1]),
                )
                for h in range(2):
                    at = (2 * tile + q) * 64 + 32 + 16 * h
                    stage[pl.ds(at + t, 32, stride=256), :] = b[h]

    def gather(rp):
        for pm in range(2):
            def block(c, _, pm=pm):
                at = rp * 32 + pm * 16 + 2 * c
                key = jnp.concatenate([tabt[pl.ds(at + k, 1), :] for k in range(2)], axis=1)
                parts = [split(flat[pl.ds(at + k, 128, stride=64), :]) for k in range(2)]
                rhs = jnp.concatenate([jnp.concatenate(p, axis=1) for p in parts], axis=0)
                for chunk in range(4):
                    tile = lax.broadcasted_iota(I32, (128, 256), 0) + chunk * 128
                    hit = jnp.where(tile == key, 1.0, 0.0).astype(BF)
                    s = dot(hit, rhs)
                    hi, lo = split(s[:, :128] + s[:, 128:])
                    for i in range(4):
                        to = pl.multiple_of((chunk * 4 + i) * 256 + c * 32, 32)
                        ghl[pm, pl.ds(to, 32), :128] = hi[i * 32:i * 32 + 32]
                        ghl[pm, pl.ds(to, 32), 128:] = lo[i * 32:i * 32 + 32]
                return 0

            lax.fori_loop(0, 8, block, 0)
        held[...] = jnp.zeros((256, 256), F32)

    def phase(rp):
        gather(rp)

        def row(t, _):
            columns(0, t)
            columns(1, 15 - t)
            z = mix(0, 0) + mix(1, 1)
            if rp == 0:
                emit(z, t)
            else:
                emit_by_m(z, t)
            return 0

        lax.fori_loop(0, 16, row, 0)

        @pl.when(first)
        def _():
            for lanes in (slice(0, 128), slice(128, 256)):
                pqh[1, :, lanes], pql[1, :, lanes] = split(held[:, lanes])
            edge = mix(1, 1)
            for tile in range(2):
                for q, rows in enumerate(turn(edge, 0, tile)):
                    for m in range(32):
                        extra[m * 4 + 2 * tile + q, rp:rp + 1, :] = rows[m:m + 1]

    def deliver(start, size, k):
        rows = pl.ds(start, size)

        def piece(d):
            return stage.at[pl.ds(pl.multiple_of(d * 64 + start, 16), size), :]

        each(lambda d, dev: push(piece(d), got.at[mine, rows], k, dev))
        keep(piece(me), got.at[mine, rows])

    wait(recv.at[pl.ds(0, 127), early], rsem.at[1])
    phase(0)
    deliver(0, 32, 4)
    wait(recv.at[pl.ds(0, 127), late], rsem.at[2])
    phase(1)
    deliver(32, 16, 5)
    deliver(48, 16, 6)

    @pl.when(first)
    def _():
        each(lambda d, dev: push(extra.at[d], gotx.at[mine], 3, dev))
        keep(extra.at[me], gotx.at[mine])

    wait(send.at[pl.ds(0, 127), early], ssem.at[1])
    wait(send.at[pl.ds(0, 127), late], ssem.at[2])
    for load in loads[9:]:
        load.wait()
    wait(got.at[pl.ds(0, 127), early], rsem.at[4])

    def transform(n, _):
        f, group = lax.div(n, 4), lax.rem(n, 4)
        turned = row_dft(
            [[got[((4 * group + k) * 2 + f) * 4 + q, :32, :] for q in range(4)] for k in range(4)],
            (wrh, wrl), tj, group,
        )
        for k in range(16):
            send[n * 16 + k] = turned[k]

        @pl.when(group == 0)
        def _():
            for k, v in enumerate(row_dft_zero([got[f * 4 + q, :32, :] for q in range(4)], (wsh, wsl))):
                send[n * 16 + k] = v

        return 0

    lax.fori_loop(0, 8, transform, 0)

    def finish(n, _, h):
        f, group = lax.div(n, 4), lax.rem(n, 4)
        here = slice(h * 32, h * 32 + 32)
        parts = []
        for k in range(4):
            base = ((4 * group + k) * 2 + f) * 4
            v = jnp.concatenate(
                [got[base + q, 32 + 16 * h:48 + 16 * h, :] for q in range(4)], axis=0
            )
            hi = v.astype(BF).astype(F32)
            a = jnp.concatenate([hi, v - hi], axis=0).T.astype(BF)
            parts.append(jnp.concatenate([a[:64], a[64:]], axis=1))
        a = jnp.concatenate(parts, axis=0)
        u = dot(a, vrh[...]) + dot(a, vrl[...])

        def add(k, pieces):
            for i, v in enumerate(pieces):
                send[n * 16 + 4 * k + i, here, :] += v

        for k in range(4):
            v = u[k * 64:k * 64 + 64]
            re, im = v[:32, :256] - v[32:, 256:], v[:32, 256:] + v[32:, :256]
            tr, ti = tj[4 * group + k, 0:1, :], tj[4 * group + k, 1:2, :]
            pieces = halves(re * tr - im * ti, re * ti + im * tr)
            if k > 0:
                add(k, pieces)
            else:
                @pl.when(group > 0)
                def _(pieces=pieces):
                    add(0, pieces)

        @pl.when(group == 0)
        def _():
            for q in range(4):
                edges[2 * q:2 * q + 2, :] = gotx[f * 4 + q]
            edge = jnp.concatenate([edges[...], jnp.zeros((120, 128), F32)], axis=0).T[:, :32]
            v = three(edge[h * 32:h * 32 + 32], (xh[0], xl[0]))
            v = v + three(edge[64 + h * 32:96 + h * 32], (xh[1], xl[1]))
            for i in range(2):
                one = parts[0][i * 32:i * 32 + 32]
                v = v + dot(one, vsh[i]) + dot(one, vsl[i])
            add(0, halves(v[:, :256], v[:, 256:]))

        return 0

    @pl.when(first)
    def _():
        wait(gotx.at[pl.ds(0, 7)], rsem.at[3])

    @pl.when(mine >= 8)
    def _():
        wait(gotx, rsem.at[3])

    for h in range(2):
        wait(got.at[pl.ds(0, 127), pl.ds(h * 16, 16)], rsem.at[5 + h])

        def picture(f, _, h=h):
            lax.fori_loop(4 * f, 4 * f + 4, functools.partial(finish, h=h), 0)

            if h == 0:
                paint(lambda k, at: send[f * 64 + k, at, :], image.at[f], out.at[f], lsem)
            else:
                mine_f = pl.ds(f * 64, 64)
                pltpu.make_async_copy(send.at[mine_f, late], rest.at[mine_f], msem).start()
            return 0

        lax.fori_loop(0, 2, picture, 0)
    wait(out, lsem)
    wait(rest, msem)

    @pl.when(first)
    def _():
        wait(extra.at[pl.ds(0, 127)], ssem.at[3])

    wait(tabr.at[pl.ds(0, 3)], ssem.at[0])
    wait(tabr.at[pl.ds(0, 124)], ssem.at[7])
    wait(got.at[pl.ds(0, 127), early], ssem.at[4])
    for p in range(2):
        wait(got.at[pl.ds(0, 127), pl.ds(p * 16, 16)], ssem.at[5 + p])


def exchange(tiles, pair, time, chan, count, weights, pixels, beams):
    t = tables()
    smem = pl.BlockSpec(memory_space=pltpu.SMEM)
    away = pl.BlockSpec(memory_space=pl.ANY)
    constants = (*t["b"], *t["wc"], *t["tw"], t["f"], *t["wr"], *t["ws"], *t["vr"], *t["vs"], *t["wx"], t["tj"])
    return pl.pallas_call(
        exchange_kernel,
        out_shape=(
            jax.ShapeDtypeStruct((2, 32, 8192), F32), jax.ShapeDtypeStruct((128, 32, 128), F32)
        ),
        in_specs=[pl.BlockSpec(memory_space=pltpu.VMEM)] + [smem] * 5 + [away] * 20,
        out_specs=(away, away),
        scratch_shapes=[
            pltpu.VMEM((128, 2, 16, 128), F32),
            pltpu.VMEM((1024, 2, 16, 128), BF),
            pltpu.VMEM((8, 2, 256, 256), BF),
            pltpu.VMEM((8, 2, 256, 256), BF),
            pltpu.VMEM((512, 256), BF),
            pltpu.VMEM((512, 256), BF),
            pltpu.VMEM((256, 128), F32),
            pltpu.VMEM((256, 128), F32),
            pltpu.VMEM((2, 2, 256, 256), BF),
            pltpu.VMEM((128, 512), BF),
            pltpu.VMEM((128, 512), BF),
            pltpu.VMEM((2, 128, 512), BF),
            pltpu.VMEM((2, 128, 512), BF),
            pltpu.VMEM((256, 512), BF),
            pltpu.VMEM((256, 512), BF),
            pltpu.VMEM((2, 256, 512), BF),
            pltpu.VMEM((2, 256, 512), BF),
            pltpu.VMEM((2, 32, 512), BF),
            pltpu.VMEM((2, 32, 512), BF),
            pltpu.VMEM((16, 2, 256), F32),
            pltpu.VMEM((128 * 32, 128), F32),
            pltpu.VMEM((8, 256, 256), BF),
            pltpu.VMEM((8, 256, 256), BF),
            pltpu.VMEM((256, 256), BF),
            pltpu.VMEM((128, 64, 128), F32),
            pltpu.VMEM((4, 1, 128), I32),
            pltpu.VMEM((128, 64, 128), F32),
            pltpu.VMEM((128, 1, 128), I32),
            pltpu.VMEM((128, 128), I32),
            pltpu.VMEM((2, 16 * 256, 256), BF),
            pltpu.VMEM((2, 256, 256), BF),
            pltpu.VMEM((2, 256, 256), BF),
            pltpu.VMEM((256, 256), F32),
            pltpu.VMEM((128 * 64, 128), F32),
            pltpu.VMEM((128, 2, 128), F32),
            pltpu.VMEM((128, 64, 128), F32),
            pltpu.VMEM((8, 2, 128), F32),
            pltpu.VMEM((8, 128), F32),
            pltpu.VMEM((2, 32, 8192), F32),
            pltpu.SemaphoreType.DMA((8,)),
            pltpu.SemaphoreType.DMA((8,)),
            pltpu.SemaphoreType.DMA,
            pltpu.SemaphoreType.DMA,
            pltpu.SemaphoreType.DMA((20,)),
        ],
        compiler_params=pltpu.CompilerParams(
            vmem_limit_bytes=VMEM, collective_id=0, has_side_effects=True
        ),
        name="exchange",
    )(tiles, pair, time, chan, count, weights, pixels, beams, *constants)


def final_kernel(half, rest, out, val, through, image, sems):
    parts = [(rest.at[pl.ds(f * 64, 64)], val.at[f]) for f in range(2)]
    parts += [(half.at[f], through.at[f]) for f in range(2)]
    loads = [pltpu.make_async_copy(src, dst, sems.at[i]) for i, (src, dst) in enumerate(parts)]
    for load in loads:
        load.start()
    for f in range(2):
        loads[f].wait()
        paint(lambda k, at: val[f, k, at, :], image.at[f], out.at[f, pl.ds(32, 32), :], sems.at[4])
        loads[2 + f].wait()
        pltpu.make_async_copy(through.at[f], out.at[f, pl.ds(0, 32), :], sems.at[5]).start()
    pltpu.make_async_copy(image, image, sems.at[4]).wait()
    pltpu.make_async_copy(through, through, sems.at[5]).wait()


def final(half, rest):
    away = pl.BlockSpec(memory_space=pl.ANY)
    return pl.pallas_call(
        final_kernel,
        out_shape=jax.ShapeDtypeStruct((2, 64, 8192), F32),
        in_specs=[away, away],
        out_specs=away,
        scratch_shapes=[
            pltpu.VMEM((2, 64, 32, 128), F32),
            pltpu.VMEM((2, 32, 8192), F32),
            pltpu.VMEM((2, 32, 8192), F32),
            pltpu.SemaphoreType.DMA((6,)),
        ],
        compiler_params=pltpu.CompilerParams(vmem_limit_bytes=VMEM),
        name="final",
    )(half, rest)


def pixel_view(pixels):
    x = pixels.reshape(128, 2, 2, 8, 128).transpose(0, 1, 3, 2, 4)
    return x.reshape(128, 2, 16, 128)


def beam_view(aterms):
    x = aterms.reshape(512, 2, 2, 2, 8, 128).transpose(0, 1, 2, 4, 3, 5)
    return x.reshape(1024, 2, 16, 128)


def local(
    subgrid_pixels, tile_offsets, station_pairs, time_blocks, channel_blocks, valid_counts,
    aterms, channel_weights,
):
    return final(*exchange(
        tile_offsets.T, station_pairs.T, time_blocks, channel_blocks, valid_counts, channel_weights,
        pixel_view(subgrid_pixels), beam_view(aterms),
    ))


def solution(mesh):
    in_specs = (
        P(("row", "col"), None, None, None),
        P(("row", "col"), None),
        P(("row", "col"), None),
        P(("row", "col")),
        P(("row", "col")),
        P(("row", "col")),
        P(),
        P(),
    )
    out_specs = P(None, ("row", "col"), None)
    return jax.shard_map(local, mesh=mesh, in_specs=in_specs, out_specs=out_specs, check_vma=False)
```
